128 devices in a mesh: win: 32 (over x, y, z_lo), seq: 4 (over z_hi, core).
Axes of the slice: x: 4, y: 4, z: 4 (z_hi: 2, z_lo: 2; z = z_hi * 2 + z_lo), core: 2. Of those that a mesh axis runs over, the one named last changes fastest.
Arguments:
- tokens: bfloat16 [2, 32, 448, 768], P(None, 'win', 'seq'), may hold values from -6 to 6
- encoder_states: bfloat16 [2, 32, 1500, 768], P(None, 'win', 'seq'), may hold values from -6 to 6
- segments: int32 [2, 32, 448], P(None, 'win'), may hold values from 0 to 3, as said below
- frame_clips: int32 [2, 32, 1500], P(None, 'win'), may hold values from 0 to 3, as said below
- out_grad: bfloat16 [2, 32, 448, 768], P(None, 'win', 'seq'), may hold values from -6 to 6
- self_gain: bfloat16 [768], P(('win', 'seq')), may hold values from 0.5 to 1.5
- self_shift: bfloat16 [768], P(('win', 'seq')), may hold values from -3 to 3
- self_query: bfloat16 [768, 768], P(('win', 'seq')), may hold values from -0.21875 to 0.21875
- self_query_bias: bfloat16 [768], P(('win', 'seq')), may hold values from -3 to 3
- self_key: bfloat16 [768, 768], P(('win', 'seq')), may hold values from -0.21875 to 0.21875
- self_value: bfloat16 [768, 768], P(('win', 'seq')), may hold values from -0.21875 to 0.21875
- self_value_bias: bfloat16 [768], P(('win', 'seq')), may hold values from -3 to 3
- self_output: bfloat16 [768, 768], P(('win', 'seq')), may hold values from -1.25 to 1.25
- self_output_bias: bfloat16 [768], P(('win', 'seq')), may hold values from -3 to 3
- cross_gain: bfloat16 [768], P(('win', 'seq')), may hold values from 0.5 to 1.5
- cross_shift: bfloat16 [768], P(('win', 'seq')), may hold values from -3 to 3
- cross_query: bfloat16 [768, 768], P(('win', 'seq')), may hold values from -0.21875 to 0.21875
- cross_query_bias: bfloat16 [768], P(('win', 'seq')), may hold values from -3 to 3
- cross_key: bfloat16 [768, 768], P(('win', 'seq')), may hold values from -0.21875 to 0.21875
- cross_value: bfloat16 [768, 768], P(('win', 'seq')), may hold values from -0.21875 to 0.21875
- cross_value_bias: bfloat16 [768], P(('win', 'seq')), may hold values from -3 to 3
- cross_output: bfloat16 [768, 768], P(('win', 'seq')), may hold values from -1.25 to 1.25
- cross_output_bias: bfloat16 [768], P(('win', 'seq')), may hold values from -3 to 3
- final_gain: bfloat16 [768], P(('win', 'seq')), may hold values from 0.5 to 1.5
- final_shift: bfloat16 [768], P(('win', 'seq')), may hold values from -3 to 3
- hidden_in: bfloat16 [768, 3072], P(('win', 'seq')), may hold values from -0.21875 to 0.21875
- hidden_in_bias: bfloat16 [3072], P(('win', 'seq')), may hold values from -3 to 3
- hidden_out: bfloat16 [3072, 768], P(('win', 'seq')), may hold values from -0.109375 to 0.109375
- hidden_out_bias: bfloat16 [768], P(('win', 'seq')), may hold values from -3 to 3
Outputs:
- block_output: bfloat16 [2, 32, 448, 768], P(None, 'win', 'seq')
- input_grad: float32 [2, 32, 448, 768], P(None, 'win', 'seq')
- encoder_grad: float32 [2, 32, 1500, 768], P(None, 'win', 'seq')
- grad_self_gain: float32 [768], P(('win', 'seq'))
- grad_self_shift: float32 [768], P(('win', 'seq'))
- grad_self_query: float32 [768, 768], P(('win', 'seq'))
- grad_self_query_bias: float32 [768], P(('win', 'seq'))
- grad_self_key: float32 [768, 768], P(('win', 'seq'))
- grad_self_value: float32 [768, 768], P(('win', 'seq'))
- grad_self_value_bias: float32 [768], P(('win', 'seq'))
- grad_self_output: float32 [768, 768], P(('win', 'seq'))
- grad_self_output_bias: float32 [768], P(('win', 'seq'))
- grad_cross_gain: float32 [768], P(('win', 'seq'))
- grad_cross_shift: float32 [768], P(('win', 'seq'))
- grad_cross_query: float32 [768, 768], P(('win', 'seq'))
- grad_cross_query_bias: float32 [768], P(('win', 'seq'))
- grad_cross_key: float32 [768, 768], P(('win', 'seq'))
- grad_cross_value: float32 [768, 768], P(('win', 'seq'))
- grad_cross_value_bias: float32 [768], P(('win', 'seq'))
- grad_cross_output: float32 [768, 768], P(('win', 'seq'))
- grad_cross_output_bias: float32 [768], P(('win', 'seq'))
- grad_final_gain: float32 [768], P(('win', 'seq'))
- grad_final_shift: float32 [768], P(('win', 'seq'))
- grad_hidden_in: float32 [768, 3072], P(('win', 'seq'))
- grad_hidden_in_bias: float32 [3072], P(('win', 'seq'))
- grad_hidden_out: float32 [3072, 768], P(('win', 'seq'))
- grad_hidden_out_bias: float32 [768], P(('win', 'seq'))
The draws below stay inside these ranges and needn't reach their ends.
Inputs may be any that keep to these rules, and one draw needn't show every extreme that they name: `segments`: for each window, the clip numbers of its 448 tokens never fall along the window, and each of the 4 clips has at least one token. `frame_clips`: for each window, the clip numbers of its 1500 frames never fall, use the same numbering as that window's segments, and each of the 4 clips has at least one frame.
All inputs are finite; a program needn't handle non-finite values.
Results may differ from the reference program's by a relative error of at most 0.025.
Values may be sent and summed in bfloat16 or wider, within the bound.
A program may use at most 256 MiB of HBM per device.

```python
import math
import jax
import jax.numpy as jnp
from jax import lax

D = 768
HEADS = 12
HEAD_DIM = 64
FF = 3072
LEN = 448
FRAMES = 1500
CLIPS = 4
MICRO = 2
WINDOWS = 32
SPAN = 112
FRAMES_DEV = 375


def longest_clip(key):
    return jax.random.randint(jax.random.fold_in(key, 11), (MICRO, WINDOWS, 1), 0, CLIPS)


def clip_numbers(key, longest, total, short_most):
    lengths = jax.random.randint(key, (MICRO, WINDOWS, CLIPS), 1, short_most + 1)
    slots = jnp.arange(CLIPS, dtype=jnp.int32)
    shorts = jnp.where(slots == longest, 0, lengths)
    lengths = jnp.where(slots == longest, total - jnp.sum(shorts, -1, keepdims=True), shorts)
    bounds = jnp.cumsum(lengths, -1)[:, :, :CLIPS - 1]
    places = jnp.arange(total, dtype=jnp.int32)
    marks = (places[None, None, :, None] >= bounds[:, :, None, :]).astype(jnp.int32)
    return jnp.sum(marks, -1).astype(jnp.int32)


def draw_segments(key, part):
    longest = longest_clip(key)
    key = jax.random.fold_in(key, 3)
    return clip_numbers(key, longest, LEN, SPAN // 4)


def draw_frame_clips(key, part):
    longest = longest_clip(key)
    key = jax.random.fold_in(key, 5)
    return clip_numbers(key, longest, FRAMES, FRAMES_DEV // 4)


def levels(own_key, shape, shards, smallest, high):
    level = 1.0
    for axis_at, parts in shards:
        steps = jax.random.uniform(jax.random.fold_in(jax.random.fold_in(own_key, 6), axis_at), (parts,), jnp.float32, smallest / len(shards), high / len(shards))
        level = level * jnp.repeat(jnp.exp(steps), shape[axis_at] // parts).reshape((-1,) + (1,) * (len(shape) - 1 - axis_at))
    return level


def noise(stream_key, extent, width, most, cuts=(), held_as=jnp.bfloat16):
    drawn = width * jax.random.normal(stream_key, extent, jnp.float32)
    if cuts:
        drawn = drawn * levels(stream_key, extent, cuts, -0.22, 0.18)
    return jnp.clip(drawn, -most, most).astype(held_as)


def setup_inputs(seed: int = 0) -> dict:
    key_of = jax.random.split(jax.random.key(seed), 30)
    return {
        "tokens": noise(key_of[0], (MICRO, WINDOWS, LEN, D), 1.0, 6.0, ((1, 32), (2, 4))),
        "encoder_states": noise(key_of[1], (MICRO, WINDOWS, FRAMES, D), 1.0, 6.0, ((1, 32), (2, 4))),
        "segments": draw_segments(jax.random.fold_in(key_of[29], 71), 0),
        "frame_clips": draw_frame_clips(jax.random.fold_in(key_of[29], 71), 0),
        "out_grad": noise(key_of[4], (MICRO, WINDOWS, LEN, D), 1.0, 6.0, ((1, 32), (2, 4))),
        "self_gain": jnp.clip(1.0 + 0.1 * jax.random.normal(key_of[5], (D,), jnp.float32), 0.5, 1.5).astype(jnp.bfloat16),
        "self_shift": noise(key_of[6], (D,), 0.3, 3.0, ((0, 128),)),
        "self_query": noise(key_of[7], (D, D), D ** -0.5, 0.21875, ((0, 128),)),
        "self_query_bias": noise(key_of[8], (D,), 0.3, 3.0, ((0, 128),)),
        "self_key": noise(key_of[9], (D, D), D ** -0.5, 0.21875, ((0, 128),)),
        "self_value": noise(key_of[10], (D, D), D ** -0.5, 0.21875, ((0, 128),)),
        "self_value_bias": noise(key_of[11], (D,), 0.3, 3.0, ((0, 128),)),
        "self_output": noise(key_of[12], (D, D), (D // 32) ** -0.5, 1.25, ((0, 128),)),
        "self_output_bias": noise(key_of[13], (D,), 0.3, 3.0, ((0, 128),)),
        "cross_gain": jnp.clip(1.0 + 0.1 * jax.random.normal(key_of[14], (D,), jnp.float32), 0.5, 1.5).astype(jnp.bfloat16),
        "cross_shift": noise(key_of[15], (D,), 0.3, 3.0, ((0, 128),)),
        "cross_query": noise(key_of[16], (D, D), D ** -0.5, 0.21875, ((0, 128),)),
        "cross_query_bias": noise(key_of[17], (D,), 0.3, 3.0, ((0, 128),)),
        "cross_key": noise(key_of[18], (D, D), D ** -0.5, 0.21875, ((0, 128),)),
        "cross_value": noise(key_of[19], (D, D), D ** -0.5, 0.21875, ((0, 128),)),
        "cross_value_bias": noise(key_of[20], (D,), 0.3, 3.0, ((0, 128),)),
        "cross_output": noise(key_of[21], (D, D), (D // 32) ** -0.5, 1.25, ((0, 128),)),
        "cross_output_bias": noise(key_of[22], (D,), 0.3, 3.0, ((0, 128),)),
        "final_gain": jnp.clip(1.0 + 0.1 * jax.random.normal(key_of[23], (D,), jnp.float32), 0.5, 1.5).astype(jnp.bfloat16),
        "final_shift": noise(key_of[24], (D,), 0.3, 3.0, ((0, 128),)),
        "hidden_in": noise(key_of[25], (D, FF), D ** -0.5, 0.21875, ((0, 128),)),
        "hidden_in_bias": noise(key_of[26], (FF,), 0.3, 3.0, ((0, 128),)),
        "hidden_out": noise(key_of[27], (FF, D), FF ** -0.5, 0.109375, ((0, 128),)),
        "hidden_out_bias": noise(key_of[28], (D,), 0.3, 3.0, ((0, 128),)),
    }


EPS = 1e-05
SCALE = 0.125
BLOCKED = -1e+30
HIGH = lax.Precision.HIGHEST

@jax.custom_vjp
def low(v):
    return lax.optimization_barrier(v.astype(jnp.bfloat16)).astype(jnp.float32)

@jax.custom_vjp
def low_back(v):
    return v

def low_keep(v):
    return (low(v), None)

def low_pass(kept, grad):
    return (grad,)

def back_keep(v):
    return (v, None)

def back_low(kept, grad):
    return (low(grad),)
low.defvjp(low_keep, low_pass)
low_back.defvjp(back_keep, back_low)

def layer_norm(values, gain, shift):
    mean = lax.optimization_barrier(jnp.mean(values, -1, keepdims=True))
    centered = values - mean
    spread = lax.optimization_barrier(jnp.mean(centered * centered, -1, keepdims=True))
    return centered * lax.rsqrt(spread + EPS) * gain + shift

def project(left, weight):
    return jnp.einsum('gcd,df->gcf', left, weight, precision=HIGH)

def attend(queries, keys, values, allowed):
    group_count, row_count = (queries.shape[0], queries.shape[1])
    head_q = queries.reshape(group_count, row_count, HEADS, HEAD_DIM)
    head_k = keys.reshape(group_count, keys.shape[1], HEADS, HEAD_DIM)
    head_v = values.reshape(group_count, values.shape[1], HEADS, HEAD_DIM)
    scores = low_back(jnp.einsum('gqhe,gkhe->ghqk', head_q, head_k, precision=HIGH) * SCALE)
    scores = jnp.where(allowed[:, None], scores, BLOCKED)
    probs = low(jax.nn.softmax(scores, axis=-1))
    mixed = jnp.einsum('ghqk,gkhe->gqhe', probs, head_v, precision=HIGH)
    return mixed.reshape(group_count, row_count, D)

def block(params, inputs, encoder, segment_ids, clip_ids):
    self_gain, self_shift, self_query, self_query_bias, self_key, self_value, self_value_bias, self_output, self_output_bias, cross_gain, cross_shift, cross_query, cross_query_bias, cross_key, cross_value, cross_value_bias, cross_output, cross_output_bias, final_gain, final_shift, hidden_in, hidden_in_bias, hidden_out, hidden_out_bias = params
    positions = jnp.arange(inputs.shape[1])
    self_allowed = (segment_ids[:, :, None] == segment_ids[:, None, :]) & (positions[None, None, :] <= positions[None, :, None])
    cross_allowed = segment_ids[:, :, None] == clip_ids[:, None, :]
    first_norm = low(layer_norm(inputs, self_gain, self_shift))
    queries = low(low_back(project(first_norm, self_query) + self_query_bias))
    keys_self = low(low_back(project(first_norm, self_key)))
    values_self = low(low_back(project(first_norm, self_value) + self_value_bias))
    self_mixed = low(low_back(attend(queries, keys_self, values_self, self_allowed)))
    after_self = inputs + low_back(project(self_mixed, self_output) + self_output_bias)
    second_norm = low(layer_norm(after_self, cross_gain, cross_shift))
    cross_queries = low(low_back(project(second_norm, cross_query) + cross_query_bias))
    cross_keys = low(project(encoder, cross_key))
    cross_values = low(project(encoder, cross_value) + cross_value_bias)
    cross_mixed = low(low_back(attend(cross_queries, cross_keys, cross_values, cross_allowed)))
    after_cross = after_self + low_back(project(cross_mixed, cross_output) + cross_output_bias)
    third_norm = low(layer_norm(after_cross, final_gain, final_shift))
    hidden_pre = low_back(project(third_norm, hidden_in) + hidden_in_bias)
    hidden_act = low(jax.nn.gelu(hidden_pre, approximate=False))
    return after_cross + low_back(project(hidden_act, hidden_out) + hidden_out_bias)

def reference(tokens, encoder_states, segments, frame_clips, out_grad, self_gain, self_shift, self_query, self_query_bias, self_key, self_value, self_value_bias, self_output, self_output_bias, cross_gain, cross_shift, cross_query, cross_query_bias, cross_key, cross_value, cross_value_bias, cross_output, cross_output_bias, final_gain, final_shift, hidden_in, hidden_in_bias, hidden_out, hidden_out_bias):
    params = tuple((weight.astype(jnp.float32) for weight in (self_gain, self_shift, self_query, self_query_bias, self_key, self_value, self_value_bias, self_output, self_output_bias, cross_gain, cross_shift, cross_query, cross_query_bias, cross_key, cross_value, cross_value_bias, cross_output, cross_output_bias, final_gain, final_shift, hidden_in, hidden_in_bias, hidden_out, hidden_out_bias)))
    group_size = math.gcd(WINDOWS, 8)
    group_steps = WINDOWS // group_size

    def forward(inputs, encoder, weights, segment_ids, clip_ids):

        def one_group(packed):
            return block(weights, packed[0], packed[1], packed[2], packed[3])
        stacked = (inputs.reshape(group_steps, group_size, LEN, D), encoder.reshape(group_steps, group_size, FRAMES, D), segment_ids.reshape(group_steps, group_size, LEN), clip_ids.reshape(group_steps, group_size, FRAMES))
        result = lax.map(jax.checkpoint(one_group), stacked)
        return result.reshape(WINDOWS, LEN, D)
    outputs, input_grads, encoder_grads = ([], [], [])
    totals = None
    for micro_step in range(MICRO):
        segment_ids = segments[micro_step]
        clip_ids = frame_clips[micro_step]

        def tied(inputs, encoder, weights):
            return forward(inputs, encoder, weights, segment_ids, clip_ids)
        result, pullback = jax.vjp(tied, tokens[micro_step].astype(jnp.float32), encoder_states[micro_step].astype(jnp.float32), params)
        grad_inputs, grad_encoder, grad_weights = pullback(out_grad[micro_step].astype(jnp.float32))
        outputs.append(result.astype(jnp.bfloat16))
        input_grads.append(grad_inputs)
        encoder_grads.append(grad_encoder)
        if totals is None:
            totals = grad_weights
        else:
            totals = tuple((first + second for first, second in zip(totals, grad_weights)))
    return (jnp.stack(outputs), jnp.stack(input_grads), jnp.stack(encoder_grads), totals[0], totals[1], totals[2], totals[3], totals[4], totals[5], totals[6], totals[7], totals[8], totals[9], totals[10], totals[11], totals[12], totals[13], totals[14], totals[15], totals[16], totals[17], totals[18], totals[19], totals[20], totals[21], totals[22], totals[23])
```

```python
from functools import partial

import jax
import jax.numpy as jnp
from jax import lax
from jax.experimental import pallas as pl
from jax.experimental.pallas import tpu as pltpu
from jax.sharding import PartitionSpec as P

bf, f32 = jnp.bfloat16, jnp.float32
HEADS, HEAD_DIM = 12, 64
EPS = 1e-05
SCALE = 0.125
BLOCKED = -1e30
MESH = pl.DeviceIdType.MESH
PIECES, ROWS, D = 16, 48, 768
HALF = D // 2


def coords():
    win, seq = lax.axis_index("win"), lax.axis_index("seq")
    x, y = win // 8, lax.rem(win // 2, 4)
    z = (seq // 2) * 2 + lax.rem(win, 2)
    return x, y, z, lax.rem(seq, 2)


def device_at(x, y, z, core):
    return (x * 8 + y * 2 + lax.rem(z, 2), (z // 2) * 2 + core)


def member(z, core):
    return lax.rem(z, 2) * 4 + (z // 2) * 2 + core


def enter(peers):
    barrier = pltpu.get_barrier_semaphore()
    for peer in peers:
        pl.semaphore_signal(barrier, inc=1, device_id=peer, device_id_type=MESH)
    pl.semaphore_wait(barrier, len(peers))


def relayout_matrix():
    r = lax.broadcasted_iota(jnp.int32, (784, 1), 0)
    piece, at = r // 48, lax.rem(r, 48)
    narrow = (at // 6) * 112 + piece * 6 + lax.rem(at, 6)
    wide = ((piece - 12) * 2 + at // 24) * 112 + 72 + lax.rem(at, 24)
    small = lax.rem(at, 8) * 112 + 96
    source = jnp.where(piece < 12, narrow, jnp.where(piece < 16, wide, small))
    cols = lax.broadcasted_iota(jnp.int32, (784, 896), 1)
    return jnp.where(cols == source, 1.0, 0.0).astype(bf)


def gather_kernel(shard, tok_in, enc_in, og_in, W, SM, tok, enc, og, zbuf, slab, smbuf,
                  zs, zr, ds, dr, ls, s1, r1, s2, r2, ss1, sr1, ss2, sr2, cs, cr, es, er, fs, fr):
    x, y, z, core = coords()
    hi = z // 2
    other = 1 - core
    partner = device_at(x, y, z, other)
    across = lax.rem(z + 2, 4)
    xp = [device_at(lax.rem(x + o, 4), y, z, core) for o in (1, 2, 3)]
    yp = [device_at(x, lax.rem(y + o, 4), z, core) for o in (1, 2, 3)]
    zp = [device_at(x, y, lax.rem(z + o, 4), core) for o in (1, 2, 3)]
    enter([partner, device_at(x, y, across, other)] + xp + yp + zp)

    def remote(src, dst, send, recv, to):
        return pltpu.make_async_remote_copy(src_ref=src, dst_ref=dst, send_sem=send, recv_sem=recv,
                                            device_id=to, device_id_type=MESH)
    sent = []

    def start(*a):
        c = remote(*a)
        c.start()
        sent.append(c)
        return c
    me = member(z, core)
    mine = pltpu.make_async_copy(shard, zbuf.at[me], ls.at[0])
    mine.start()
    for o in (1, 2, 3):
        start(shard, zbuf.at[me], zs.at[o], zr.at[o], zp[o - 1])
    start(shard, zbuf.at[me], ds.at[0], dr.at[0], partner)

    block = hi * 2 + core
    locals_ = []

    def local(src, dst, sem):
        c = pltpu.make_async_copy(src, dst, sem)
        c.start()
        locals_.append(c)
    home = device_at(x, y, across, core)
    for i, (src, dst) in enumerate(((tok_in, tok), (enc_in, enc))):
        start(src.at[1 - hi], dst.at[block], es.at[i], er.at[i], home)
        start(src.at[hi], dst.at[block], es.at[2 + i], er.at[2 + i], partner)
        local(src.at[hi], dst.at[block], ls.at[1 + i])
    start(og_in.at[1 - hi], og.at[core], es.at[4], er.at[4 + core], device_at(x, y, across, hi))

    @pl.when(core == hi)
    def _():
        c = pltpu.make_async_copy(og_in.at[hi], og.at[core], ls.at[3])
        c.start()
        c.wait()

    @pl.when(core != hi)
    def _():
        c = remote(og_in.at[hi], og.at[core], es.at[5], er.at[6], partner)
        c.start()
        c.wait_send()
    for o in (1, 2, 3):
        remote(shard, zbuf.at[me], zs.at[o], zr.at[o], zp[0]).wait_recv()
        src = member(lax.rem(z + 4 - o, 4), core)
        start(zbuf.at[src], zbuf.at[src], ds.at[o], dr.at[o], partner)
    for o in range(4):
        remote(shard, zbuf.at[me], ds.at[o], dr.at[o], partner).wait_recv()
    mine.wait()
    spread = jnp.dot(relayout_matrix(), zbuf[...].reshape(896, D), preferred_element_type=jnp.float32).astype(bf)
    slab[...] = spread[:768].reshape(PIECES, ROWS, D)
    smbuf[...] = spread[768:, :128]

    def rows(gx, gy):
        return pl.ds(pl.multiple_of((gx * 4 + gy) * 48, 16), 48)
    part = pl.ds(pl.multiple_of(core * 8, 8), 8)
    cols = (pl.ds(0, HALF), pl.ds(HALF, HALF))
    local(slab, W.at[:, rows(x, y), :], ls.at[4])
    local(smbuf, SM.at[x * 4 + y], ls.at[5])
    first, second = (xp, yp), (yp, xp)
    for o in (1, 2, 3):
        for k in (0, 1):
            start(slab.at[part, :, cols[k]], W.at[part, rows(x, y), cols[k]], s1.at[k, o], r1.at[k, o], first[k][o - 1])
        start(smbuf, SM.at[x * 4 + y], ss1.at[o], sr1.at[o], xp[o - 1])
    for o in (1, 2, 3):
        for k in (0, 1):
            start(slab.at[part, :, cols[k]], W.at[part, rows(x, y), cols[k]], s2.at[k, 0, o], r2.at[k, 0, o], second[k][o - 1])
        start(smbuf, SM.at[x * 4 + y], ss2.at[0, o], sr2.at[0, o], yp[o - 1])

    def origin(k, b, p):
        if k == 0:
            return lax.rem(x + 4 - b, 4), lax.rem(y + 4 - p, 4)
        return lax.rem(x + 4 - p, 4), lax.rem(y + 4 - b, 4)

    def hand_over(k, b, p):
        at = W.at[part, rows(*origin(k, b, p)), cols[k]]
        start(at, at, cs.at[k, b * 4 + p], cr.at[k, b * 4 + p], partner)
    for b in (1, 2, 3):
        for k in (0, 1):
            at = W.at[part, rows(*origin(k, b, 0)), cols[k]]
            remote(at, at, s1.at[k, b], r1.at[k, b], partner).wait_recv()
            for p in (1, 2, 3):
                start(at, at, s2.at[k, b, p], r2.at[k, b, p], second[k][p - 1])
            hand_over(k, b, 0)
        at = SM.at[lax.rem(x + 4 - b, 4) * 4 + y]
        remote(at, at, ss1.at[b], sr1.at[b], partner).wait_recv()
        for p in (1, 2, 3):
            start(at, at, ss2.at[b, p], sr2.at[b, p], yp[p - 1])
    for i, (src, dst) in enumerate(((tok_in, tok), (enc_in, enc))):
        far = dst.at[(1 - hi) * 2 + core]
        remote(far, far, es.at[i], er.at[i], partner).wait_recv()
        start(far, far, fs.at[i], fr.at[i], partner)
    for b in range(4):
        for p in (1, 2, 3):
            for k in (0, 1):
                at = W.at[part, rows(*origin(k, b, p)), cols[k]]
                remote(at, at, s2.at[k, b, p], r2.at[k, b, p], partner).wait_recv()
                hand_over(k, b, p)
            at = SM.at[0]
            remote(at, at, ss2.at[b, p], sr2.at[b, p], partner).wait_recv()
    for k in (0, 1):
        for q in range(1, 16):
            at = W.at[part, rows(x, y), cols[k]]
            remote(at, at, cs.at[k, q], cr.at[k, q], partner).wait_recv()
    for i, dst in enumerate((tok, enc)):
        remote(dst.at[0], dst.at[0], es.at[2 + i], er.at[2 + i], partner).wait_recv()
        remote(dst.at[0], dst.at[0], fs.at[i], fr.at[i], partner).wait_recv()
    at = og.at[0]

    @pl.when(hi == core)
    def _():
        remote(at, at, es.at[4], er.at[6], partner).wait_recv()

    @pl.when(hi != core)
    def _():
        for s in (0, 1):
            remote(at, at, es.at[4], er.at[4 + s], partner).wait_recv()
    for c in sent:
        c.wait_send()
    for c in locals_:
        c.wait()


def gather_all(shard, tok, enc, og):
    any_ = pl.BlockSpec(memory_space=pl.ANY)
    DMA = pltpu.SemaphoreType.DMA
    return pl.pallas_call(
        gather_kernel,
        out_shape=[jax.ShapeDtypeStruct((16, D, D), bf), jax.ShapeDtypeStruct((16, 16, 128), bf),
                   jax.ShapeDtypeStruct((4, 112, D), bf), jax.ShapeDtypeStruct((4, 384, D), bf),
                   jax.ShapeDtypeStruct((2, 112, D), bf)],
        in_specs=[any_] * 4, out_specs=[any_] * 5,
        scratch_shapes=[pltpu.VMEM((8, 112, D), bf), pltpu.VMEM((16, 48, D), bf), pltpu.VMEM((16, 128), bf),
                        DMA((4,)), DMA((4,)), DMA((4,)), DMA((4,)), DMA((6,)),
                        DMA((2, 4)), DMA((2, 4)), DMA((2, 4, 4)), DMA((2, 4, 4)),
                        DMA((4,)), DMA((4,)), DMA((4, 4)), DMA((4, 4)),
                        DMA((2, 16)), DMA((2, 16)), DMA((6,)), DMA((7,)), DMA((2,)), DMA((2,))],
        compiler_params=pltpu.CompilerParams(collective_id=0, has_side_effects=True, vmem_limit_bytes=40 << 20),
        name="gather_all",
    )(shard, tok, enc, og)


def split_matrix(core):
    r = lax.broadcasted_iota(jnp.int32, (384, 1), 0)
    k, i = r // 48, lax.rem(r, 48)
    narrow = (i // 6) * 48 + k * 6 + lax.rem(i, 6)
    wide = (4 + k // 2) * 48 + lax.rem(k, 2) * 24 + i - 24
    source = jnp.where((core == 1) & (i >= 24), wide, narrow)
    cols = lax.broadcasted_iota(jnp.int32, (384, 384), 1)
    return jnp.where(cols == source, 1.0, 0.0).astype(bf)


def reduce_kernel(G, SG, BO, PI, EP, gw, gs, bo_out, pi_out, ep_out,
                  db, own, r1, r2, slab, shares, r3, r4, sgb, sd, s1b, s2b, s3b,
                  pib, pio, pz, pf, eib, eio, ez, ef, gwv, gsv,
                  ls, ds, dr, s1, q1, s2, q2, s3, q3, s4, ss, sr, ts, tr, os_):
    x, y, z, core = coords()
    hi = z // 2
    other = 1 - core
    partner = device_at(x, y, z, other)
    across = lax.rem(z + 2, 4)
    home = device_at(x, y, across, core)
    xp = [None] + [device_at(lax.rem(x + o, 4), y, z, core) for o in (1, 2, 3)]
    yp = [None] + [device_at(x, lax.rem(y + o, 4), z, core) for o in (1, 2, 3)]
    zp = [None] + [device_at(x, y, lax.rem(z + o, 4), core) for o in (1, 2, 3)]
    enter([partner, device_at(x, y, across, other)] + xp[1:] + yp[1:] + zp[1:])
    sent = []

    def remote(src, dst, send, recv, to):
        return pltpu.make_async_remote_copy(src_ref=src, dst_ref=dst, send_sem=send, recv_sem=recv,
                                            device_id=to, device_id_type=MESH)

    def start(*a):
        c = remote(*a)
        c.start()
        sent.append(c)

    def arrived(at, sem):
        remote(at, at, s4, sem, partner).wait_recv()

    def local(src, dst, sem):
        c = pltpu.make_async_copy(src, dst, sem)
        c.start()
        return c

    def rows(gx, gy):
        return pl.ds(pl.multiple_of((gx * 4 + gy) * 48, 16), 48)
    cols = (pl.ds(0, HALF), pl.ds(HALF, HALF))
    part = pl.ds(pl.multiple_of(core * 8, 8), 8)
    part_other = pl.ds(pl.multiple_of(other * 8, 8), 8)

    def target(k, b, p):
        if k == 0:
            return lax.rem(x + b, 4), lax.rem(y + p, 4)
        return lax.rem(x + p, 4), lax.rem(y + b, 4)
    order = [(p, b, k) for p in (2, 1, 3, 0) for b in range(4) for k in (0, 1)]
    loads = {}
    start(SG, sd, ss.at[0], sr.at[0], partner)
    sg_load = local(SG, sgb, ls.at[2, 0, 0])
    for p, b, k in order:
        at = rows(*target(k, b, p))
        start(G.at[part_other, at, cols[k]], db.at[k, p, b], ds.at[k, p, b], dr.at[k, p, b], partner)
        loads[k, p, b] = local(G.at[part, at, cols[k]], own.at[k, p, b], ls.at[k, p, b])
    act = []
    for i, (src, buf, mine_buf) in enumerate(((PI, pib, pio), (EP, eib, eio))):
        for s in (0, 1):
            start(src.at[2 * s + other], buf.at[s], ts.at[i, s], tr.at[i, s], partner)
            act.append(local(src.at[2 * s + core], mine_buf.at[s], ls.at[2, 1 + i, s]))
    same = core == hi

    @pl.when(same)
    def _():
        c = pltpu.make_async_copy(BO.at[core], bo_out.at[hi], ls.at[2, 3, 0])
        c.start()
        c.wait()
        d = remote(BO.at[other], bo_out.at[hi], os_.at[0], tr.at[3, 0], partner)
        d.start()
        d.wait_send()

    @pl.when(jnp.logical_not(same))
    def _():
        copies = [remote(BO.at[s], bo_out.at[hi], os_.at[s], tr.at[3, 1], device_at(x, y, across, s)) for s in (0, 1)]
        for c in copies:
            c.start()
        for c in copies:
            c.wait_send()

    first, second = (yp, xp), (xp, yp)
    sg_load.wait()
    arrived(sd, sr.at[0])
    sgb[...] = sgb[...] + sd[...]
    for p in (1, 2, 3):
        start(sgb.at[:, lax.rem(y + p, 4)], s1b.at[p], ss.at[p], sr.at[p], yp[p])
    for p, b, k in order:
        arrived(db.at[k, p, b], dr.at[k, p, b])
        loads[k, p, b].wait()

        @pl.loop(0, 8)
        def _(i):
            db[k, p, b, i] = (db[k, p, b, i].astype(f32) + own[k, p, b, i].astype(f32)).astype(bf)
        if p:
            start(db.at[k, p, b], r1.at[k, p, b], s1.at[k, p, b], q1.at[k, p, b], first[k][p])
    for c in act:
        c.wait()
    for i, (buf, mine_buf, out, zbuf, fb) in enumerate(((pib, pio, pi_out, pz, pf), (eib, eio, ep_out, ez, ef))):
        for s in (0, 1):
            arrived(buf.at[s], tr.at[i, s])
        n = buf.shape[1] // 16

        @pl.loop(0, n)
        def _(t):
            at = pl.ds(pl.multiple_of(t * 16, 16), 16)
            mine_buf[1 - hi, at] = (mine_buf[1 - hi, at].astype(f32) + buf[1 - hi, at].astype(f32)).astype(bf)
        start(mine_buf.at[1 - hi], zbuf, ts.at[2, i], tr.at[2, i], home)

        @pl.loop(0, n)
        def _(t):
            at = pl.ds(pl.multiple_of(t * 16, 16), 16)
            fb[hi, at] = mine_buf[hi, at].astype(f32) + buf[hi, at].astype(f32)
    for b in (1, 2, 3, 0):
        for k in (0, 1):
            for p in (1, 2, 3):
                arrived(r1.at[k, p, b], q1.at[k, p, b])

            @pl.loop(0, 8)
            def _(i):
                total = db[k, 0, b, i].astype(f32)
                for p in (1, 2, 3):
                    total = total + r1[k, p, b, i].astype(f32)
                db[k, 0, b, i] = total.astype(bf)
            if b:
                start(db.at[k, 0, b], r2.at[k, b], s2.at[k, b], q2.at[k, b], second[k][b])
    total = sgb[:, y]
    for p in (1, 2, 3):
        arrived(s1b.at[p], sr.at[p])
        total = total + s1b[p]
    sgb[:, y] = total
    for b in (1, 2, 3):
        start(sgb.at[lax.rem(x + b, 4), y], s2b.at[b], ss.at[3 + b], sr.at[3 + b], xp[b])
    for k in (0, 1):
        for b in (1, 2, 3):
            arrived(r2.at[k, b], q2.at[k, b])

        @pl.loop(0, 8)
        def _(i):
            total = db[k, 0, 0, i].astype(f32)
            for b in (1, 2, 3):
                total = total + r2[k, b, i].astype(f32)
            slab[i, :, k * HALF:(k + 1) * HALF] = total.astype(bf)
    total = sgb[x, y]
    for b in (1, 2, 3):
        arrived(s2b.at[b], sr.at[3 + b])
        total = total + s2b[b]
    s3b[0] = total
    for o in (1, 2, 3):
        start(s3b.at[0], s3b.at[o], ss.at[6 + o], sr.at[6 + o], zp[o])
    shares[...] = jnp.dot(split_matrix(core), slab[...].reshape(384, D), preferred_element_type=f32).astype(bf).reshape(8, 48, D)
    for o in (1, 2, 3):
        to = member(lax.rem(z + o, 4), 0)
        start(shares.at[pl.ds(to, 2)], r3.at[o], s3.at[o], q3.at[o], zp[o])
    for o in (1, 2, 3):
        arrived(r3.at[o], q3.at[o])
    base = member(z, 0)

    def share(c):
        total = shares[base + c].astype(f32)
        for o in (1, 2, 3):
            total = total + r3[o, c].astype(f32)
        return total
    gwv[core] = share(core)
    slab[0] = share(other).astype(bf)
    start(slab.at[0], r4, s4, q3.at[0], partner)
    total = s3b[0]
    for o in (1, 2, 3):
        arrived(s3b.at[o], sr.at[6 + o])
        total = total + s3b[o]
    own_row = lax.broadcasted_iota(jnp.int32, (8, 128), 0) == member(z, core)
    gsv[...] = jnp.broadcast_to(jnp.sum(jnp.where(own_row, total, 0.0), 0, keepdims=True), (8, 128))
    for i, (zbuf, fb) in enumerate(((pz, pf), (ez, ef))):
        arrived(zbuf, tr.at[2, i])

        @pl.loop(0, zbuf.shape[0] // 16)
        def _(t):
            at = pl.ds(pl.multiple_of(t * 16, 16), 16)
            fb[1 - hi, at] = zbuf[at].astype(f32)
    arrived(r4, q3.at[0])
    gwv[other] = r4[...].astype(f32)
    outs = [local(gwv, gw, ls.at[2, 0, 0]), local(gsv, gs, ls.at[2, 0, 1]),
            local(pf, pi_out, ls.at[2, 0, 2]), local(ef, ep_out, ls.at[2, 0, 3])]

    @pl.when(core != hi)
    def _():
        arrived(bo_out.at[0], tr.at[3, 0])
    arrived(bo_out.at[0], tr.at[3, 1])
    for c in sent:
        c.wait_send()
    for c in outs:
        c.wait()


def reduce_all(G, SG, BO, PI, EP):
    any_ = pl.BlockSpec(memory_space=pl.ANY)
    DMA = pltpu.SemaphoreType.DMA
    V = pltpu.VMEM
    return pl.pallas_call(
        reduce_kernel,
        out_shape=[jax.ShapeDtypeStruct((2, 48, D), f32), jax.ShapeDtypeStruct((8, 128), f32),
                   jax.ShapeDtypeStruct((2, 112, D), bf), jax.ShapeDtypeStruct((2, 112, D), f32),
                   jax.ShapeDtypeStruct((2, 384, D), f32)],
        in_specs=[any_] * 5, out_specs=[any_] * 5,
        scratch_shapes=[
            V((2, 4, 4, 8, 48, HALF), bf), V((2, 4, 4, 8, 48, HALF), bf), V((2, 4, 4, 8, 48, HALF), bf), V((2, 4, 8, 48, HALF), bf),
            V((8, 48, D), bf), V((8, 48, D), bf), V((4, 2, 48, D), bf), V((48, D), bf),
            V((4, 4, 8, 128), f32), V((4, 4, 8, 128), f32), V((4, 4, 8, 128), f32), V((4, 8, 128), f32), V((4, 8, 128), f32),
            V((2, 112, D), bf), V((2, 112, D), bf), V((112, D), bf), V((2, 112, D), f32),
            V((2, 384, D), bf), V((2, 384, D), bf), V((384, D), bf), V((2, 384, D), f32),
            V((2, 48, D), f32), V((8, 128), f32),
            DMA((3, 4, 4)), DMA((2, 4, 4)), DMA((2, 4, 4)), DMA((2, 4, 4)), DMA((2, 4, 4)), DMA((2, 4)), DMA((2, 4)),
            DMA((4,)), DMA((4,)), DMA, DMA((10,)), DMA((10,)), DMA((4, 2)), DMA((4, 2)), DMA((2,))],
        compiler_params=pltpu.CompilerParams(collective_id=1, has_side_effects=True, vmem_limit_bytes=60 << 20),
        name="reduce_all",
    )(G, SG, BO, PI, EP)


def layer_norm(values):
    mean = jnp.mean(values, -1, keepdims=True)
    centered = values - mean
    spread = jnp.mean(centered * centered, -1, keepdims=True)
    r = lax.rsqrt(spread + EPS)
    return centered * r, r


def norm_back(e, n, r, gain):
    eg = e * gain
    return r * (eg - jnp.mean(eg, -1, keepdims=True) - n * jnp.mean(eg * n, -1, keepdims=True))


def dot(a, b):
    return jnp.dot(a, b, preferred_element_type=f32)


def dot_back(a, b):
    return lax.dot_general(a, b, (((1,), (1,)), ((), ())), preferred_element_type=f32)


def dot_grad(a, b):
    return lax.dot_general(a, b, (((0,), (0,)), ((), ())), preferred_element_type=f32).astype(bf)


def heads(v):
    return v.reshape(v.shape[0], HEADS, HEAD_DIM)


def attend(q, k, v, allowed):
    s = jnp.einsum("qhe,khe->hqk", heads(q), heads(k), preferred_element_type=f32) * SCALE
    s = jnp.where(allowed[None], s, BLOCKED)
    top = jnp.max(s, -1, keepdims=True)
    p = jnp.exp(s - top)
    total = jnp.sum(p, -1, keepdims=True)
    mixed = jnp.einsum("hqk,khe->qhe", (p / total).astype(bf), heads(v), preferred_element_type=f32)
    return mixed.reshape(q.shape).astype(bf), top + jnp.log(total)


def attend_back(q, k, v, allowed, log_total, g):
    s = jnp.einsum("qhe,khe->hqk", heads(q), heads(k), preferred_element_type=f32) * SCALE
    p = jnp.exp(jnp.where(allowed[None], s, BLOCKED) - log_total)
    dp = jnp.einsum("qhe,khe->hqk", heads(g), heads(v), preferred_element_type=f32)
    ds = (p * (dp - jnp.sum(p * dp, -1, keepdims=True))).astype(bf)
    gq = jnp.einsum("hqk,khe->qhe", ds, heads(k), preferred_element_type=f32) * SCALE
    gk = jnp.einsum("hqk,qhe->khe", ds, heads(q), preferred_element_type=f32) * SCALE
    gv = jnp.einsum("hqk,qhe->khe", p.astype(bf), heads(g), preferred_element_type=f32)
    return gq.reshape(q.shape).astype(bf), gk.reshape(k.shape).astype(bf), gv.reshape(k.shape).astype(bf)


def middle(W, vec, hidden_in_bias, tok, enc, og, seg, clip, core):
    (self_gain, self_shift, bq, bv, bo, cross_gain, cross_shift, bcq, bcv, bco, final_gain, final_shift, bho) = vec
    half = lax.dynamic_slice_in_dim
    tokens = tok.reshape(448, D).astype(f32)
    enc = enc.reshape(1536, D)
    og = og.reshape(224, D)
    places = jnp.arange(448, dtype=jnp.int32)
    my_seg = half(seg, core * 224, 224, 0)
    my_places = half(places, core * 224, 224, 0)
    self_allowed = (my_seg[:, None] == seg[None]) & (places[None] <= my_places[:, None])
    cross_allowed = my_seg[:, None] == clip[None]
    n1, rs1 = layer_norm(tokens)
    first = (n1 * self_gain + self_shift).astype(bf)
    first_q = half(first, core * 224, 224, 0)
    q = (dot(first_q, W[0]) + bq).astype(bf)
    k = dot(first, W[1]).astype(bf)
    v = (dot(first, W[2]) + bv).astype(bf)
    mixed, total = attend(q, k, v, self_allowed)
    after_self = half(tokens, core * 224, 224, 0) + dot(mixed, W[3]) + bo
    n2, rs2 = layer_norm(after_self)
    second = (n2 * cross_gain + cross_shift).astype(bf)
    cq = (dot(second, W[4]) + bcq).astype(bf)
    ck = dot(enc, W[5]).astype(bf)
    cv = (dot(enc, W[6]) + bcv).astype(bf)
    cmixed, ctotal = attend(cq, ck, cv, cross_allowed)
    after_cross = after_self + dot(cmixed, W[7]) + bco
    n3, rs3 = layer_norm(after_cross)
    third = (n3 * final_gain + final_shift).astype(bf)
    acts, g_pres, dW = [], [], [None] * 16
    g_third = jnp.zeros((224, D), f32)
    result = after_cross + bho
    g_hib = []
    for n in range(4):
        pre = dot(third, W[8 + n]) + hidden_in_bias[n]
        act, back = jax.vjp(lambda t: jax.nn.gelu(t, approximate=False), pre)
        act = act.astype(bf)
        result = result + dot(act, W[12 + n])
        dW[12 + n] = dot_grad(act, og)
        g_pre = back(dot_back(og, W[12 + n]))[0].astype(bf)
        dW[8 + n] = dot_grad(third, g_pre)
        g_third = g_third + dot_back(g_pre, W[8 + n])
        g_hib.append(jnp.sum(g_pre.astype(f32), 0))
    block_output = result.astype(bf).reshape(2, 112, D)
    ogf = og.astype(f32)
    g_bho = jnp.sum(ogf, 0)
    g_fg, g_fs = jnp.sum(g_third * n3, 0), jnp.sum(g_third, 0)
    g_cross = ogf + norm_back(g_third, n3, rs3, final_gain)
    branch = g_cross.astype(bf)
    dW[7] = dot_grad(cmixed, branch)
    g_bco = jnp.sum(branch.astype(f32), 0)
    g_cmixed = dot_back(branch, W[7]).astype(bf)
    gcq, gck, gcv = attend_back(cq, ck, cv, cross_allowed, ctotal, g_cmixed)
    dW[5] = dot_grad(enc, gck)
    dW[6] = dot_grad(enc, gcv)
    g_bcv = jnp.sum(gcv.astype(f32), 0)
    enc_grad = (dot_back(gck, W[5]) + dot_back(gcv, W[6])).astype(bf).reshape(4, 384, D)
    dW[4] = dot_grad(second, gcq)
    g_bcq = jnp.sum(gcq.astype(f32), 0)
    e2 = dot_back(gcq, W[4])
    g_cg, g_cs = jnp.sum(e2 * n2, 0), jnp.sum(e2, 0)
    g_self = g_cross + norm_back(e2, n2, rs2, cross_gain)
    branch = g_self.astype(bf)
    dW[3] = dot_grad(mixed, branch)
    g_bo = jnp.sum(branch.astype(f32), 0)
    g_mixed = dot_back(branch, W[3]).astype(bf)
    gq, gk, gv = attend_back(q, k, v, self_allowed, total, g_mixed)
    dW[0] = dot_grad(first_q, gq)
    dW[1] = dot_grad(first, gk)
    dW[2] = dot_grad(first, gv)
    g_bq, g_bv = jnp.sum(gq.astype(f32), 0), jnp.sum(gv.astype(f32), 0)
    e1 = dot_back(gk, W[1]) + dot_back(gv, W[2])
    e1 = lax.dynamic_update_slice_in_dim(e1, half(e1, core * 224, 224, 0) + dot_back(gq, W[0]), core * 224, 0)
    g_sg, g_ss = jnp.sum(e1 * n1, 0), jnp.sum(e1, 0)
    g_in = norm_back(e1, n1, rs1, self_gain)
    g_in = lax.dynamic_update_slice_in_dim(g_in, half(g_in, core * 224, 224, 0) + g_self, core * 224, 0)
    input_grad = g_in.astype(bf).reshape(4, 112, D)
    g_vec = jnp.stack([g_sg, g_ss, g_bq, g_bv, g_bo, g_cg, g_cs, g_bcq, g_bcv, g_bco, g_fg, g_fs, g_bho])
    return block_output, input_grad, enc_grad, jnp.stack(dW), g_vec, jnp.stack(g_hib)


def per_device(
    tokens, encoder_states, segments, frame_clips, out_grad,
    self_gain, self_shift, self_query, self_query_bias, self_key, self_value, self_value_bias, self_output,
    self_output_bias, cross_gain, cross_shift, cross_query, cross_query_bias, cross_key, cross_value,
    cross_value_bias, cross_output, cross_output_bias, final_gain, final_shift, hidden_in, hidden_in_bias,
    hidden_out, hidden_out_bias,
):
    seq = lax.axis_index("seq")
    hi, core = seq // 2, lax.rem(seq, 2)
    hidden = hidden_in.reshape(6, 16, 4, 48).transpose(2, 0, 1, 3).reshape(24, D)
    vectors = (self_gain, self_shift, self_query_bias, self_value_bias, self_output_bias, cross_gain, cross_shift,
               cross_query_bias, cross_value_bias, cross_output_bias, final_gain, final_shift, hidden_out_bias)
    small = jnp.pad(jnp.concatenate(vectors + (hidden_in_bias,)), (0, D - 102))[None]
    shard = jnp.concatenate([self_query, self_key, self_value, self_output, cross_query, cross_key, cross_value,
                             cross_output, hidden, hidden_out, small, jnp.zeros((15, D), bf)])
    frames = jnp.pad(encoder_states[:, 0], ((0, 0), (0, 9), (0, 0)))
    W, SM, tok, enc, og = gather_all(shard, tokens[:, 0], frames, out_grad[:, 0])
    small = SM[:, :8].reshape(128, 128).astype(f32)
    vec = small[:, :78].reshape(128, 13, 6).transpose(1, 0, 2).reshape(13, D)
    hib = small[:, 78:102].reshape(16, 4, 48).transpose(1, 0, 2).reshape(4, D)
    seg = segments[:, 0][hi]
    clip = jnp.pad(frame_clips[:, 0][hi].reshape(4, 375), ((0, 0), (0, 9)), constant_values=-1).reshape(1536)
    block_output, input_grad, enc_grad, dW, g_vec, g_hib = middle(W, vec, hib, tok, enc, og, seg, clip, core)
    g_small = jnp.concatenate([g_vec.reshape(13, 128, 6).transpose(1, 0, 2).reshape(128, 78),
                               g_hib.reshape(4, 16, 48).transpose(1, 0, 2).reshape(128, 24),
                               jnp.zeros((128, 26), f32)], 1).reshape(4, 4, 8, 128)
    gw, gs, bo, gi, ge = reduce_all(dW, g_small, block_output, input_grad, enc_grad)
    gv = [gs[0, 6 * i:6 * i + 6] for i in range(13)]
    m = [gw[0, 6 * i:6 * i + 6] for i in range(8)]
    g_hidden_in = gw[1, :24].reshape(4, 6, 16, 48).transpose(1, 2, 0, 3).reshape(6, 4 * D)
    return (bo[:, None], gi[:, None], ge[:, None, :375],
            gv[0], gv[1], m[0], gv[2], m[1], m[2], gv[3], m[3], gv[4],
            gv[5], gv[6], m[4], gv[7], m[5], m[6], gv[8], m[7], gv[9],
            gv[10], gv[11], g_hidden_in, gs[0, 78:102], gw[1, 24:], gv[12])


def solution(mesh):
    rows = P(None, "win", "seq", None)
    vector, matrix = P(("win", "seq")), P(("win", "seq"), None)
    kinds = "vvmvmmvmvvvmvmmvmvvvmvmv"
    weights = tuple(matrix if kind == "m" else vector for kind in kinds)
    in_specs = (rows, rows, P(None, "win", None), P(None, "win", None), rows) + weights
    return jax.shard_map(per_device, mesh=mesh, in_specs=in_specs, out_specs=(rows, rows, rows) + weights, check_vma=False)
```

```python
from functools import partial

import jax
import jax.numpy as jnp
from jax import lax
from jax.experimental import pallas as pl
from jax.experimental.pallas import tpu as pltpu
from jax.sharding import PartitionSpec as P

bf, f32 = jnp.bfloat16, jnp.float32
HEADS, HEAD_DIM = 12, 64
EPS = 1e-05
SCALE = 0.125
BLOCKED = -1e30
MESH = pl.DeviceIdType.MESH
PIECES, ROWS, D = 16, 48, 768
HALF = D // 2


def coords():
    win, seq = lax.axis_index("win"), lax.axis_index("seq")
    x, y = win // 8, lax.rem(win // 2, 4)
    z = (seq // 2) * 2 + lax.rem(win, 2)
    return x, y, z, lax.rem(seq, 2)


def device_at(x, y, z, core):
    return (x * 8 + y * 2 + lax.rem(z, 2), (z // 2) * 2 + core)


def member(z, core):
    return lax.rem(z, 2) * 4 + (z // 2) * 2 + core


def enter(peers):
    barrier = pltpu.get_barrier_semaphore()
    for peer in peers:
        pl.semaphore_signal(barrier, inc=1, device_id=peer, device_id_type=MESH)
    pl.semaphore_wait(barrier, len(peers))


def relayout_matrix():
    r = lax.broadcasted_iota(jnp.int32, (784, 1), 0)
    piece, at = r // 48, lax.rem(r, 48)
    narrow = (at // 6) * 112 + piece * 6 + lax.rem(at, 6)
    wide = ((piece - 12) * 2 + at // 24) * 112 + 72 + lax.rem(at, 24)
    small = lax.rem(at, 8) * 112 + 96
    source = jnp.where(piece < 12, narrow, jnp.where(piece < 16, wide, small))
    cols = lax.broadcasted_iota(jnp.int32, (784, 896), 1)
    return jnp.where(cols == source, 1.0, 0.0).astype(bf)


def gather_kernel(shard, tok_in, enc_in, og_in, W, SM, tok, enc, og, zbuf, slab, smbuf,
                  zs, zr, ds, dr, ls, s1, r1, s2, r2, ss1, sr1, ss2, sr2, cs, cr, es, er, fs, fr):
    x, y, z, core = coords()
    hi = z // 2
    other = 1 - core
    partner = device_at(x, y, z, other)
    across = lax.rem(z + 2, 4)
    xp = [device_at(lax.rem(x + o, 4), y, z, core) for o in (1, 2, 3)]
    yp = [device_at(x, lax.rem(y + o, 4), z, core) for o in (1, 2, 3)]
    zp = [device_at(x, y, lax.rem(z + o, 4), core) for o in (1, 2, 3)]
    enter([partner, device_at(x, y, across, other)] + xp + yp + zp)

    def remote(src, dst, send, recv, to):
        return pltpu.make_async_remote_copy(src_ref=src, dst_ref=dst, send_sem=send, recv_sem=recv,
                                            device_id=to, device_id_type=MESH)
    sent = []

    def start(*a):
        c = remote(*a)
        c.start()
        sent.append(c)
        return c
    me = member(z, core)
    mine = pltpu.make_async_copy(shard, zbuf.at[me], ls.at[0])
    mine.start()
    for o in (1, 2, 3):
        start(shard, zbuf.at[me], zs.at[o], zr.at[o], zp[o - 1])
    start(shard, zbuf.at[me], ds.at[0], dr.at[0], partner)

    block = hi * 2 + core
    locals_ = []

    def local(src, dst, sem):
        c = pltpu.make_async_copy(src, dst, sem)
        c.start()
        locals_.append(c)
    home = device_at(x, y, across, core)
    for i, (src, dst) in enumerate(((tok_in, tok), (enc_in, enc))):
        start(src.at[1 - hi], dst.at[block], es.at[i], er.at[i], home)
        start(src.at[hi], dst.at[block], es.at[2 + i], er.at[2 + i], partner)
        local(src.at[hi], dst.at[block], ls.at[1 + i])
    start(og_in.at[1 - hi], og.at[core], es.at[4], er.at[4 + core], device_at(x, y, across, hi))

    @pl.when(core == hi)
    def _():
        c = pltpu.make_async_copy(og_in.at[hi], og.at[core], ls.at[3])
        c.start()
        c.wait()

    @pl.when(core != hi)
    def _():
        c = remote(og_in.at[hi], og.at[core], es.at[5], er.at[6], partner)
        c.start()
        c.wait_send()
    for o in (1, 2, 3):
        remote(shard, zbuf.at[me], zs.at[o], zr.at[o], zp[0]).wait_recv()
        src = member(lax.rem(z + 4 - o, 4), core)
        start(zbuf.at[src], zbuf.at[src], ds.at[o], dr.at[o], partner)
    for o in range(4):
        remote(shard, zbuf.at[me], ds.at[o], dr.at[o], partner).wait_recv()
    mine.wait()
    spread = jnp.dot(relayout_matrix(), zbuf[...].reshape(896, D), preferred_element_type=jnp.float32).astype(bf)
    slab[...] = spread[:768].reshape(PIECES, ROWS, D)
    smbuf[...] = spread[768:, :128]

    def rows(gx, gy):
        return pl.ds(pl.multiple_of((gx * 4 + gy) * 48, 16), 48)
    part = pl.ds(pl.multiple_of(core * 8, 8), 8)
    cols = (pl.ds(0, HALF), pl.ds(HALF, HALF))
    local(slab, W.at[:, rows(x, y), :], ls.at[4])
    local(smbuf, SM.at[x * 4 + y], ls.at[5])
    first, second = (xp, yp), (yp, xp)
    for o in (1, 2, 3):
        for k in (0, 1):
            start(slab.at[part, :, cols[k]], W.at[part, rows(x, y), cols[k]], s1.at[k, o], r1.at[k, o], first[k][o - 1])
        start(smbuf, SM.at[x * 4 + y], ss1.at[o], sr1.at[o], xp[o - 1])
    for o in (1, 2, 3):
        for k in (0, 1):
            start(slab.at[part, :, cols[k]], W.at[part, rows(x, y), cols[k]], s2.at[k, 0, o], r2.at[k, 0, o], second[k][o - 1])
        start(smbuf, SM.at[x * 4 + y], ss2.at[0, o], sr2.at[0, o], yp[o - 1])

    def origin(k, b, p):
        if k == 0:
            return lax.rem(x + 4 - b, 4), lax.rem(y + 4 - p, 4)
        return lax.rem(x + 4 - p, 4), lax.rem(y + 4 - b, 4)

    def hand_over(k, b, p):
        at = W.at[part, rows(*origin(k, b, p)), cols[k]]
        start(at, at, cs.at[k, b * 4 + p], cr.at[k, b * 4 + p], partner)
    for b in (1, 2, 3):
        for k in (0, 1):
            at = W.at[part, rows(*origin(k, b, 0)), cols[k]]
            remote(at, at, s1.at[k, b], r1.at[k, b], partner).wait_recv()
            for p in (1, 2, 3):
                start(at, at, s2.at[k, b, p], r2.at[k, b, p], second[k][p - 1])
            hand_over(k, b, 0)
        at = SM.at[lax.rem(x + 4 - b, 4) * 4 + y]
        remote(at, at, ss1.at[b], sr1.at[b], partner).wait_recv()
        for p in (1, 2, 3):
            start(at, at, ss2.at[b, p], sr2.at[b, p], yp[p - 1])
    for i, (src, dst) in enumerate(((tok_in, tok), (enc_in, enc))):
        far = dst.at[(1 - hi) * 2 + core]
        remote(far, far, es.at[i], er.at[i], partner).wait_recv()
        start(far, far, fs.at[i], fr.at[i], partner)
    for b in range(4):
        for p in (1, 2, 3):
            for k in (0, 1):
                at = W.at[part, rows(*origin(k, b, p)), cols[k]]
                remote(at, at, s2.at[k, b, p], r2.at[k, b, p], partner).wait_recv()
                hand_over(k, b, p)
            at = SM.at[0]
            remote(at, at, ss2.at[b, p], sr2.at[b, p], partner).wait_recv()
    for k in (0, 1):
        for q in range(1, 16):
            at = W.at[part, rows(x, y), cols[k]]
            remote(at, at, cs.at[k, q], cr.at[k, q], partner).wait_recv()
    for i, dst in enumerate((tok, enc)):
        remote(dst.at[0], dst.at[0], es.at[2 + i], er.at[2 + i], partner).wait_recv()
        remote(dst.at[0], dst.at[0], fs.at[i], fr.at[i], partner).wait_recv()
    at = og.at[0]

    @pl.when(hi == core)
    def _():
        remote(at, at, es.at[4], er.at[6], partner).wait_recv()

    @pl.when(hi != core)
    def _():
        for s in (0, 1):
            remote(at, at, es.at[4], er.at[4 + s], partner).wait_recv()
    for c in sent:
        c.wait_send()
    for c in locals_:
        c.wait()


def gather_all(shard, tok, enc, og):
    any_ = pl.BlockSpec(memory_space=pl.ANY)
    DMA = pltpu.SemaphoreType.DMA
    return pl.pallas_call(
        gather_kernel,
        out_shape=[jax.ShapeDtypeStruct((16, D, D), bf), jax.ShapeDtypeStruct((16, 16, 128), bf),
                   jax.ShapeDtypeStruct((4, 112, D), bf), jax.ShapeDtypeStruct((4, 384, D), bf),
                   jax.ShapeDtypeStruct((2, 112, D), bf)],
        in_specs=[any_] * 4, out_specs=[any_] * 5,
        scratch_shapes=[pltpu.VMEM((8, 112, D), bf), pltpu.VMEM((16, 48, D), bf), pltpu.VMEM((16, 128), bf),
                        DMA((4,)), DMA((4,)), DMA((4,)), DMA((4,)), DMA((6,)),
                        DMA((2, 4)), DMA((2, 4)), DMA((2, 4, 4)), DMA((2, 4, 4)),
                        DMA((4,)), DMA((4,)), DMA((4, 4)), DMA((4, 4)),
                        DMA((2, 16)), DMA((2, 16)), DMA((6,)), DMA((7,)), DMA((2,)), DMA((2,))],
        compiler_params=pltpu.CompilerParams(collective_id=0, has_side_effects=True, vmem_limit_bytes=40 << 20),
        name="gather_all",
    )(shard, tok, enc, og)


def split_matrix(core):
    r = lax.broadcasted_iota(jnp.int32, (384, 1), 0)
    k, i = r // 48, lax.rem(r, 48)
    narrow = (i // 6) * 48 + k * 6 + lax.rem(i, 6)
    wide = (4 + k // 2) * 48 + lax.rem(k, 2) * 24 + i - 24
    source = jnp.where((core == 1) & (i >= 24), wide, narrow)
    cols = lax.broadcasted_iota(jnp.int32, (384, 384), 1)
    return jnp.where(cols == source, 1.0, 0.0).astype(bf)


def reduce_kernel(G, SG, BO, PI, EP, gw, gs, bo_out, pi_out, ep_out,
                  db, own, r1, r2, slab, shares, r3, r4, sgb, sd, s1b, s2b, s3b,
                  pib, pio, pz, pf, eib, eio, ez, ef, gwv, gsv,
                  ls, ds, dr, s1, q1, s2, q2, s3, q3, s4, ss, sr, ts, tr, os_):
    x, y, z, core = coords()
    hi = z // 2
    other = 1 - core
    partner = device_at(x, y, z, other)
    across = lax.rem(z + 2, 4)
    home = device_at(x, y, across, core)
    xp = [None] + [device_at(lax.rem(x + o, 4), y, z, core) for o in (1, 2, 3)]
    yp = [None] + [device_at(x, lax.rem(y + o, 4), z, core) for o in (1, 2, 3)]
    zp = [None] + [device_at(x, y, lax.rem(z + o, 4), core) for o in (1, 2, 3)]
    enter([partner, device_at(x, y, across, other)] + xp[1:] + yp[1:] + zp[1:])
    sent = []

    def remote(src, dst, send, recv, to):
        return pltpu.make_async_remote_copy(src_ref=src, dst_ref=dst, send_sem=send, recv_sem=recv,
                                            device_id=to, device_id_type=MESH)

    def start(*a):
        c = remote(*a)
        c.start()
        sent.append(c)

    def arrived(at, sem):
        remote(at, at, s4, sem, partner).wait_recv()

    def local(src, dst, sem):
        c = pltpu.make_async_copy(src, dst, sem)
        c.start()
        return c

    def rows(gx, gy):
        return pl.ds(pl.multiple_of((gx * 4 + gy) * 48, 16), 48)
    cols = (pl.ds(0, HALF), pl.ds(HALF, HALF))
    part = pl.ds(pl.multiple_of(core * 8, 8), 8)
    part_other = pl.ds(pl.multiple_of(other * 8, 8), 8)

    def target(k, b, p):
        if k == 0:
            return lax.rem(x + b, 4), lax.rem(y + p, 4)
        return lax.rem(x + p, 4), lax.rem(y + b, 4)
    order = [(p, b, k) for p in (2, 1, 3, 0) for b in range(4) for k in (0, 1)]
    loads = {}
    start(SG, sd, ss.at[0], sr.at[0], partner)
    sg_load = local(SG, sgb, ls.at[2, 0, 0])
    for p, b, k in order:
        at = rows(*target(k, b, p))
        start(G.at[part_other, at, cols[k]], db.at[k, p, b], ds.at[k, p, b], dr.at[k, p, b], partner)
        loads[k, p, b] = local(G.at[part, at, cols[k]], own.at[k, p, b], ls.at[k, p, b])
    act = []
    for i, (src, buf, mine_buf) in enumerate(((PI, pib, pio), (EP, eib, eio))):
        for s in (0, 1):
            start(src.at[2 * s + other], buf.at[s], ts.at[i, s], tr.at[i, s], partner)
            act.append(local(src.at[2 * s + core], mine_buf.at[s], ls.at[2, 1 + i, s]))
    same = core == hi

    @pl.when(same)
    def _():
        c = pltpu.make_async_copy(BO.at[core], bo_out.at[hi], ls.at[2, 3, 0])
        c.start()
        c.wait()
        d = remote(BO.at[other], bo_out.at[hi], os_.at[0], tr.at[3, 0], partner)
        d.start()
        d.wait_send()

    @pl.when(jnp.logical_not(same))
    def _():
        copies = [remote(BO.at[s], bo_out.at[hi], os_.at[s], tr.at[3, 1], device_at(x, y, across, s)) for s in (0, 1)]
        for c in copies:
            c.start()
        for c in copies:
            c.wait_send()

    first, second = (yp, xp), (xp, yp)
    sg_load.wait()
    arrived(sd, sr.at[0])
    sgb[...] = sgb[...] + sd[...]
    for p in (1, 2, 3):
        start(sgb.at[:, lax.rem(y + p, 4)], s1b.at[p], ss.at[p], sr.at[p], yp[p])
    for p, b, k in order:
        arrived(db.at[k, p, b], dr.at[k, p, b])
        loads[k, p, b].wait()

        @pl.loop(0, 8)
        def _(i):
            db[k, p, b, i] = (db[k, p, b, i].astype(f32) + own[k, p, b, i].astype(f32)).astype(bf)
        if p:
            start(db.at[k, p, b], r1.at[k, p, b], s1.at[k, p, b], q1.at[k, p, b], first[k][p])
    for c in act:
        c.wait()
    for i, (buf, mine_buf, out, zbuf, fb) in enumerate(((pib, pio, pi_out, pz, pf), (eib, eio, ep_out, ez, ef))):
        for s in (0, 1):
            arrived(buf.at[s], tr.at[i, s])
        n = buf.shape[1] // 16

        @pl.loop(0, n)
        def _(t):
            at = pl.ds(pl.multiple_of(t * 16, 16), 16)
            mine_buf[1 - hi, at] = (mine_buf[1 - hi, at].astype(f32) + buf[1 - hi, at].astype(f32)).astype(bf)
        start(mine_buf.at[1 - hi], zbuf, ts.at[2, i], tr.at[2, i], home)

        @pl.loop(0, n)
        def _(t):
            at = pl.ds(pl.multiple_of(t * 16, 16), 16)
            fb[hi, at] = mine_buf[hi, at].astype(f32) + buf[hi, at].astype(f32)
    for b in (1, 2, 3, 0):
        for k in (0, 1):
            for p in (1, 2, 3):
                arrived(r1.at[k, p, b], q1.at[k, p, b])

            @pl.loop(0, 8)
            def _(i):
                total = db[k, 0, b, i].astype(f32)
                for p in (1, 2, 3):
                    total = total + r1[k, p, b, i].astype(f32)
                db[k, 0, b, i] = total.astype(bf)
            if b:
                start(db.at[k, 0, b], r2.at[k, b], s2.at[k, b], q2.at[k, b], second[k][b])
    total = sgb[:, y]
    for p in (1, 2, 3):
        arrived(s1b.at[p], sr.at[p])
        total = total + s1b[p]
    sgb[:, y] = total
    for b in (1, 2, 3):
        start(sgb.at[lax.rem(x + b, 4), y], s2b.at[b], ss.at[3 + b], sr.at[3 + b], xp[b])
    for k in (0, 1):
        for b in (1, 2, 3):
            arrived(r2.at[k, b], q2.at[k, b])

        @pl.loop(0, 8)
        def _(i):
            total = db[k, 0, 0, i].astype(f32)
            for b in (1, 2, 3):
                total = total + r2[k, b, i].astype(f32)
            slab[i, :, k * HALF:(k + 1) * HALF] = total.astype(bf)
    total = sgb[x, y]
    for b in (1, 2, 3):
        arrived(s2b.at[b], sr.at[3 + b])
        total = total + s2b[b]
    s3b[0] = total
    for o in (1, 2, 3):
        start(s3b.at[0], s3b.at[o], ss.at[6 + o], sr.at[6 + o], zp[o])
    shares[...] = jnp.dot(split_matrix(core), slab[...].reshape(384, D), preferred_element_type=f32).astype(bf).reshape(8, 48, D)
    for o in (1, 2, 3):
        to = member(lax.rem(z + o, 4), 0)
        start(shares.at[pl.ds(to, 2)], r3.at[o], s3.at[o], q3.at[o], zp[o])
    for o in (1, 2, 3):
        arrived(r3.at[o], q3.at[o])
    base = member(z, 0)

    def share(c):
        total = shares[base + c].astype(f32)
        for o in (1, 2, 3):
            total = total + r3[o, c].astype(f32)
        return total
    gwv[core] = share(core)
    slab[0] = share(other).astype(bf)
    start(slab.at[0], r4, s4, q3.at[0], partner)
    total = s3b[0]
    for o in (1, 2, 3):
        arrived(s3b.at[o], sr.at[6 + o])
        total = total + s3b[o]
    own_row = lax.broadcasted_iota(jnp.int32, (8, 128), 0) == member(z, core)
    gsv[...] = jnp.broadcast_to(jnp.sum(jnp.where(own_row, total, 0.0), 0, keepdims=True), (8, 128))
    for i, (zbuf, fb) in enumerate(((pz, pf), (ez, ef))):
        arrived(zbuf, tr.at[2, i])

        @pl.loop(0, zbuf.shape[0] // 16)
        def _(t):
            at = pl.ds(pl.multiple_of(t * 16, 16), 16)
            fb[1 - hi, at] = zbuf[at].astype(f32)
    arrived(r4, q3.at[0])
    gwv[other] = r4[...].astype(f32)
    outs = [local(gwv, gw, ls.at[2, 0, 0]), local(gsv, gs, ls.at[2, 0, 1]),
            local(pf, pi_out, ls.at[2, 0, 2]), local(ef, ep_out, ls.at[2, 0, 3])]

    @pl.when(core != hi)
    def _():
        arrived(bo_out.at[0], tr.at[3, 0])
    arrived(bo_out.at[0], tr.at[3, 1])
    for c in sent:
        c.wait_send()
    for c in outs:
        c.wait()


def reduce_all(G, SG, BO, PI, EP):
    any_ = pl.BlockSpec(memory_space=pl.ANY)
    DMA = pltpu.SemaphoreType.DMA
    V = pltpu.VMEM
    return pl.pallas_call(
        reduce_kernel,
        out_shape=[jax.ShapeDtypeStruct((2, 48, D), f32), jax.ShapeDtypeStruct((8, 128), f32),
                   jax.ShapeDtypeStruct((2, 112, D), bf), jax.ShapeDtypeStruct((2, 112, D), f32),
                   jax.ShapeDtypeStruct((2, 384, D), f32)],
        in_specs=[any_] * 5, out_specs=[any_] * 5,
        scratch_shapes=[
            V((2, 4, 4, 8, 48, HALF), bf), V((2, 4, 4, 8, 48, HALF), bf), V((2, 4, 4, 8, 48, HALF), bf), V((2, 4, 8, 48, HALF), bf),
            V((8, 48, D), bf), V((8, 48, D), bf), V((4, 2, 48, D), bf), V((48, D), bf),
            V((4, 4, 8, 128), f32), V((4, 4, 8, 128), f32), V((4, 4, 8, 128), f32), V((4, 8, 128), f32), V((4, 8, 128), f32),
            V((2, 112, D), bf), V((2, 112, D), bf), V((112, D), bf), V((2, 112, D), f32),
            V((2, 384, D), bf), V((2, 384, D), bf), V((384, D), bf), V((2, 384, D), f32),
            V((2, 48, D), f32), V((8, 128), f32),
            DMA((3, 4, 4)), DMA((2, 4, 4)), DMA((2, 4, 4)), DMA((2, 4, 4)), DMA((2, 4, 4)), DMA((2, 4)), DMA((2, 4)),
            DMA((4,)), DMA((4,)), DMA, DMA((10,)), DMA((10,)), DMA((4, 2)), DMA((4, 2)), DMA((2,))],
        compiler_params=pltpu.CompilerParams(collective_id=1, has_side_effects=True, vmem_limit_bytes=60 << 20),
        name="reduce_all",
    )(G, SG, BO, PI, EP)


WIDE = 12 * HEAD_DIM
KEYS, FRAMES, SPAN = 448, 1536, 224


def dot(a, b):
    return jnp.dot(a, b, preferred_element_type=f32)


def dot_back(a, b):
    return lax.dot_general(a, b, (((1,), (1,)), ((), ())), preferred_element_type=f32)


def dot_grad(a, b):
    return lax.dot_general(a, b, (((0,), (0,)), ((), ())), preferred_element_type=f32)


def normed(values):
    mean = jnp.mean(values, -1, keepdims=True)
    centered = values - mean
    spread = jnp.mean(centered * centered, -1, keepdims=True)
    r = lax.rsqrt(spread + EPS)
    return centered * r, r


def norm_back(e, n, r, gain):
    eg = e * gain
    return r * (eg - jnp.mean(eg, -1, keepdims=True) - n * jnp.mean(eg * n, -1, keepdims=True))


def row_sum(v):
    return jnp.sum(v, 0, keepdims=True)


def one_head(v, e):
    at = lax.broadcasted_iota(jnp.int32, v.shape, 1)
    return jnp.where((at < 64) if e == 0 else (at >= 64), v, jnp.zeros_like(v))


def two_heads(a, b):
    at = lax.broadcasted_iota(jnp.int32, a.shape, 1)
    return jnp.where(at < 64, a, b)


def attend(q, k, v, bias, mixed, lse):
    @pl.loop(0, 6)
    def _(j):
        at = pl.ds(pl.multiple_of(j * 128, 128), 128)
        qp, kp, vp = q[:, at], k[:, at], v[:, at]
        outs, logs = [], []
        for e in (0, 1):
            s = dot_back(one_head(qp, e), kp) + bias[...]
            top = jnp.max(s, 1, keepdims=True)
            p = jnp.exp(s - top)
            total = jnp.sum(p, 1, keepdims=True)
            outs.append(dot(p.astype(bf), vp) / total)
            logs.append(top + jnp.log(total))
        mixed[:, at] = two_heads(*outs).astype(bf)
        lse[j] = two_heads(*[jnp.broadcast_to(log, (SPAN, 128)) for log in logs])


def attend_back(q, k, v, bias, mixed, lse, g, gq, gk, gv):
    @pl.loop(0, 6)
    def _(j):
        at = pl.ds(pl.multiple_of(j * 128, 128), 128)
        qp, kp, vp, gp = q[:, at], k[:, at], v[:, at], g[:, at]
        product = gp.astype(f32) * mixed[:, at].astype(f32)
        dq, dk, dv = [], 0.0, 0.0
        for e in (0, 1):
            qe, ge = one_head(qp, e), one_head(gp, e)
            s = dot_back(qe, kp) + bias[...]
            p = jnp.exp(s - lse[j, :, 64 * e:64 * e + 1])
            dp = dot_back(ge, vp)
            delta = jnp.sum(one_head(product, e), 1, keepdims=True)
            ds = (p * (dp - delta)).astype(bf)
            dk = dk + dot_grad(ds, qe)
            dv = dv + dot_grad(p.astype(bf), ge)
            dq.append(dot(ds, kp) * SCALE)
        gk[:, at] = dk.astype(bf)
        gv[:, at] = dv.astype(bf)
        gq[:, at] = two_heads(*dq).astype(bf)


def blocks(total, step, body):
    @pl.loop(0, total // step)
    def _(i):
        body(pl.ds(pl.multiple_of(i * step, step), step))


def layer_kernel(W, vec, hib, tok, enc_hbm, og, qcol, krow, crow, G, BO, PI, EP, gvec, ghib,
                 w, enc, first, q, k, v, mixed, lse, second, cq, ck, cv, cmixed, clse, after_self, stream, third,
                 acc, bias_s, bias_c, g, gq, gk, gv, gck, gcv, wide, wsem, gsem, esem):
    core = lax.rem(lax.axis_index("seq"), 2)
    mine = pl.ds(pl.multiple_of(core * SPAN, 32), SPAN)
    loads, stores = {}, {}
    enc_load = pltpu.make_async_copy(enc_hbm, enc, esem)
    for u in (1, 2, 0, 3, 4, 5, 6, 7, 8, 12, 9, 13, 10, 14, 11, 15):
        loads[u] = pltpu.make_async_copy(W.at[u], w.at[u], wsem.at[u])
        loads[u].start()
        if u == 3:
            enc_load.start()

    def ready(u):
        loads[u].wait()
        return w.at[u]

    def put(u):
        stores[u] = pltpu.make_async_copy(w.at[u], G.at[u], gsem.at[u])
        stores[u].start()

    def weight_grad(u, a, b):
        def body(at):
            w[u, :, at] = dot_grad(a[...], b[:, at]).astype(bf)
        blocks(D, 256, body)
        put(u)

    same = qcol[...] == krow[...]
    key_at = lax.broadcasted_iota(jnp.int32, (SPAN, KEYS), 1)
    query_at = lax.broadcasted_iota(jnp.int32, (SPAN, KEYS), 0) + core * SPAN
    bias_s[...] = jnp.where(same & (key_at <= query_at), 0.0, BLOCKED)
    bias_c[...] = jnp.where(qcol[...] == crow[...], 0.0, BLOCKED)

    def norm_first(at):
        n, _ = normed(tok[at].astype(f32))
        first[at] = (n * vec[0:1] + vec[1:2]).astype(bf)
    blocks(KEYS, 112, norm_first)
    wk = ready(1)

    def keys(at):
        k[at] = dot(first[at], wk[...]).astype(bf)
    blocks(KEYS, SPAN, keys)
    wv = ready(2)

    def values(at):
        v[at] = (dot(first[at], wv[...]) + vec[3:4]).astype(bf)
    blocks(KEYS, SPAN, values)
    wq = ready(0)
    q[...] = (dot(first[mine], wq[...]) + vec[2:3]).astype(bf) * SCALE
    attend(q, k, v, bias_s, mixed, lse)
    wo = ready(3)
    after_self[...] = tok[mine].astype(f32) + dot(mixed[...], wo[...]) + vec[4:5]
    n, _ = normed(after_self[...])
    second[...] = (n * vec[5:6] + vec[6:7]).astype(bf)
    wcq = ready(4)
    cq[...] = (dot(second[...], wcq[...]) + vec[7:8]).astype(bf) * SCALE
    enc_load.wait()
    wck = ready(5)

    def cross_keys(at):
        ck[at] = dot(enc[at], wck[...]).astype(bf)
    blocks(FRAMES, 384, cross_keys)
    wcv = ready(6)

    def cross_values(at):
        cv[at] = (dot(enc[at], wcv[...]) + vec[8:9]).astype(bf)
    blocks(FRAMES, 384, cross_values)
    attend(cq, ck, cv, bias_c, cmixed, clse)
    wco = ready(7)
    stream[...] = after_self[...] + dot(cmixed[...], wco[...]) + vec[9:10]
    n, r = normed(stream[...])
    third[...] = (n * vec[10:11] + vec[11:12]).astype(bf)
    acc[0] = stream[...] + vec[12:13]
    acc[1] = jnp.zeros((SPAN, D), f32)
    for i in range(4):
        w1, w2 = ready(8 + i), ready(12 + i)
        pre = dot(third[...], w1[...]) + hib[i:i + 1]
        cdf = 0.5 * (1.0 + lax.erf(pre * 0.7071067811865476))
        act = (pre * cdf).astype(bf)
        slope = cdf + pre * (0.3989422804014327 * jnp.exp(-0.5 * pre * pre))
        wide[0] = act
        acc[0] += dot(act, w2[...])
        g_pre = (dot_back(og[...], w2[...]) * slope).astype(bf)
        wide[1] = g_pre
        weight_grad(12 + i, wide.at[0], og)
        ghib[i:i + 1] = row_sum(g_pre.astype(f32))
        acc[1] += dot_back(g_pre, w1[...])
        weight_grad(8 + i, third, wide.at[1])
    BO[...] = acc[0].astype(bf)
    e = acc[1]
    ogf = og[...].astype(f32)
    n, r = normed(stream[...])
    gvec[12:13] = row_sum(ogf)
    gvec[10:11] = row_sum(e * n)
    gvec[11:12] = row_sum(e)
    stream[...] = ogf + norm_back(e, n, r, vec[10:11])
    wide[0] = stream[...].astype(bf)
    gvec[9:10] = row_sum(wide[0].astype(f32))
    g[...] = dot_back(wide[0], wco[...]).astype(bf)
    weight_grad(7, cmixed, wide.at[0])
    attend_back(cq, ck, cv, bias_c, cmixed, clse, g, gq, gck, gcv)
    gvec[7:8] = row_sum(gq[...].astype(f32))
    gvec[8:9] = row_sum(gcv[...].astype(f32))

    def frames_back(at):
        EP[at] = (dot_back(gck[at], wck[...]) + dot_back(gcv[at], wcv[...])).astype(bf)
    blocks(FRAMES, 384, frames_back)
    weight_grad(5, enc, gck)
    weight_grad(6, enc, gcv)
    e = dot_back(gq[...], wcq[...])
    weight_grad(4, second, gq)
    n, r = normed(after_self[...])
    gvec[5:6] = row_sum(e * n)
    gvec[6:7] = row_sum(e)
    stream[...] += norm_back(e, n, r, vec[5:6])
    wide[0] = stream[...].astype(bf)
    gvec[4:5] = row_sum(wide[0].astype(f32))
    g[...] = dot_back(wide[0], wo[...]).astype(bf)
    weight_grad(3, mixed, wide.at[0])
    attend_back(q, k, v, bias_s, mixed, lse, g, gq, gk, gv)
    gvec[2:3] = row_sum(gq[...].astype(f32))
    gvec[3:4] = row_sum(gv[...].astype(f32))
    gvec[0:2] = jnp.zeros((2, D), f32)
    acc[0] = dot_back(gq[...], wq[...])

    for h in (0, 1):
        at = pl.ds(h * SPAN, SPAN)
        own = core == h
        e = dot_back(gk[at], wk[...]) + dot_back(gv[at], wv[...]) + jnp.where(own, acc[0], 0.0)
        n, r = normed(tok[at].astype(f32))
        gvec[0:1] += row_sum(e * n)
        gvec[1:2] += row_sum(e)
        PI[at] = (norm_back(e, n, r, vec[0:1]) + jnp.where(own, stream[...], 0.0)).astype(bf)
    wide[0] = first[mine]
    weight_grad(0, wide.at[0], gq)
    weight_grad(1, first, gk)
    weight_grad(2, first, gv)
    for u in range(16):
        stores[u].wait()


def middle(W, vec, hidden_in_bias, tok, enc, og, seg, clip, core):
    V, DMA, S = pltpu.VMEM, pltpu.SemaphoreType.DMA, jax.ShapeDtypeStruct
    vec = jnp.pad(vec, ((0, 3), (0, 0)))
    qcol = lax.dynamic_slice_in_dim(seg, core * SPAN, SPAN, 0).reshape(SPAN, 1)
    vm, hbm = pl.BlockSpec(memory_space=pltpu.VMEM), pl.BlockSpec(memory_space=pl.ANY)
    G, BO, PI, EP, gvec, ghib = pl.pallas_call(
        layer_kernel,
        out_shape=[S((16, D, D), bf), S((SPAN, D), bf), S((KEYS, D), bf), S((FRAMES, D), bf), S((16, D), f32), S((4, D), f32)],
        in_specs=[hbm, vm, vm, vm, hbm, vm, vm, vm, vm], out_specs=[hbm, vm, vm, vm, vm, vm],
        scratch_shapes=[
            V((16, D, D), bf), V((FRAMES, D), bf), V((KEYS, D), bf), V((SPAN, D), bf), V((KEYS, D), bf), V((KEYS, D), bf),
            V((SPAN, D), bf), V((6, SPAN, 128), f32), V((SPAN, D), bf), V((SPAN, D), bf), V((FRAMES, D), bf), V((FRAMES, D), bf),
            V((SPAN, D), bf), V((6, SPAN, 128), f32), V((SPAN, D), f32), V((SPAN, D), f32), V((SPAN, D), bf),
            V((2, SPAN, D), f32), V((SPAN, KEYS), f32), V((SPAN, FRAMES), f32), V((SPAN, D), bf), V((SPAN, D), bf),
            V((KEYS, D), bf), V((KEYS, D), bf), V((FRAMES, D), bf), V((FRAMES, D), bf), V((2, SPAN, D), bf),
            DMA((16,)), DMA((16,)), DMA],
        compiler_params=pltpu.CompilerParams(vmem_limit_bytes=60 << 20),
        name="layer",
    )(W, vec, hidden_in_bias, tok.reshape(KEYS, D), enc.reshape(FRAMES, D), og.reshape(SPAN, D), qcol, seg[None], clip[None])
    return BO.reshape(2, 112, D), PI.reshape(4, 112, D), EP.reshape(4, 384, D), G, gvec[:13], ghib


def per_device(
    tokens, encoder_states, segments, frame_clips, out_grad,
    self_gain, self_shift, self_query, self_query_bias, self_key, self_value, self_value_bias, self_output,
    self_output_bias, cross_gain, cross_shift, cross_query, cross_query_bias, cross_key, cross_value,
    cross_value_bias, cross_output, cross_output_bias, final_gain, final_shift, hidden_in, hidden_in_bias,
    hidden_out, hidden_out_bias,
):
    seq = lax.axis_index("seq")
    hi, core = seq // 2, lax.rem(seq, 2)
    hidden = hidden_in.reshape(6, 16, 4, 48).transpose(2, 0, 1, 3).reshape(24, D)
    vectors = (self_gain, self_shift, self_query_bias, self_value_bias, self_output_bias, cross_gain, cross_shift,
               cross_query_bias, cross_value_bias, cross_output_bias, final_gain, final_shift, hidden_out_bias)
    small = jnp.pad(jnp.concatenate(vectors + (hidden_in_bias,)), (0, D - 102))[None]
    shard = jnp.concatenate([self_query, self_key, self_value, self_output, cross_query, cross_key, cross_value,
                             cross_output, hidden, hidden_out, small, jnp.zeros((15, D), bf)])
    frames = jnp.pad(encoder_states[:, 0], ((0, 0), (0, 9), (0, 0)))
    W, SM, tok, enc, og = gather_all(shard, tokens[:, 0], frames, out_grad[:, 0])
    small = SM[:, :8].reshape(128, 128).astype(f32)
    vec = small[:, :78].reshape(128, 13, 6).transpose(1, 0, 2).reshape(13, D)
    hib = small[:, 78:102].reshape(16, 4, 48).transpose(1, 0, 2).reshape(4, D)
    seg = segments[:, 0][hi]
    clip = jnp.pad(frame_clips[:, 0][hi].reshape(4, 375), ((0, 0), (0, 9)), constant_values=-1).reshape(1536)
    block_output, input_grad, enc_grad, dW, g_vec, g_hib = middle(W, vec, hib, tok, enc, og, seg, clip, core)
    g_small = jnp.concatenate([g_vec.reshape(13, 128, 6).transpose(1, 0, 2).reshape(128, 78),
                               g_hib.reshape(4, 16, 48).transpose(1, 0, 2).reshape(128, 24),
                               jnp.zeros((128, 26), f32)], 1).reshape(4, 4, 8, 128)
    gw, gs, bo, gi, ge = reduce_all(dW, g_small, block_output, input_grad, enc_grad)
    gv = [gs[0, 6 * i:6 * i + 6] for i in range(13)]
    m = [gw[0, 6 * i:6 * i + 6] for i in range(8)]
    g_hidden_in = gw[1, :24].reshape(4, 6, 16, 48).transpose(1, 2, 0, 3).reshape(6, 4 * D)
    return (bo[:, None], gi[:, None], ge[:, None, :375],
            gv[0], gv[1], m[0], gv[2], m[1], m[2], gv[3], m[3], gv[4],
            gv[5], gv[6], m[4], gv[7], m[5], m[6], gv[8], m[7], gv[9],
            gv[10], gv[11], g_hidden_in, gs[0, 78:102], gw[1, 24:], gv[12])


def solution(mesh):
    rows = P(None, "win", "seq", None)
    vector, matrix = P(("win", "seq")), P(("win", "seq"), None)
    kinds = "vvmvmmvmvvvmvmmvmvvvmvmv"
    weights = tuple(matrix if kind == "m" else vector for kind in kinds)
    in_specs = (rows, rows, P(None, "win", None), P(None, "win", None), rows) + weights
    return jax.shard_map(per_device, mesh=mesh, in_specs=in_specs, out_specs=(rows, rows, rows) + weights, check_vma=False)
```

```python
import jax
import jax.numpy as jnp
from jax import lax
from jax.experimental import pallas as pl
from jax.experimental.pallas import tpu as pltpu
from jax.sharding import PartitionSpec as P

bf, f32 = jnp.bfloat16, jnp.float32
HEAD_DIM = 64
EPS = 1e-05
SCALE = 0.125
BLOCKED = -1e30
MESH = pl.DeviceIdType.MESH
D = 768
HALF = D // 2


def coords():
    win, seq = lax.axis_index("win"), lax.axis_index("seq")
    x, y = win // 8, lax.rem(win // 2, 4)
    z = (seq // 2) * 2 + lax.rem(win, 2)
    return x, y, z, lax.rem(seq, 2)


def device_at(x, y, z, core):
    return (x * 8 + y * 2 + lax.rem(z, 2), (z // 2) * 2 + core)


def member(z, core):
    return lax.rem(z, 2) * 4 + (z // 2) * 2 + core


KEYS, FRAMES, SPAN = 448, 1536, 224


def dot(a, b):
    return jnp.dot(a, b, preferred_element_type=f32)


def dot_back(a, b):
    return lax.dot_general(a, b, (((1,), (1,)), ((), ())), preferred_element_type=f32)


def dot_grad(a, b):
    return lax.dot_general(a, b, (((0,), (0,)), ((), ())), preferred_element_type=f32)


def normed(values):
    mean = jnp.mean(values, -1, keepdims=True)
    centered = values - mean
    spread = jnp.mean(centered * centered, -1, keepdims=True)
    r = lax.rsqrt(spread + EPS)
    return centered * r, r


def norm_back(e, n, r, gain):
    eg = e * gain
    return r * (eg - jnp.mean(eg, -1, keepdims=True) - n * jnp.mean(eg * n, -1, keepdims=True))


def row_sum(v):
    return jnp.sum(v, 0, keepdims=True)


def one_head(v, e):
    at = lax.broadcasted_iota(jnp.int32, v.shape, 1)
    return jnp.where((at < 64) if e == 0 else (at >= 64), v, jnp.zeros_like(v))


def two_heads(a, b):
    at = lax.broadcasted_iota(jnp.int32, a.shape, 1)
    return jnp.where(at < 64, a, b)


def attend(q, k, v, bias, mixed, lse, begin, end):
    @pl.loop(begin, end)
    def _(j):
        at = pl.ds(pl.multiple_of(j * 128, 128), 128)
        qp, kp, vp = q[:, at], k[:, at], v[:, at]
        outs, logs = [], []
        for e in (0, 1):
            s = dot_back(one_head(qp, e), kp) + bias[...]
            top = jnp.max(s, 1, keepdims=True)
            p = jnp.exp(s - top)
            total = jnp.sum(p, 1, keepdims=True)
            outs.append(dot(p.astype(bf), vp) / total)
            logs.append(top + jnp.log(total))
        mixed[:, at] = two_heads(*outs).astype(bf)
        lse[j] = two_heads(*[jnp.broadcast_to(log, (SPAN, 128)) for log in logs])


def attend_back(q, k, v, bias, mixed, lse, g, gq, gk, gv, begin, end):
    @pl.loop(begin, end)
    def _(j):
        at = pl.ds(pl.multiple_of(j * 128, 128), 128)
        qp, kp, vp, gp = q[:, at], k[:, at], v[:, at], g[:, at]
        product = gp.astype(f32) * mixed[:, at].astype(f32)
        dq, dk, dv = [], 0.0, 0.0
        for e in (0, 1):
            qe, ge = one_head(qp, e), one_head(gp, e)
            s = dot_back(qe, kp) + bias[...]
            p = jnp.exp(s - lse[j, :, 64 * e:64 * e + 1])
            dp = dot_back(ge, vp)
            delta = jnp.sum(one_head(product, e), 1, keepdims=True)
            ds = (p * (dp - delta)).astype(bf)
            dk = dk + dot_grad(ds, qe)
            dv = dv + dot_grad(p.astype(bf), ge)
            dq.append(dot(ds, kp) * SCALE)
        gk[:, at] = dk.astype(bf)
        gv[:, at] = dv.astype(bf)
        gq[:, at] = two_heads(*dq).astype(bf)


def blocks(total, step, body):
    @pl.loop(0, total // step)
    def _(i):
        body(pl.ds(pl.multiple_of(i * step, step), step))


class Chunk:
    def __init__(self, index, base, out, slot):
        self.index, self.base, self.out, self.slot = index, base, out, slot
        self.sent, self.back = [], []


def one_hot(source, width):
    cols = lax.broadcasted_iota(jnp.int32, (source.shape[0], width), 1)
    return jnp.where(cols == source, 1.0, 0.0).astype(bf)


def spread_matrix(core):
    r = lax.broadcasted_iota(jnp.int32, (96, 1), 0)
    piece, at = r // 48, lax.rem(r, 48)
    return one_hot((at // 6) * 32 + (2 * core + piece) * 6 + lax.rem(at, 6), 256)


def split_matrix():
    r = lax.broadcasted_iota(jnp.int32, (128, 1), 0)
    k, i = r // 16, lax.rem(r, 16)
    return one_hot(jnp.where(i < 12, (i // 6) * 48 + 6 * k + lax.rem(i, 6), -1), 96)


def vector_tables():
    f = lax.broadcasted_iota(jnp.int32, (D, 128), 0)
    c = lax.broadcasted_iota(jnp.int32, (D, 128), 1)
    owner = jnp.where((f >= 6 * c) & (f < 6 * c + 6), 1.0, 0.0).astype(bf)
    inner = jnp.where(lax.rem(f, 6) == lax.rem(c, 6), 1.0, 0.0)
    v = lax.broadcasted_iota(jnp.int32, (16, 128), 0)
    c = lax.broadcasted_iota(jnp.int32, (16, 128), 1)
    which = jnp.where((c >= 6 * v) & (c < 6 * v + 6) & (v < 13), 1.0, 0.0).astype(bf)
    return owner, inner, which


def hidden_tables(n):
    q = lax.broadcasted_iota(jnp.int32, (D, 128), 0)
    c = lax.broadcasted_iota(jnp.int32, (D, 128), 1)
    start = 24 * (c - 32 * n)
    owner = jnp.where((q >= start) & (q < start + 24), 1.0, 0.0).astype(bf)
    inner = jnp.where(c == 78 + lax.rem(q, 24), 1.0, 0.0)
    return owner, inner


def layer_kernel(m0, m1, m2, m3, m4, m5, m6, m7, h_in, h_out, small, tok_in, enc_in, og_in, seg2, clip2,
                 fin, fin2, gs, bo_out, pi_out, ep_out,
                 w, s6, sh1, sh2, zbuf, c2buf, sm, smbuf, tok, enc, og, vec, hib, first, q, k, v, mixed, lse, second, cq, ck, cv,
                 cmixed, clse, after_self, stream, third, acc, bias_s, bias_c, g, gq, wide, gvec, ghib,
                 BO, PI, pib, eib, db, r1, r2, r2b, red, shares, r3, sx, r4, c2sum, c2r, SG, sd, s1b, s2b, s3b,
                 ls, zs, zr, ds, dr, as1, ar1, as2, ar2, cs, cr, ss1, sr1, ss2, sr2, es, er, fs, fr,
                 bds, bdr, b1s, b1r, b2s, b2r, b3s, b3r, b4s, b4r, gss, gsr, ts, tr, os_, credit):
    x, y, z, core = coords()
    hi = z // 2
    other = 1 - core
    s = 1 - 2 * core
    partner = device_at(x, y, z, other)
    across = lax.rem(z + 2, 4)
    home = device_at(x, y, across, core)
    pos = (x, y, z)

    def turn(axis, off):
        return lax.rem(pos[axis] + off + 8, 4)

    def peer(axis, off):
        at = list(pos)
        at[axis] = turn(axis, off)
        return device_at(at[0], at[1], at[2], core)
    xp = [None] + [peer(0, o) for o in (1, 2, 3)]
    yp = [None] + [peer(1, o) for o in (1, 2, 3)]
    zp = [None] + [peer(2, o) for o in (1, 2, 3)]
    near = [partner] + xp[1:] + yp[1:]
    peers = near + [device_at(x, y, across, other)] + zp[1:]
    barrier = pltpu.get_barrier_semaphore()
    for to in peers:
        pl.semaphore_signal(barrier, inc=1, device_id=to, device_id_type=MESH)
    me = member(z, core)
    qm = me // 2
    lanes = pl.ds(pl.multiple_of(core * HALF, 128), HALF)
    lanes_other = pl.ds(pl.multiple_of(other * HALF, 128), HALF)
    halves = (pl.ds(0, HALF), pl.ds(HALF, HALF))
    A, B, C1, C2 = Chunk(0, 0, 8, 0), Chunk(1, 4, 12, 1), Chunk(2, 8, 8, 1), Chunk(3, 12, 12, 0)
    moved = []

    def remote(src, dst, send, recv, to):
        return pltpu.make_async_remote_copy(src_ref=src, dst_ref=dst, send_sem=send, recv_sem=recv,
                                            device_id=to, device_id_type=MESH)

    def start(sent, *a):
        c = remote(*a)
        c.start()
        sent.append(c)

    def arrived(at, sem):
        remote(at, at, fs.at[0], sem, partner).wait_recv()

    def local(src, dst, sem):
        c = pltpu.make_async_copy(src, dst, sem)
        c.start()
        return c

    def sends_done(sent):
        for c in sent:
            c.wait_send()
        sent.clear()

    def z_start(t):
        at = pl.ds(32 * t.index, 32)
        for o in (1, 3, 2):
            start(t.sent, zbuf.at[me, at], zbuf.at[me, at], zs.at[t.index, o], zr.at[t.index, o], zp[o])
        start(t.sent, zbuf.at[me, at], zbuf.at[me, at], ds.at[t.index, 0], dr.at[t.index, 0], partner)

    def z_mid(t):
        at = pl.ds(32 * t.index, 32)
        for o in (1, 3, 2):
            here = zbuf.at[member(turn(2, -o), core), at]
            arrived(here, zr.at[t.index, o])
            start(t.sent, here, here, ds.at[t.index, o], dr.at[t.index, o], partner)

    def spread(t):
        at = pl.ds(32 * t.index, 32)
        for o in range(4):
            arrived(zbuf.at[me, at], dr.at[t.index, o])
        packed = zbuf[:, at].reshape(256, D)
        w[pl.ds(t.base + core * 2, 2), x, y] = dot(spread_matrix(core), packed).astype(bf).reshape(2, 48, D)
        if t is A:
            r = lax.broadcasted_iota(jnp.int32, (16, 1), 0)
            smbuf[...] = dot(one_hot(lax.rem(r, 8) * 32 + 24, 256), packed[:, :128]).astype(bf)
            sm[x, y] = smbuf[...]

    def xy1(t):
        for o in (1, 3, 2):
            for c in (0, 1):
                here = w.at[t.base + core * 2 + c, x, y]
                start(t.sent, here, here, as1.at[t.index, c, o], ar1.at[t.index, c, o], (xp, yp)[c][o])
            if t is A:
                start(t.sent, smbuf, sm.at[x, y], ss1.at[o], sr1.at[o], xp[o])

    def line(t, c, off):
        if c == 0:
            return w.at[t.base + core * 2, :, turn(1, off)]
        return w.at[t.base + core * 2 + 1, turn(0, off)]

    def hand(t, c, p, off):
        start(t.sent, line(t, c, off), line(t, c, off), cs.at[t.index, c, p], cr.at[t.index, c, p], partner)

    def xy2(t):
        for c in (0, 1):
            here = w.at[t.base + core * 2 + c, x, y]
            for o in (1, 2, 3):
                arrived(here, ar1.at[t.index, c, o])
            here = line(t, c, 0)
            for p, off in ((1, s), (3, -s)):
                start(t.sent, here, here, as2.at[t.index, c, p], ar2.at[t.index, c, p], peer(1 - c, off))
            hand(t, c, 0, 0)
        if t is A:
            for o in (1, 2, 3):
                arrived(smbuf, sr1.at[o])
            for p in (1, 2, 3):
                start(t.sent, sm.at[:, y], sm.at[:, y], ss2.at[p], sr2.at[p], yp[p])

    def relay(t):
        for c in (0, 1):
            here = line(t, c, -s)
            arrived(here, ar2.at[t.index, c, 1])
            start(t.sent, here, here, as2.at[t.index, c, 2], ar2.at[t.index, c, 2], peer(1 - c, s))
            hand(t, c, 1, -s)

    def hand_over(t):
        for p, off in ((3, s), (2, 2)):
            for c in (0, 1):
                arrived(line(t, c, off), ar2.at[t.index, c, p])
                hand(t, c, p, off)
        if t is A:
            for p in (1, 2, 3):
                arrived(sm.at[:, y], sr2.at[p])

    def finish(t):
        for p in (0, 1, 3, 2):
            for c in (0, 1):
                arrived(line(t, c, 0), cr.at[t.index, c, p])

    def plane(off):
        there = turn(2, off)
        return w.at[12:16, :, lax.rem(there, 2) * 2 + there // 2, :, lanes]

    def c2_first():
        arrived(c2buf.at[0], dr.at[3, 0])
        both = c2buf[...].astype(f32)[:, :24].reshape(48, D).astype(bf)
        w[12 + x, y, qm, :, lanes] = jnp.where(core == 0, both[:, :HALF], both[:, HALF:])
        here = w.at[12 + x, y, qm, :, lanes]
        for o in (1, 3, 2):
            start(C2.sent, here, here, as1.at[3, 0, o], ar1.at[3, 0, o], xp[o])

    def c2_second():
        here = w.at[12 + x, y, qm, :, lanes]
        for o in (1, 2, 3):
            arrived(here, ar1.at[3, 0, o])
        here = w.at[12:16, y, qm, :, lanes]
        for o in (1, 3, 2):
            start(C2.sent, here, here, as1.at[3, 1, o], ar1.at[3, 1, o], yp[o])

    def c2_third():
        for o in (1, 2, 3):
            arrived(w.at[12:16, y, qm, :, lanes], ar1.at[3, 1, o])
        here = plane(0)
        for p, off in ((1, s), (3, -s)):
            start(C2.sent, here, here, as2.at[3, 0, p], ar2.at[3, 0, p], peer(2, off))
        start(C2.sent, here, here, cs.at[3, 0, 0], cr.at[3, 0, 0], partner)

    def c2_relay():
        here = plane(-s)
        arrived(here, ar2.at[3, 0, 1])
        start(C2.sent, here, here, as2.at[3, 0, 2], ar2.at[3, 0, 2], peer(2, s))
        start(C2.sent, here, here, cs.at[3, 0, 1], cr.at[3, 0, 1], partner)

    def c2_hand():
        for p, off in ((3, s), (2, 2)):
            here = plane(off)
            arrived(here, ar2.at[3, 0, p])
            start(C2.sent, here, here, cs.at[3, 0, p], cr.at[3, 0, p], partner)

    def c2_finish():
        for p in range(4):
            arrived(plane(0), cr.at[3, 0, p])

    block = hi * 2 + core
    pairs = ((tok_in, tok), (enc_in, enc))
    own = {}

    def input_start(i):
        src, dst = pairs[i]
        start(moved, src.at[1 - hi], dst.at[block], es.at[i], er.at[i], home)
        start(moved, src.at[hi], dst.at[block], es.at[2 + i], er.at[2 + i], partner)
        own[i] = local(src.at[hi], dst.at[block], ls.at[1 + i])

    def input_forward(i):
        far = pairs[i][1].at[(1 - hi) * 2 + core]
        arrived(far, er.at[i])
        start(moved, far, far, fs.at[i], fr.at[i], partner)

    def input_ready(i):
        here = pairs[i][1].at[0]
        own[i].wait()
        arrived(here, er.at[2 + i])
        arrived(here, fr.at[i])

    def grad_start():
        start(moved, og_in.at[1 - hi], og.at[core], es.at[4], er.at[4 + core], device_at(x, y, across, hi))

        @pl.when(core == hi)
        def _():
            c = pltpu.make_async_copy(og_in.at[hi], og.at[core], ls.at[3])
            c.start()
            c.wait()

        @pl.when(core != hi)
        def _():
            c = remote(og_in.at[hi], og.at[core], es.at[5], er.at[6], partner)
            c.start()
            c.wait_send()

    def grad_ready():
        @pl.when(hi == core)
        def _():
            arrived(og.at[0], er.at[6])

        @pl.when(hi != core)
        def _():
            for i in (0, 1):
                arrived(og.at[0], er.at[4 + i])

    def out_start(t):
        for i in range(4):
            src = w.at[12 + i, :, :, :, lanes_other] if t is C2 else w.at[t.out + 2 * other + i // 2, :, :, :, halves[i % 2]]
            start(t.sent, src, db.at[t.slot, i], bds.at[t.index, i], bdr.at[t.index, i], partner)

    def out_line(t, c, off):
        if t is C2:
            there = turn(2, off)
            return db.at[t.slot, :, :, lax.rem(there, 2) * 2 + there // 2]
        if c == 0:
            return db.at[t.slot, 0:2, :, turn(1, off)]
        return db.at[t.slot, 2:4, turn(0, off)]

    def out_axis(t, c):
        return 2 if t is C2 else 1 - c

    def out_colors(t):
        return (0,) if t is C2 else (0, 1)

    def out_slot(t, c, p):
        return r1.at[t.slot, p] if t is C2 else r1.at[t.slot, p, 2 * c:2 * c + 2]

    def add_into(to, *terms):
        n = to.shape[0]

        @pl.loop(0, n)
        def _(i):
            total = to[i].astype(f32)
            for term in terms:
                total = total + term[i].astype(f32)
            to[i] = total.astype(bf)

    def out_first(t):
        for i in range(4):
            arrived(db.at[t.slot, i], bdr.at[t.index, i])
            if t is C2:
                add_into(db.at[t.slot, i], w.at[12 + i, :, :, :, lanes])
            else:
                add_into(db.at[t.slot, i], w.at[t.out + 2 * core + i // 2, :, :, :, halves[i % 2]])
            if t is C2 and i < 3 or i % 2 == 0:
                continue
            c = 0 if t is C2 else i // 2
            for p, off, to in ((0, 2, s), (1, -s, -s)):
                start(t.back, out_line(t, c, off), out_slot(t, c, p), b1s.at[t.index, c, p], b1r.at[t.index, c, p],
                      peer(out_axis(t, c), to))

    def out_second(t):
        for c in out_colors(t):
            arrived(out_slot(t, c, 0), b1r.at[t.index, c, 0])
            here = out_line(t, c, s)
            add_into(here, out_slot(t, c, 0))
            start(t.back, here, out_slot(t, c, 2), b1s.at[t.index, c, 2], b1r.at[t.index, c, 2], peer(out_axis(t, c), s))

    def out_third(t):
        for c in out_colors(t):
            for p in (1, 2):
                arrived(out_slot(t, c, p), b1r.at[t.index, c, p])
            add_into(out_line(t, c, 0), out_slot(t, c, 1), out_slot(t, c, 2))
            for o in (1, 3, 2):
                if t is C2:
                    src, dst, to = db.at[t.slot, :, turn(1, o), qm], r2.at[t.slot, o - 1], yp[o]
                elif c == 0:
                    src, dst, to = db.at[t.slot, 0:2, turn(0, o), y], r2.at[t.slot, o - 1, 0:2], xp[o]
                else:
                    src, dst, to = db.at[t.slot, 2:4, x, turn(1, o)], r2.at[t.slot, o - 1, 2:4], yp[o]
                start(t.back, src, dst, b2s.at[t.index, c, o - 1], b2r.at[t.index, c, o - 1], to)

    def out_fourth(t):
        if t is C2:
            for o in (0, 1, 2):
                arrived(r2.at[t.slot, o], b2r.at[3, 0, o])
            add_into(db.at[t.slot, :, y, qm], *[r2.at[t.slot, o] for o in (0, 1, 2)])
            for o in (1, 3, 2):
                start(t.back, db.at[t.slot, turn(0, o), y, qm], r2b.at[o - 1], b2s.at[3, 1, o - 1], b2r.at[3, 1, o - 1], xp[o])
            return
        for c in (0, 1):
            for o in (0, 1, 2):
                arrived(r2.at[t.slot, o, 2 * c:2 * c + 2], b2r.at[t.index, c, o])
            for h in (0, 1):
                total = db[t.slot, 2 * c + h, x, y].astype(f32)
                for o in (0, 1, 2):
                    total = total + r2[t.slot, o, 2 * c + h].astype(f32)
                red[c, :, h * HALF:(h + 1) * HALF] = total.astype(bf)
        shares[t.index] = dot(split_matrix(), red[...].reshape(96, D)).astype(bf).reshape(8, 16, D)
        for o in (1, 3, 2):
            start(t.back, shares.at[t.index, pl.ds(member(turn(2, o), 0), 2)], r3.at[t.index, o - 1], b3s.at[t.index, o - 1],
                  b3r.at[t.index, o - 1], zp[o])

    def out_fifth(t):
        if t is C2:
            for o in (0, 1, 2):
                arrived(r2b.at[o], b2r.at[3, 1, o])
            total = db[t.slot, x, y, qm].astype(f32)
            for o in (0, 1, 2):
                total = total + r2b[o].astype(f32)
            c2sum[core] = total.astype(bf)
            start(t.back, c2sum.at[core], c2sum.at[core], b4s.at[3], b4r.at[3], partner)
            return
        for o in (0, 1, 2):
            arrived(r3.at[t.index, o], b3r.at[t.index, o])
        base = member(z, 0)

        def share(c):
            total = shares[t.index, base + c].astype(f32)
            for o in (0, 1, 2):
                total = total + r3[t.index, o, c].astype(f32)
            return total
        fin[t.index, core] = share(core)
        sx[t.index] = share(other).astype(bf)
        start(t.back, sx.at[t.index], r4.at[t.index], b4s.at[t.index], b4r.at[t.index], partner)

    def out_last(t):
        if t is C2:
            arrived(c2sum.at[other], b4r.at[3])
            rows = jnp.concatenate([c2sum[0], c2sum[1]], 1).astype(f32)
            fin2[...] = jnp.where(core == 0, rows[:24], rows[24:])
            return
        arrived(r4.at[t.index], b4r.at[t.index])
        fin[t.index, other] = r4[t.index].astype(f32)

    def give_credit(t):
        sends_done(t.back)
        for to in near:
            pl.semaphore_signal(credit.at[t.slot], inc=1, device_id=to, device_id_type=MESH)

    def take_credit(t):
        pl.semaphore_wait(credit.at[t.slot], len(near))

    def home_start(i, src, buf):
        for n in (0, 1):
            start(moved, src.at[2 * n + other], buf.at[n], ts.at[i, n], tr.at[i, n], partner)

    def home_sum(i, src, buf, out):
        for n in (0, 1):
            arrived(buf.at[n], tr.at[i, n])

            @pl.loop(0, buf.shape[1] // 16)
            def _(a):
                at = pl.ds(pl.multiple_of(a * 16, 16), 16)
                src[2 * n + core, at] = (src[2 * n + core, at].astype(f32) + buf[n, at].astype(f32)).astype(bf)
        start(moved, src.at[2 * (1 - hi) + core], out.at[hi], ts.at[2, i], tr.at[2, i], home)
        return local(src.at[2 * hi + core], out.at[hi], ls.at[4 + i])

    def result_start():
        @pl.when(core == hi)
        def _():
            c = pltpu.make_async_copy(BO.at[core], bo_out.at[hi], ls.at[3])
            c.start()
            d = remote(BO.at[other], bo_out.at[hi], os_.at[0], tr.at[3, 0], partner)
            d.start()
            c.wait()
            d.wait_send()

        @pl.when(core != hi)
        def _():
            copies = [remote(BO.at[n], bo_out.at[hi], os_.at[n], tr.at[3, 1], device_at(x, y, across, n)) for n in (0, 1)]
            for c in copies:
                c.start()
            for c in copies:
                c.wait_send()

    def weight(u):
        return w[u].reshape(D, D)

    def weight_grad(u, a, b):
        @pl.loop(0, 3)
        def _(i):
            at = pl.ds(pl.multiple_of(i * 256, 256), 256)
            w[u, :, :, :, at] = dot_grad(a[...].reshape(-1, D), b[:, at]).astype(bf).reshape(4, 4, 48, 256)

    mine = pl.ds(pl.multiple_of(core * SPAN, 32), SPAN)

    loads = [local(m, s6.at[i], ls.at[6 + i]) for i, m in enumerate((m0, m1, m2, m3, m4, m5, m6, m7))]
    loads += [local(h_in, sh1, ls.at[14]), local(h_out, sh2, ls.at[15])]
    acc[0, 0:96] = jnp.zeros((96, D), f32)
    acc[1, 0:32] = jnp.zeros((32, D), f32)
    for c in loads:
        c.wait()
    for i in range(4):
        acc[0, 6 * i:6 * i + 6] = s6[i].astype(f32)
        acc[0, 32 + 6 * i:38 + 6 * i] = s6[4 + i].astype(f32)
        acc[0, 64 + 6 * i:70 + 6 * i] = sh1[:, D * i:D * i + D].astype(f32)
    acc[0, 24:25, 0:128] = small[0:1].astype(f32)
    acc[1, 0:24] = sh2[...].astype(f32)
    zbuf[me] = acc[0, 0:96].astype(bf)
    c2buf[core] = acc[1, 0:32].astype(bf)
    krow = seg2[pl.ds(hi, 1)]
    crow = clip2[pl.ds(hi, 1)]
    ids = jnp.broadcast_to(krow, (8, KEYS)).astype(f32).T[:, 0:1].astype(jnp.int32)
    qcol = jnp.where(core == 0, ids[:SPAN], ids[SPAN:])
    key_at = lax.broadcasted_iota(jnp.int32, (SPAN, KEYS), 1)
    query_at = lax.broadcasted_iota(jnp.int32, (SPAN, KEYS), 0) + core * SPAN
    bias_s[...] = jnp.where((qcol == krow) & (key_at <= query_at), 0.0, BLOCKED)
    bias_c[...] = jnp.where(qcol == crow, 0.0, BLOCKED)
    pl.semaphore_wait(barrier, len(peers))
    z_start(A)
    z_start(B)
    z_start(C1)
    start(C2.sent, c2buf.at[core], c2buf.at[core], ds.at[3, 0], dr.at[3, 0], partner)
    input_start(0)
    z_mid(A)
    spread(A)
    xy1(A)
    c2_first()
    z_mid(B)
    spread(B)
    xy1(B)
    input_start(1)
    xy2(A)
    z_mid(C1)
    spread(C1)
    input_forward(0)
    relay(A)
    xy2(B)
    c2_second()
    xy1(C1)
    input_ready(0)
    hand_over(A)

    S = sm[...].astype(f32).reshape(16, 16, 128)[:, :8].reshape(128, 128).astype(bf)
    owner, inner, which = vector_tables()
    vec[...] = dot_back(which, (dot(owner, S) * inner).astype(bf))
    for n in range(4):
        owner, inner = hidden_tables(n)
        hib[n:n + 1] = dot_back(jnp.ones((8, 128), bf), (dot(owner, S) * inner).astype(bf))[0:1]

    @pl.loop(0, 4)
    def _(i):
        n, _ = normed(tok[i].astype(f32))
        first[pl.ds(pl.multiple_of(i * 112, 16), 112)] = (n * vec[0:1] + vec[1:2]).astype(bf)
    c2_third()
    grad_start()
    finish(A)

    def keys(at):
        k[at] = dot(first[at], weight(1)).astype(bf)
    blocks(KEYS, SPAN, keys)
    relay(B)
    xy2(C1)

    def values(at):
        v[at] = (dot(first[at], weight(2)) + vec[3:4]).astype(bf)
    blocks(KEYS, SPAN, values)
    q[...] = (dot(first[mine], weight(0)) + vec[2:3]).astype(bf) * SCALE
    hand_over(B)
    attend(q, k, v, bias_s, mixed, lse, 0, 3)
    input_forward(1)
    relay(C1)
    attend(q, k, v, bias_s, mixed, lse, 3, 6)
    after_self[...] = tok[pl.ds(2 * core, 2)].reshape(SPAN, D).astype(f32) + dot(mixed[...], weight(3)) + vec[4:5]
    n, r = normed(after_self[...])
    second[...] = (n * vec[5:6] + vec[6:7]).astype(bf)
    finish(B)
    c2_relay()
    cq[...] = (dot(second[...], weight(4)) + vec[7:8]).astype(bf) * SCALE
    hand_over(C1)
    input_ready(1)

    @pl.loop(0, 4)
    def _(i):
        ck[pl.ds(pl.multiple_of(i * 384, 128), 384)] = dot(enc[i], weight(5)).astype(bf)

    @pl.loop(0, 4)
    def _(i):
        cv[pl.ds(pl.multiple_of(i * 384, 128), 384)] = (dot(enc[i], weight(6)) + vec[8:9]).astype(bf)
    attend(cq, ck, cv, bias_c, cmixed, clse, 0, 3)
    c2_hand()
    attend(cq, ck, cv, bias_c, cmixed, clse, 3, 6)
    stream[...] = after_self[...] + dot(cmixed[...], weight(7)) + vec[9:10]
    n, r = normed(stream[...])
    third[...] = (n * vec[10:11] + vec[11:12]).astype(bf)
    acc[0] = stream[...] + vec[12:13]
    acc[1] = jnp.zeros((SPAN, D), f32)
    grad_ready()
    g[...] = og[...].reshape(SPAN, D)
    finish(C1)
    c2_finish()
    for t in (A, B, C1, C2):
        sends_done(t.sent)
    sends_done(moved)
    for i in range(4):
        pre = dot(third[...], weight(8 + i)) + hib[i:i + 1]
        cdf = 0.5 * (1.0 + lax.erf(pre * 0.7071067811865476))
        act = (pre * cdf).astype(bf)
        slope = cdf + pre * (0.3989422804014327 * jnp.exp(-0.5 * pre * pre))
        wide[0] = act
        acc[0] += dot(act, weight(12 + i))
        g_pre = (dot_back(g[...], weight(12 + i)) * slope).astype(bf)
        wide[1] = g_pre
        weight_grad(12 + i, wide.at[0], g)
        ghib[i:i + 1] = row_sum(g_pre.astype(f32))
        acc[1] += dot_back(g_pre, weight(8 + i))
        weight_grad(8 + i, third, wide.at[1])
    out_start(C2)
    out_start(C1)
    BO[...] = acc[0].astype(bf).reshape(2, 112, D)
    e = acc[1]
    ogf = g[...].astype(f32)
    n, r = normed(stream[...])
    gvec[13:16] = jnp.zeros((3, D), f32)
    gvec[12:13] = row_sum(ogf)
    gvec[10:11] = row_sum(e * n)
    gvec[11:12] = row_sum(e)
    stream[...] = ogf + norm_back(e, n, r, vec[10:11])
    wide[0] = stream[...].astype(bf)
    gvec[9:10] = row_sum(wide[0].astype(f32))
    out_first(C2)
    g[...] = dot_back(wide[0], weight(7)).astype(bf)
    out_first(C1)
    result_start()
    sends_done(C2.sent)
    sends_done(C1.sent)
    weight_grad(15, cmixed, wide.at[0])
    attend_back(cq, ck, cv, bias_c, cmixed, clse, g, gq, ck, cv, 0, 2)
    out_second(C1)
    attend_back(cq, ck, cv, bias_c, cmixed, clse, g, gq, ck, cv, 2, 4)
    out_third(C1)
    out_second(C2)
    attend_back(cq, ck, cv, bias_c, cmixed, clse, g, gq, ck, cv, 4, 6)
    out_fourth(C1)
    weight_grad(13, enc, ck)
    out_third(C2)
    weight_grad(14, enc, cv)
    out_fifth(C1)
    weight_grad(12, second, gq)
    give_credit(C1)
    take_credit(B)
    out_start(B)

    @pl.loop(0, 4)
    def _(i):
        at = pl.ds(pl.multiple_of(i * 384, 128), 384)
        enc[i] = (dot_back(ck[at], weight(5)) + dot_back(cv[at], weight(6))).astype(bf)
    home_start(1, enc, eib)
    out_first(B)
    out_fourth(C2)
    e = dot_back(gq[...], weight(4))
    gvec[7:8] = row_sum(gq[...].astype(f32))
    gvec[8:9] = row_sum(cv[...].astype(f32))
    n, r = normed(after_self[...])
    gvec[5:6] = row_sum(e * n)
    gvec[6:7] = row_sum(e)
    stream[...] += norm_back(e, n, r, vec[5:6])
    wide[0] = stream[...].astype(bf)
    gvec[4:5] = row_sum(wide[0].astype(f32))
    g[...] = dot_back(wide[0], weight(3)).astype(bf)
    ends = [home_sum(1, enc, eib, ep_out)]
    weight_grad(11, mixed, wide.at[0])
    out_fifth(C2)
    out_second(B)
    attend_back(q, k, v, bias_s, mixed, lse, g, gq, k, v, 0, 6)
    give_credit(C2)
    out_third(B)
    wide[0] = first[mine]
    weight_grad(8, wide.at[0], gq)
    weight_grad(9, first, k)
    weight_grad(10, first, v)
    take_credit(A)
    out_start(A)
    gvec[2:3] = row_sum(gq[...].astype(f32))
    gvec[3:4] = row_sum(v[...].astype(f32))
    gvec[0:2] = jnp.zeros((2, D), f32)
    acc[0] = dot_back(gq[...], weight(0))
    for h in (0, 1):
        at = pl.ds(h * SPAN, SPAN)
        is_own = core == h
        e = dot_back(k[at], weight(1)) + dot_back(v[at], weight(2)) + jnp.where(is_own, acc[0], 0.0)
        n, r = normed(tok[2 * h:2 * h + 2].reshape(SPAN, D).astype(f32))
        gvec[0:1] += row_sum(e * n)
        gvec[1:2] += row_sum(e)
        PI[2 * h:2 * h + 2] = (norm_back(e, n, r, vec[0:1]) + jnp.where(is_own, stream[...], 0.0)).astype(bf).reshape(2, 112, D)
        if h == 0:
            out_first(A)
    home_start(0, PI, pib)
    out_fourth(B)
    owner, inner, which = vector_tables()
    spread_out = lax.dot_general(gvec[...].astype(bf), which, (((0,), (0,)), ((), ())), preferred_element_type=f32)
    total = dot_grad(owner, (spread_out * inner).astype(bf))
    for n in range(4):
        owner, inner = hidden_tables(n)
        column = jnp.broadcast_to(ghib[n:n + 1], (8, D)).T[:, 0:1]
        total = total + dot_grad(owner, (column * inner).astype(bf))
    SG[...] = total.reshape(4, 4, 8, 128)
    swap = remote(SG, sd, gss.at[0], gsr.at[0], partner)
    swap.start()
    out_second(A)
    swap.wait()
    SG[...] = SG[...] + sd[...]
    for p in (1, 2, 3):
        start(moved, SG.at[:, turn(1, p)], s1b.at[p], gss.at[p], gsr.at[p], yp[p])
    ends.append(home_sum(0, PI, pib, pi_out))
    out_fifth(B)
    out_third(A)
    total = SG[:, y]
    for p in (1, 2, 3):
        arrived(s1b.at[p], gsr.at[p])
        total = total + s1b[p]
    SG[:, y] = total
    for b in (1, 2, 3):
        start(moved, SG.at[turn(0, b), y], s2b.at[b], gss.at[3 + b], gsr.at[3 + b], xp[b])
    out_last(C2)
    out_last(C1)
    out_last(B)
    out_fourth(A)
    total = SG[x, y]
    for b in (1, 2, 3):
        arrived(s2b.at[b], gsr.at[3 + b])
        total = total + s2b[b]
    s3b[0] = total
    for o in (1, 2, 3):
        start(moved, s3b.at[0], s3b.at[o], gss.at[6 + o], gsr.at[6 + o], zp[o])
    out_fifth(A)
    total = s3b[0]
    for o in (1, 2, 3):
        arrived(s3b.at[o], gsr.at[6 + o])
        total = total + s3b[o]
    own_row = lax.broadcasted_iota(jnp.int32, (8, 128), 0) == me
    gs[...] = jnp.broadcast_to(jnp.sum(jnp.where(own_row, total, 0.0), 0, keepdims=True), (8, 128))
    arrived(ep_out.at[0], tr.at[2, 1])
    arrived(pi_out.at[0], tr.at[2, 0])

    @pl.when(core != hi)
    def _():
        arrived(bo_out.at[0], tr.at[3, 0])
    arrived(bo_out.at[0], tr.at[3, 1])
    out_last(A)
    for c in ends:
        c.wait()
    for t in (A, B, C1, C2):
        sends_done(t.sent)
        sends_done(t.back)
    sends_done(moved)


def layer(*operands):
    V, DMA, S = pltpu.VMEM, pltpu.SemaphoreType.DMA, jax.ShapeDtypeStruct
    vm, hbm = pl.BlockSpec(memory_space=pltpu.VMEM), pl.BlockSpec(memory_space=pl.ANY)
    return pl.pallas_call(
        layer_kernel,
        out_shape=[S((3, 2, 16, D), f32), S((24, D), f32), S((8, 128), f32), S((2, 112, D), bf), S((2, 112, D), bf), S((2, 384, D), bf)],
        in_specs=[hbm] * 10 + [vm] + [hbm] * 3 + [vm] * 2, out_specs=[vm] * 3 + [hbm] * 3,
        scratch_shapes=[
            V((16, 4, 4, 48, D), bf), V((8, 6, D), bf), V((6, 4 * D), bf), V((24, D), bf), V((8, 96, D), bf), V((2, 32, D), bf),
            V((4, 4, 16, 128), bf), V((16, 128), bf), V((4, 112, D), bf), V((4, 384, D), bf), V((2, 112, D), bf),
            V((16, D), f32), V((8, D), f32), V((KEYS, D), bf), V((SPAN, D), bf), V((KEYS, D), bf), V((KEYS, D), bf),
            V((SPAN, D), bf), V((6, SPAN, 128), f32), V((SPAN, D), bf), V((SPAN, D), bf), V((FRAMES, D), bf), V((FRAMES, D), bf),
            V((SPAN, D), bf), V((6, SPAN, 128), f32), V((SPAN, D), f32), V((SPAN, D), f32), V((SPAN, D), bf),
            V((2, SPAN, D), f32), V((SPAN, KEYS), f32), V((SPAN, FRAMES), f32), V((SPAN, D), bf), V((SPAN, D), bf),
            V((2, SPAN, D), bf), V((16, D), f32), V((8, D), f32),
            V((2, 112, D), bf), V((4, 112, D), bf), V((2, 112, D), bf), V((2, 384, D), bf),
            V((2, 4, 4, 4, 48, HALF), bf), V((2, 3, 4, 4, 48, HALF), bf), V((2, 3, 4, 48, HALF), bf), V((3, 48, HALF), bf),
            V((2, 48, D), bf), V((3, 8, 16, D), bf), V((3, 3, 2, 16, D), bf), V((3, 16, D), bf), V((3, 16, D), bf),
            V((2, 48, HALF), bf), V((16, 128), f32),
            V((4, 4, 8, 128), f32), V((4, 4, 8, 128), f32), V((4, 4, 8, 128), f32), V((4, 8, 128), f32), V((4, 8, 128), f32),
            DMA((16,)), DMA((4, 4)), DMA((4, 4)), DMA((4, 4)), DMA((4, 4)), DMA((4, 2, 4)), DMA((4, 2, 4)), DMA((4, 2, 4)), DMA((4, 2, 4)),
            DMA((4, 2, 4)), DMA((4, 2, 4)), DMA((4,)), DMA((4,)), DMA((4,)), DMA((4,)), DMA((6,)), DMA((7,)), DMA((2,)), DMA((2,)),
            DMA((4, 4)), DMA((4, 4)), DMA((4, 2, 3)), DMA((4, 2, 3)), DMA((4, 2, 3)), DMA((4, 2, 3)), DMA((3, 3)), DMA((3, 3)),
            DMA((4,)), DMA((4,)), DMA((10,)), DMA((10,)), DMA((3, 2)), DMA((4, 2)), DMA((2,)), pltpu.SemaphoreType.REGULAR((2,))],
        compiler_params=pltpu.CompilerParams(collective_id=0, has_side_effects=True, vmem_limit_bytes=63 << 20),
        name="layer",
    )(*operands)


def unpack_kernel(fin, fin2, bo, pi, ep, *outs):
    out, gi, ge, mats, h_in, h_out = outs[0], outs[1], outs[2], outs[3:11], outs[11], outs[12]
    out[...] = bo[...][:, None]
    gi[...] = pi[...].astype(f32)[:, None]
    ge[...] = ep[:, :375].astype(f32)[:, None]
    for i in range(4):
        mats[i][...] = fin[0, i // 2, 6 * (i % 2):6 * (i % 2) + 6]
        mats[4 + i][...] = fin[1, i // 2, 6 * (i % 2):6 * (i % 2) + 6]
        h_in[:, D * i:D * i + D] = fin[2, i // 2, 6 * (i % 2):6 * (i % 2) + 6]
    h_out[...] = fin2[...]


def unpack(fin, fin2, bo, pi, ep):
    S = jax.ShapeDtypeStruct
    return pl.pallas_call(
        unpack_kernel,
        out_shape=[S((2, 1, 112, D), bf), S((2, 1, 112, D), f32), S((2, 1, 375, D), f32)] + [S((6, D), f32)] * 8 + [S((6, 4 * D), f32), S((24, D), f32)],
        compiler_params=pltpu.CompilerParams(vmem_limit_bytes=32 << 20),
        name="unpack",
    )(fin, fin2, bo, pi, ep)


def per_device(
    tokens, encoder_states, segments, frame_clips, out_grad,
    self_gain, self_shift, self_query, self_query_bias, self_key, self_value, self_value_bias, self_output,
    self_output_bias, cross_gain, cross_shift, cross_query, cross_query_bias, cross_key, cross_value,
    cross_value_bias, cross_output, cross_output_bias, final_gain, final_shift, hidden_in, hidden_in_bias,
    hidden_out, hidden_out_bias,
):
    vectors = (self_gain, self_shift, self_query_bias, self_value_bias, self_output_bias, cross_gain, cross_shift,
               cross_query_bias, cross_value_bias, cross_output_bias, final_gain, final_shift, hidden_out_bias)
    small = jnp.pad(hidden_in_bias.astype(f32), (78, 26))
    for i, vector in enumerate(vectors):
        small = small + jnp.pad(vector.astype(f32), (6 * i, 122 - 6 * i))
    small = jnp.broadcast_to(small[None], (8, 128))
    frames = jnp.pad(encoder_states, ((0, 0), (0, 0), (0, 9), (0, 0))).reshape(2, 384, D)
    clip = jnp.pad(frame_clips.reshape(2, 4, 375), ((0, 0), (0, 0), (0, 9)), constant_values=-1).reshape(2, FRAMES)
    fin, fin2, gs, bo, pi, ep = layer(
        self_query, self_key, self_value, self_output, cross_query, cross_key, cross_value, cross_output, hidden_in, hidden_out,
        small, tokens[:, 0], frames, out_grad[:, 0], segments[:, 0], clip)
    out, gi, ge, *m = unpack(fin, fin2, bo, pi, ep)
    gv = [gs[0, 6 * i:6 * i + 6] for i in range(13)]
    return (out, gi, ge,
            gv[0], gv[1], m[0], gv[2], m[1], m[2], gv[3], m[3], gv[4],
            gv[5], gv[6], m[4], gv[7], m[5], m[6], gv[8], m[7], gv[9],
            gv[10], gv[11], m[8], gs[0, 78:102], m[9], gv[12])


def solution(mesh):
    rows = P(None, "win", "seq", None)
    vector, matrix = P(("win", "seq")), P(("win", "seq"), None)
    kinds = "vvmvmmvmvvvmvmmvmvvvmvmv"
    weights = tuple(matrix if kind == "m" else vector for kind in kinds)
    in_specs = (rows, rows, P(None, "win", None), P(None, "win", None), rows) + weights
    return jax.shard_map(per_device, mesh=mesh, in_specs=in_specs, out_specs=(rows, rows, rows) + weights, check_vma=False)
```

```python
import jax
import jax.numpy as jnp
from jax import lax
from jax.experimental import pallas as pl
from jax.experimental.pallas import tpu as pltpu
from jax.sharding import PartitionSpec as P

bf, f32 = jnp.bfloat16, jnp.float32
HEAD_DIM = 64
EPS = 1e-05
SCALE = 0.125
BLOCKED = -1e30
MESH = pl.DeviceIdType.MESH
D = 768
HALF = D // 2


def coords():
    win, seq = lax.axis_index("win"), lax.axis_index("seq")
    x, y = win // 8, lax.rem(win // 2, 4)
    z = (seq // 2) * 2 + lax.rem(win, 2)
    return x, y, z, lax.rem(seq, 2)


def device_at(x, y, z, core):
    return (x * 8 + y * 2 + lax.rem(z, 2), (z // 2) * 2 + core)


def member(z, core):
    return lax.rem(z, 2) * 4 + (z // 2) * 2 + core


KEYS, FRAMES, SPAN = 448, 1536, 224


def dot(a, b):
    return jnp.dot(a, b, preferred_element_type=f32)


def dot_back(a, b):
    return lax.dot_general(a, b, (((1,), (1,)), ((), ())), preferred_element_type=f32)


def dot_grad(a, b):
    return lax.dot_general(a, b, (((0,), (0,)), ((), ())), preferred_element_type=f32)


def normed(values):
    mean = jnp.mean(values, -1, keepdims=True)
    centered = values - mean
    spread = jnp.mean(centered * centered, -1, keepdims=True)
    r = lax.rsqrt(spread + EPS)
    return centered * r, r


def norm_back(e, n, r, gain):
    eg = e * gain
    return r * (eg - jnp.mean(eg, -1, keepdims=True) - n * jnp.mean(eg * n, -1, keepdims=True))


def row_sum(v):
    return jnp.sum(v, 0, keepdims=True)


def one_head(v, e):
    at = lax.broadcasted_iota(jnp.int32, v.shape, 1)
    return jnp.where((at < 64) if e == 0 else (at >= 64), v, jnp.zeros_like(v))


def two_heads(a, b):
    at = lax.broadcasted_iota(jnp.int32, a.shape, 1)
    return jnp.where(at < 64, a, b)


def attend(q, k, v, bias, mixed, lse, begin, end):
    @pl.loop(begin, end)
    def _(j):
        at = pl.ds(pl.multiple_of(j * 128, 128), 128)
        qp, kp, vp = q[:, at], k[:, at], v[:, at]
        outs, logs = [], []
        for e in (0, 1):
            s = dot_back(one_head(qp, e), kp) + bias[...]
            top = jnp.max(s, 1, keepdims=True)
            p = jnp.exp(s - top)
            total = jnp.sum(p, 1, keepdims=True)
            outs.append(dot(p.astype(bf), vp) / total)
            logs.append(top + jnp.log(total))
        mixed[:, at] = two_heads(*outs).astype(bf)
        lse[j] = two_heads(*[jnp.broadcast_to(log, (SPAN, 128)) for log in logs])


def attend_back(q, k, v, bias, mixed, lse, g, gq, gk, gv, begin, end):
    @pl.loop(begin, end)
    def _(j):
        at = pl.ds(pl.multiple_of(j * 128, 128), 128)
        qp, kp, vp, gp = q[:, at], k[:, at], v[:, at], g[:, at]
        product = gp.astype(f32) * mixed[:, at].astype(f32)
        dq, dk, dv = [], 0.0, 0.0
        for e in (0, 1):
            qe, ge = one_head(qp, e), one_head(gp, e)
            s = dot_back(qe, kp) + bias[...]
            p = jnp.exp(s - lse[j, :, 64 * e:64 * e + 1])
            dp = dot_back(ge, vp)
            delta = jnp.sum(one_head(product, e), 1, keepdims=True)
            ds = (p * (dp - delta)).astype(bf)
            dk = dk + dot_grad(ds, qe)
            dv = dv + dot_grad(p.astype(bf), ge)
            dq.append(dot(ds, kp) * SCALE)
        gk[:, at] = dk.astype(bf)
        gv[:, at] = dv.astype(bf)
        gq[:, at] = two_heads(*dq).astype(bf)


def blocks(total, step, body):
    @pl.loop(0, total // step)
    def _(i):
        body(pl.ds(pl.multiple_of(i * step, step), step))


class Chunk:
    def __init__(self, index, base, out, slot):
        self.index, self.base, self.out, self.slot = index, base, out, slot
        self.sent, self.back, self.late = [], [], []


def one_hot(source, width):
    cols = lax.broadcasted_iota(jnp.int32, (source.shape[0], width), 1)
    return jnp.where(cols == source, 1.0, 0.0).astype(bf)


def spread_matrix(core):
    r = lax.broadcasted_iota(jnp.int32, (96, 1), 0)
    piece, at = r // 48, lax.rem(r, 48)
    return one_hot((at // 6) * 32 + (2 * core + piece) * 6 + lax.rem(at, 6), 256)


def split_matrix():
    r = lax.broadcasted_iota(jnp.int32, (128, 1), 0)
    k, i = r // 16, lax.rem(r, 16)
    return one_hot(jnp.where(i < 12, (i // 6) * 48 + 6 * k + lax.rem(i, 6), -1), 96)


def vector_tables():
    f = lax.broadcasted_iota(jnp.int32, (D, 128), 0)
    c = lax.broadcasted_iota(jnp.int32, (D, 128), 1)
    owner = jnp.where((f >= 6 * c) & (f < 6 * c + 6), 1.0, 0.0).astype(bf)
    inner = jnp.where(lax.rem(f, 6) == lax.rem(c, 6), 1.0, 0.0)
    v = lax.broadcasted_iota(jnp.int32, (16, 128), 0)
    c = lax.broadcasted_iota(jnp.int32, (16, 128), 1)
    which = jnp.where((c >= 6 * v) & (c < 6 * v + 6) & (v < 13), 1.0, 0.0).astype(bf)
    return owner, inner, which


def hidden_tables(n):
    q = lax.broadcasted_iota(jnp.int32, (D, 128), 0)
    c = lax.broadcasted_iota(jnp.int32, (D, 128), 1)
    start = 24 * (c - 32 * n)
    owner = jnp.where((q >= start) & (q < start + 24), 1.0, 0.0).astype(bf)
    inner = jnp.where(c == 78 + lax.rem(q, 24), 1.0, 0.0)
    return owner, inner


def layer_kernel(m0, m1, m2, m3, m4, m5, m6, m7, h_in, h_out, small, tok_in, enc_in, og_in, seg2, clip2,
                 fin, fin2, gs, bo_out, pi_out, ep_out,
                 w, s6, sh1, sh2, zbuf, c2buf, sm, smbuf, tok, enc, og, vec, hib, first, q, k, v, mixed, lse, second, cq, ck, cv,
                 cmixed, clse, after_self, stream, third, acc, bias_s, bias_c, g, gq, wide, gvec, ghib,
                 BO, PI, pib, eib, db, r1, r2, r2a, r2b, ptot, red, shares, r3, sx, r4, c2sum, c2r, SG, sd, s1b, s2b, s3b,
                 ls, zs, zr, ds, dr, as1, ar1, as2, ar2, cs, cr, ss1, sr1, ss2, sr2, es, er, fs, fr,
                 bds, bdr, b1s, b1r, b2s, b2r, b3s, b3r, b4s, b4r, gss, gsr, ts, tr, os_, credit):
    x, y, z, core = coords()
    hi = z // 2
    other = 1 - core
    s = 1 - 2 * core
    partner = device_at(x, y, z, other)
    across = lax.rem(z + 2, 4)
    home = device_at(x, y, across, core)
    pos = (x, y, z)

    def turn(axis, off):
        return lax.rem(pos[axis] + off + 8, 4)

    def peer(axis, off):
        at = list(pos)
        at[axis] = turn(axis, off)
        return device_at(at[0], at[1], at[2], core)
    xp = [None] + [peer(0, o) for o in (1, 2, 3)]
    yp = [None] + [peer(1, o) for o in (1, 2, 3)]
    zp = [None] + [peer(2, o) for o in (1, 2, 3)]
    near = [partner] + xp[1:] + yp[1:]
    peers = near + [device_at(x, y, across, other)] + zp[1:]
    barrier = pltpu.get_barrier_semaphore()
    for to in peers:
        pl.semaphore_signal(barrier, inc=1, device_id=to, device_id_type=MESH)
    me = member(z, core)
    qm = me // 2
    lanes = pl.ds(pl.multiple_of(core * HALF, 128), HALF)
    lanes_other = pl.ds(pl.multiple_of(other * HALF, 128), HALF)
    halves = (pl.ds(0, HALF), pl.ds(HALF, HALF))
    A, B, C1, C2 = Chunk(0, 0, 8, 0), Chunk(1, 4, 12, 1), Chunk(2, 8, 8, 1), Chunk(3, 12, 12, 0)
    moved = []

    def remote(src, dst, send, recv, to):
        return pltpu.make_async_remote_copy(src_ref=src, dst_ref=dst, send_sem=send, recv_sem=recv,
                                            device_id=to, device_id_type=MESH)

    def start(sent, *a):
        c = remote(*a)
        c.start()
        sent.append(c)

    def arrived(at, sem):
        remote(at, at, fs.at[0], sem, partner).wait_recv()

    def local(src, dst, sem):
        c = pltpu.make_async_copy(src, dst, sem)
        c.start()
        return c

    def sends_done(sent):
        for c in sent:
            c.wait_send()
        sent.clear()

    def z_start(t):
        at = pl.ds(32 * t.index, 32)
        for o in (1, 3, 2):
            start(t.sent, zbuf.at[me, at], zbuf.at[me, at], zs.at[t.index, o], zr.at[t.index, o], zp[o])
        start(t.sent, zbuf.at[me, at], zbuf.at[me, at], ds.at[t.index, 0], dr.at[t.index, 0], partner)

    def z_mid(t):
        at = pl.ds(32 * t.index, 32)
        for o in (1, 3, 2):
            here = zbuf.at[member(turn(2, -o), core), at]
            arrived(here, zr.at[t.index, o])
            start(t.sent, here, here, ds.at[t.index, o], dr.at[t.index, o], partner)

    def spread(t):
        at = pl.ds(32 * t.index, 32)
        for o in range(4):
            arrived(zbuf.at[me, at], dr.at[t.index, o])
        packed = zbuf[:, at].reshape(256, D)
        w[pl.ds(t.base + core * 2, 2), x, y] = dot(spread_matrix(core), packed).astype(bf).reshape(2, 48, D)
        if t is A:
            r = lax.broadcasted_iota(jnp.int32, (16, 1), 0)
            smbuf[...] = dot(one_hot(lax.rem(r, 8) * 32 + 24, 256), packed[:, :128]).astype(bf)
            sm[x, y] = smbuf[...]

    def xy1(t):
        for o in (1, 3, 2):
            for c in (0, 1):
                here = w.at[t.base + core * 2 + c, x, y]
                start(t.sent, here, here, as1.at[t.index, c, o], ar1.at[t.index, c, o], (xp, yp)[c][o])
            if t is A:
                start(t.sent, smbuf, sm.at[x, y], ss1.at[o], sr1.at[o], xp[o])

    both = (0, 1)

    def line(t, c, off, h):
        at = pl.ds(2 * h, 2)
        if c == 0:
            return w.at[t.base + core * 2, at, turn(1, off)]
        return w.at[t.base + core * 2 + 1, turn(0, off), at]

    def hand(t, c, p, off, h):
        here = line(t, c, off, h)
        start(t.sent, here, here, cs.at[t.index, c, 2 * p + h], cr.at[t.index, c, 2 * p + h], partner)

    def xy2(t):
        for c in (0, 1):
            here = w.at[t.base + core * 2 + c, x, y]
            for o in (1, 2, 3):
                arrived(here, ar1.at[t.index, c, o])
        for p, off in ((1, s), (3, -s)):
            for h in both:
                for c in (0, 1):
                    here = line(t, c, 0, h)
                    start(t.sent, here, here, as2.at[t.index, c, 2 * p + h], ar2.at[t.index, c, 2 * p + h], peer(1 - c, off))
        for h in both:
            for c in (0, 1):
                hand(t, c, 0, 0, h)
        if t is A:
            for o in (1, 2, 3):
                arrived(smbuf, sr1.at[o])
            for p in (1, 2, 3):
                start(t.sent, sm.at[:, y], sm.at[:, y], ss2.at[p], sr2.at[p], yp[p])

    def relay(t):
        for h in both:
            for c in (0, 1):
                here = line(t, c, -s, h)
                arrived(here, ar2.at[t.index, c, 2 + h])
                start(t.sent, here, here, as2.at[t.index, c, 4 + h], ar2.at[t.index, c, 4 + h], peer(1 - c, s))
                hand(t, c, 1, -s, h)

    def hand_over(t):
        for p, off in ((3, s), (2, 2)):
            for h in both:
                for c in (0, 1):
                    arrived(line(t, c, off, h), ar2.at[t.index, c, 2 * p + h])
                    hand(t, c, p, off, h)
        if t is A:
            for p in (1, 2, 3):
                arrived(sm.at[:, y], sr2.at[p])

    def finish(t):
        for p in (0, 1, 3, 2):
            for h in both:
                for c in (0, 1):
                    arrived(line(t, c, 0, h), cr.at[t.index, c, 2 * p + h])

    def plane(off, h):
        there = turn(2, off)
        return w.at[pl.ds(12 + 2 * h, 2), :, lax.rem(there, 2) * 2 + there // 2, :, lanes]

    def plane_hand(p, off, h):
        start(C2.sent, plane(off, h), plane(off, h), cs.at[3, 0, 2 * p + h], cr.at[3, 0, 2 * p + h], partner)

    def c2_first():
        arrived(c2buf.at[0], dr.at[3, 0])
        both = c2buf[...].astype(f32)[:, :24].reshape(48, D).astype(bf)
        w[12 + x, y, qm, :, lanes] = jnp.where(core == 0, both[:, :HALF], both[:, HALF:])
        here = w.at[12 + x, y, qm, :, lanes]
        for o in (1, 3, 2):
            start(C2.sent, here, here, as1.at[3, 0, o], ar1.at[3, 0, o], xp[o])

    def c2_second():
        here = w.at[12 + x, y, qm, :, lanes]
        for o in (1, 2, 3):
            arrived(here, ar1.at[3, 0, o])
        here = w.at[12:16, y, qm, :, lanes]
        for o in (1, 3, 2):
            start(C2.sent, here, here, as1.at[3, 1, o], ar1.at[3, 1, o], yp[o])

    def c2_third():
        for o in (1, 2, 3):
            arrived(w.at[12:16, y, qm, :, lanes], ar1.at[3, 1, o])
        for p, off in ((1, s), (3, -s)):
            for h in both:
                start(C2.sent, plane(0, h), plane(0, h), as2.at[3, 0, 2 * p + h], ar2.at[3, 0, 2 * p + h], peer(2, off))
        for h in both:
            plane_hand(0, 0, h)

    def c2_relay():
        for h in both:
            here = plane(-s, h)
            arrived(here, ar2.at[3, 0, 2 + h])
            start(C2.sent, here, here, as2.at[3, 0, 4 + h], ar2.at[3, 0, 4 + h], peer(2, s))
            plane_hand(1, -s, h)

    def c2_hand():
        for p, off in ((3, s), (2, 2)):
            for h in both:
                arrived(plane(off, h), ar2.at[3, 0, 2 * p + h])
                plane_hand(p, off, h)

    def c2_finish():
        for p in range(4):
            for h in both:
                arrived(plane(0, h), cr.at[3, 0, 2 * p + h])

    block = hi * 2 + core
    pairs = ((tok_in, tok), (enc_in, enc))
    own = {}

    def input_start(i):
        src, dst = pairs[i]
        start(moved, src.at[1 - hi], dst.at[block], es.at[i], er.at[i], home)
        start(moved, src.at[hi], dst.at[block], es.at[2 + i], er.at[2 + i], partner)
        own[i] = local(src.at[hi], dst.at[block], ls.at[1 + i])

    def input_forward(i):
        far = pairs[i][1].at[(1 - hi) * 2 + core]
        arrived(far, er.at[i])
        start(moved, far, far, fs.at[i], fr.at[i], partner)

    def input_ready(i):
        here = pairs[i][1].at[0]
        own[i].wait()
        arrived(here, er.at[2 + i])
        arrived(here, fr.at[i])

    def grad_start():
        start(moved, og_in.at[1 - hi], og.at[core], es.at[4], er.at[4 + core], device_at(x, y, across, hi))

        @pl.when(core == hi)
        def _():
            c = pltpu.make_async_copy(og_in.at[hi], og.at[core], ls.at[3])
            c.start()
            c.wait()

        @pl.when(core != hi)
        def _():
            c = remote(og_in.at[hi], og.at[core], es.at[5], er.at[6], partner)
            c.start()
            c.wait_send()

    def grad_ready():
        @pl.when(hi == core)
        def _():
            arrived(og.at[0], er.at[6])

        @pl.when(hi != core)
        def _():
            for i in (0, 1):
                arrived(og.at[0], er.at[4 + i])

    def out_piece(t, i):
        if t is C2:
            src = w.at[12 + i, :, :, :, lanes_other]
        else:
            src = w.at[t.out + 2 * other + i // 2, :, :, :, halves[i % 2]]
        return remote(src, db.at[t.slot, i], bds.at[t.index, i], bdr.at[t.index, i], partner)

    def out_start(t):
        for i in range(4):
            c = out_piece(t, i)
            c.start()
            t.sent.append(c)

    def out_early(i):
        c = out_piece(C2, i)
        c.start()
        C2.sent.append(c)
        pieces = [out_piece(C1, 2 * (i % 2) + h) for h in both]

        @pl.when(other == i // 2)
        def _():
            for c in pieces:
                c.start()
        if i < 2:
            C1.sent.extend(pieces)

    def out_line(t, c, off, at):
        if t is C2:
            there = turn(2, off)
            return db.at[t.slot, at, :, lax.rem(there, 2) * 2 + there // 2]
        if c == 0:
            return db.at[t.slot, 0:2, at, turn(1, off)]
        return db.at[t.slot, 2:4, turn(0, off), at]

    def out_axis(t, c):
        return 2 if t is C2 else 1 - c

    def out_colors(t):
        return (0,) if t is C2 else (0, 1)

    def out_slot(t, c, p, at):
        return r1.at[t.slot, p, at] if t is C2 else r1.at[t.slot, p, 2 * c:2 * c + 2, at]

    parts = (pl.ds(0, 2), pl.ds(2, 2))
    whole = pl.ds(0, 4)

    def add_into(to, *terms):
        n = to.shape[0]

        @pl.loop(0, n)
        def _(i):
            if len(terms) == 1:
                to[i] = to[i] + terms[0][i]
            else:
                total = to[i].astype(f32)
                for term in terms:
                    total = total + term[i].astype(f32)
                to[i] = total.astype(bf)

    def out_first(t):
        for i in range(4):
            arrived(db.at[t.slot, i], bdr.at[t.index, i])
            if t is C2:
                add_into(db.at[t.slot, i], w.at[12 + i, :, :, :, lanes])
            else:
                add_into(db.at[t.slot, i], w.at[t.out + 2 * core + i // 2, :, :, :, halves[i % 2]])
            if t is C2 and i < 3 or i % 2 == 0:
                continue
            c = 0 if t is C2 else i // 2
            for p, off, to in ((0, 2, s), (1, -s, -s)):
                for h, at in enumerate(parts):
                    start(t.back, out_line(t, c, off, at), out_slot(t, c, p, at), b1s.at[t.index, c, 2 * p + h],
                          b1r.at[t.index, c, 2 * p + h], peer(out_axis(t, c), to))

    def out_second(t):
        for h, at in enumerate(parts):
            for c in out_colors(t):
                arrived(out_slot(t, c, 0, at), b1r.at[t.index, c, h])
                here = out_line(t, c, s, at)
                add_into(here, out_slot(t, c, 0, at))
                start(t.back, here, out_slot(t, c, 2, at), b1s.at[t.index, c, 4 + h], b1r.at[t.index, c, 4 + h],
                      peer(out_axis(t, c), s))

    def out_third(t):
        for c in out_colors(t):
            for p in (1, 2):
                for h, at in enumerate(parts):
                    arrived(out_slot(t, c, p, at), b1r.at[t.index, c, 2 * p + h])
            if t is C2:
                @pl.loop(0, 4)
                def _(i):
                    total = db[t.slot, i, :, qm].astype(f32)
                    for p in (1, 2):
                        total = total + r1[t.slot, p, i].astype(f32)
                    ptot[i] = total.astype(bf)
            else:
                add_into(out_line(t, c, 0, whole), out_slot(t, c, 1, whole), out_slot(t, c, 2, whole))
            for o in (1, 3, 2):
                if t is C2:
                    src, dst, to, sent = ptot.at[:, turn(1, o)], r2a.at[o - 1], yp[o], t.late
                elif c == 0:
                    src, dst, to, sent = db.at[t.slot, 0:2, turn(0, o), y], r2.at[t.slot, o - 1, 0:2], xp[o], t.back
                else:
                    src, dst, to, sent = db.at[t.slot, 2:4, x, turn(1, o)], r2.at[t.slot, o - 1, 2:4], yp[o], t.back
                start(sent, src, dst, b2s.at[t.index, c, o - 1], b2r.at[t.index, c, o - 1], to)

    def out_fourth(t):
        if t is C2:
            for o in (0, 1, 2):
                arrived(r2a.at[o], b2r.at[3, 0, o])
            add_into(ptot.at[:, y], *[r2a.at[o] for o in (0, 1, 2)])
            for o in (1, 3, 2):
                start(t.late, ptot.at[turn(0, o), y], r2b.at[o - 1], b2s.at[3, 1, o - 1], b2r.at[3, 1, o - 1], xp[o])
            return
        for c in (0, 1):
            for o in (0, 1, 2):
                arrived(r2.at[t.slot, o, 2 * c:2 * c + 2], b2r.at[t.index, c, o])
            for h in (0, 1):
                total = db[t.slot, 2 * c + h, x, y].astype(f32)
                for o in (0, 1, 2):
                    total = total + r2[t.slot, o, 2 * c + h].astype(f32)
                red[c, :, h * HALF:(h + 1) * HALF] = total.astype(bf)
        shares[t.index] = dot(split_matrix(), red[...].reshape(96, D)).astype(bf).reshape(8, 16, D)
        for o in (1, 3, 2):
            start(t.late, shares.at[t.index, pl.ds(member(turn(2, o), 0), 2)], r3.at[t.index, o - 1], b3s.at[t.index, o - 1],
                  b3r.at[t.index, o - 1], zp[o])

    def out_fifth(t):
        if t is C2:
            for o in (0, 1, 2):
                arrived(r2b.at[o], b2r.at[3, 1, o])
            total = ptot[x, y].astype(f32)
            for o in (0, 1, 2):
                total = total + r2b[o].astype(f32)
            c2sum[core] = total.astype(bf)
            start(t.late, c2sum.at[core], c2sum.at[core], b4s.at[3], b4r.at[3], partner)
            return
        for o in (0, 1, 2):
            arrived(r3.at[t.index, o], b3r.at[t.index, o])
        base = member(z, 0)

        def share(c):
            total = shares[t.index, base + c].astype(f32)
            for o in (0, 1, 2):
                total = total + r3[t.index, o, c].astype(f32)
            return total
        fin[t.index, core] = share(core)
        sx[t.index] = share(other).astype(bf)
        start(t.late, sx.at[t.index], r4.at[t.index], b4s.at[t.index], b4r.at[t.index], partner)

    def out_last(t):
        if t is C2:
            arrived(c2sum.at[other], b4r.at[3])
            rows = jnp.concatenate([c2sum[0], c2sum[1]], 1).astype(f32)
            fin2[...] = jnp.where(core == 0, rows[:24], rows[24:])
            return
        arrived(r4.at[t.index], b4r.at[t.index])
        fin[t.index, other] = r4[t.index].astype(f32)

    def give_credit(t):
        sends_done(t.back)
        for to in near:
            pl.semaphore_signal(credit.at[t.slot], inc=1, device_id=to, device_id_type=MESH)

    def take_credit(t):
        pl.semaphore_wait(credit.at[t.slot], len(near))

    def home_start(i, src, buf):
        for n in (0, 1):
            start(moved, src.at[2 * n + other], buf.at[n], ts.at[i, n], tr.at[i, n], partner)

    def home_sum(i, src, buf, out):
        for n in (0, 1):
            arrived(buf.at[n], tr.at[i, n])

            @pl.loop(0, buf.shape[1] // 16)
            def _(a):
                at = pl.ds(pl.multiple_of(a * 16, 16), 16)
                src[2 * n + core, at] = src[2 * n + core, at] + buf[n, at]
        start(moved, src.at[2 * (1 - hi) + core], out.at[hi], ts.at[2, i], tr.at[2, i], home)
        return local(src.at[2 * hi + core], out.at[hi], ls.at[4 + i])

    def result_copies():
        stays = pltpu.make_async_copy(BO.at[core], bo_out.at[hi], ls.at[3])
        passed = remote(BO.at[other], bo_out.at[hi], os_.at[0], tr.at[3, 0], partner)
        crossed = [remote(BO.at[n], bo_out.at[hi], os_.at[n], tr.at[3, 1], device_at(x, y, across, n)) for n in (0, 1)]
        return stays, passed, crossed

    def result_start():
        @pl.when(core == hi)
        def _():
            stays, passed, _ = result_copies()
            stays.start()
            passed.start()

        @pl.when(core != hi)
        def _():
            for c in result_copies()[2]:
                c.start()

    def result_done():
        @pl.when(core == hi)
        def _():
            stays, passed, _ = result_copies()
            stays.wait()
            passed.wait_send()

        @pl.when(core != hi)
        def _():
            for c in result_copies()[2]:
                c.wait_send()
            arrived(bo_out.at[0], tr.at[3, 0])
        arrived(bo_out.at[0], tr.at[3, 1])

    def weight(u):
        return w[u].reshape(D, D)

    def weight_grad(u, a, b):
        @pl.loop(0, 3)
        def _(i):
            at = pl.ds(pl.multiple_of(i * 256, 256), 256)
            w[u, :, :, :, at] = dot_grad(a[...].reshape(-1, D), b[:, at]).astype(bf).reshape(4, 4, 48, 256)

    mine = pl.ds(pl.multiple_of(core * SPAN, 32), SPAN)

    loads = [local(m, s6.at[i], ls.at[6 + i]) for i, m in enumerate((m0, m1, m2, m3, m4, m5, m6, m7))]
    loads += [local(h_in, sh1, ls.at[14]), local(h_out, sh2, ls.at[15])]
    acc[0, 0:96] = jnp.zeros((96, D), f32)
    acc[1, 0:32] = jnp.zeros((32, D), f32)
    for c in loads:
        c.wait()
    for i in range(4):
        acc[0, 6 * i:6 * i + 6] = s6[i].astype(f32)
        acc[0, 32 + 6 * i:38 + 6 * i] = s6[4 + i].astype(f32)
        acc[0, 64 + 6 * i:70 + 6 * i] = sh1[:, D * i:D * i + D].astype(f32)
    acc[0, 24:25, 0:128] = small[0:1].astype(f32)
    acc[1, 0:24] = sh2[...].astype(f32)
    zbuf[me] = acc[0, 0:96].astype(bf)
    c2buf[core] = acc[1, 0:32].astype(bf)
    pl.semaphore_wait(barrier, len(peers))
    z_start(A)
    start(C2.sent, c2buf.at[core], c2buf.at[core], ds.at[3, 0], dr.at[3, 0], partner)
    z_start(B)
    z_start(C1)
    input_start(0)
    input_start(1)
    c2_first()
    z_mid(A)
    spread(A)
    xy1(A)
    c2_second()
    z_mid(B)
    spread(B)
    xy1(B)
    krow = seg2[pl.ds(hi, 1)]
    crow = clip2[pl.ds(hi, 1)]
    ids = jnp.broadcast_to(krow, (8, KEYS)).astype(f32).T[:, 0:1].astype(jnp.int32)
    qcol = jnp.where(core == 0, ids[:SPAN], ids[SPAN:])
    key_at = lax.broadcasted_iota(jnp.int32, (SPAN, KEYS), 1)
    query_at = lax.broadcasted_iota(jnp.int32, (SPAN, KEYS), 0) + core * SPAN
    bias_s[...] = jnp.where((qcol == krow) & (key_at <= query_at), 0.0, BLOCKED)
    bias_c[...] = jnp.where(qcol == crow, 0.0, BLOCKED).astype(bf)
    xy2(A)
    z_mid(C1)
    spread(C1)
    input_forward(0)
    relay(A)
    xy2(B)
    xy1(C1)
    c2_third()
    input_ready(0)
    hand_over(A)

    S = sm[...].astype(f32).reshape(16, 16, 128)[:, :8].reshape(128, 128).astype(bf)
    owner, inner, which = vector_tables()
    vec[...] = dot_back(which, (dot(owner, S) * inner).astype(bf))
    for n in range(4):
        owner, inner = hidden_tables(n)
        hib[n:n + 1] = dot_back(jnp.ones((8, 128), bf), (dot(owner, S) * inner).astype(bf))[0:1]

    @pl.loop(0, 4)
    def _(i):
        n, _ = normed(tok[i].astype(f32))
        first[pl.ds(pl.multiple_of(i * 112, 16), 112)] = (n * vec[0:1] + vec[1:2]).astype(bf)
    grad_start()
    finish(A)

    def keys(at):
        k[at] = dot(first[at], weight(1)).astype(bf)
    blocks(KEYS, SPAN, keys)
    relay(B)
    xy2(C1)

    def values(at):
        v[at] = (dot(first[at], weight(2)) + vec[3:4]).astype(bf)
    blocks(KEYS, SPAN, values)
    q[...] = (dot(first[mine], weight(0)) + vec[2:3]).astype(bf) * SCALE
    hand_over(B)
    attend(q, k, v, bias_s, mixed, lse, 0, 3)
    relay(C1)
    input_forward(1)
    attend(q, k, v, bias_s, mixed, lse, 3, 6)
    after_self[...] = tok[pl.ds(2 * core, 2)].reshape(SPAN, D).astype(f32) + dot(mixed[...], weight(3)) + vec[4:5]
    n, r = normed(after_self[...])
    second[...] = (n * vec[5:6] + vec[6:7]).astype(bf)
    finish(B)
    c2_relay()
    cq[...] = (dot(second[...], weight(4)) + vec[7:8]).astype(bf) * SCALE
    hand_over(C1)
    input_ready(1)

    @pl.loop(0, 4)
    def _(i):
        ck[pl.ds(pl.multiple_of(i * 384, 128), 384)] = dot(enc[i], weight(5)).astype(bf)

    @pl.loop(0, 4)
    def _(i):
        cv[pl.ds(pl.multiple_of(i * 384, 128), 384)] = (dot(enc[i], weight(6)) + vec[8:9]).astype(bf)
    attend(cq, ck, cv, bias_c, cmixed, clse, 0, 3)
    c2_hand()
    attend(cq, ck, cv, bias_c, cmixed, clse, 3, 6)
    stream[...] = after_self[...] + dot(cmixed[...], weight(7)) + vec[9:10]
    n, r = normed(stream[...])
    third[...] = (n * vec[10:11] + vec[11:12]).astype(bf)
    acc[0] = stream[...] + vec[12:13]
    acc[1] = jnp.zeros((SPAN, D), f32)
    grad_ready()
    g[...] = og[...].reshape(SPAN, D)
    finish(C1)
    c2_finish()
    for t in (A, B, C1, C2):
        sends_done(t.sent)
    sends_done(moved)
    for i in range(4):
        pre = dot(third[...], weight(8 + i)) + hib[i:i + 1]
        cdf = 0.5 * (1.0 + lax.erf(pre * 0.7071067811865476))
        act = (pre * cdf).astype(bf)
        slope = cdf + pre * (0.3989422804014327 * jnp.exp(-0.5 * pre * pre))
        wide[0] = act
        acc[0] += dot(act, weight(12 + i))
        g_pre = (dot_back(g[...], weight(12 + i)) * slope).astype(bf)
        wide[1] = g_pre
        weight_grad(12 + i, wide.at[0], g)
        ghib[i:i + 1] = row_sum(g_pre.astype(f32))
        acc[1] += dot_back(g_pre, weight(8 + i))
        weight_grad(8 + i, third, wide.at[1])
        out_early(i)
    BO[...] = acc[0].astype(bf).reshape(2, 112, D)
    e = acc[1]
    ogf = g[...].astype(f32)
    n, r = normed(stream[...])
    gvec[13:16] = jnp.zeros((3, D), f32)
    gvec[12:13] = row_sum(ogf)
    gvec[10:11] = row_sum(e * n)
    gvec[11:12] = row_sum(e)
    stream[...] = ogf + norm_back(e, n, r, vec[10:11])
    wide[0] = stream[...].astype(bf)
    gvec[9:10] = row_sum(wide[0].astype(f32))
    out_first(C2)
    g[...] = dot_back(wide[0], weight(7)).astype(bf)
    out_first(C1)
    result_start()
    sends_done(C2.sent)
    sends_done(C1.sent)
    weight_grad(15, cmixed, wide.at[0])
    attend_back(cq, ck, cv, bias_c, cmixed, clse, g, gq, ck, cv, 0, 2)
    out_second(C1)
    attend_back(cq, ck, cv, bias_c, cmixed, clse, g, gq, ck, cv, 2, 4)
    out_third(C1)
    out_second(C2)
    attend_back(cq, ck, cv, bias_c, cmixed, clse, g, gq, ck, cv, 4, 6)
    out_fourth(C1)
    give_credit(C1)
    weight_grad(13, enc, ck)
    weight_grad(14, enc, cv)
    weight_grad(12, second, gq)
    take_credit(B)
    out_start(B)
    out_third(C2)
    e = dot_back(gq[...], weight(4))
    gvec[7:8] = row_sum(gq[...].astype(f32))
    gvec[8:9] = row_sum(cv[...].astype(f32))
    n, r = normed(after_self[...])
    gvec[5:6] = row_sum(e * n)
    gvec[6:7] = row_sum(e)
    stream[...] += norm_back(e, n, r, vec[5:6])
    out_first(B)
    give_credit(C2)
    wide[0] = stream[...].astype(bf)
    gvec[4:5] = row_sum(wide[0].astype(f32))
    g[...] = dot_back(wide[0], weight(3)).astype(bf)
    weight_grad(11, mixed, wide.at[0])
    attend_back(q, k, v, bias_s, mixed, lse, g, gq, k, v, 0, 6)
    out_second(B)
    wide[0] = first[mine]
    weight_grad(8, wide.at[0], gq)
    weight_grad(9, first, k)
    weight_grad(10, first, v)
    take_credit(A)
    out_start(A)
    out_third(B)

    @pl.loop(0, 4)
    def _(i):
        at = pl.ds(pl.multiple_of(i * 384, 128), 384)
        enc[i] = (dot_back(ck[at], weight(5)) + dot_back(cv[at], weight(6))).astype(bf)
    home_start(1, enc, eib)
    out_first(A)
    out_fourth(B)
    out_fourth(C2)
    ends = [home_sum(1, enc, eib, ep_out)]
    gvec[2:3] = row_sum(gq[...].astype(f32))
    gvec[3:4] = row_sum(v[...].astype(f32))
    gvec[0:2] = jnp.zeros((2, D), f32)
    acc[0] = dot_back(gq[...], weight(0))
    for h in (0, 1):
        at = pl.ds(h * SPAN, SPAN)
        is_own = core == h
        e = dot_back(k[at], weight(1)) + dot_back(v[at], weight(2)) + jnp.where(is_own, acc[0], 0.0)
        n, r = normed(tok[2 * h:2 * h + 2].reshape(SPAN, D).astype(f32))
        gvec[0:1] += row_sum(e * n)
        gvec[1:2] += row_sum(e)
        PI[2 * h:2 * h + 2] = (norm_back(e, n, r, vec[0:1]) + jnp.where(is_own, stream[...], 0.0)).astype(bf).reshape(2, 112, D)
    home_start(0, PI, pib)
    out_second(A)
    owner, inner, which = vector_tables()
    spread_out = lax.dot_general(gvec[...].astype(bf), which, (((0,), (0,)), ((), ())), preferred_element_type=f32)
    total = dot_grad(owner, (spread_out * inner).astype(bf))
    for n in range(4):
        owner, inner = hidden_tables(n)
        column = jnp.broadcast_to(ghib[n:n + 1], (8, D)).T[:, 0:1]
        total = total + dot_grad(owner, (column * inner).astype(bf))
    SG[...] = total.reshape(4, 4, 8, 128)
    swap = remote(SG, sd, gss.at[0], gsr.at[0], partner)
    swap.start()
    swap.wait()
    SG[...] = SG[...] + sd[...]
    for p in (1, 2, 3):
        start(moved, SG.at[:, turn(1, p)], s1b.at[p], gss.at[p], gsr.at[p], yp[p])
    ends.append(home_sum(0, PI, pib, pi_out))
    out_third(A)
    out_fifth(C2)
    out_fifth(C1)
    out_fifth(B)
    total = SG[:, y]
    for p in (1, 2, 3):
        arrived(s1b.at[p], gsr.at[p])
        total = total + s1b[p]
    SG[:, y] = total
    for b in (1, 2, 3):
        start(moved, SG.at[turn(0, b), y], s2b.at[b], gss.at[3 + b], gsr.at[3 + b], xp[b])
    out_fourth(A)
    total = SG[x, y]
    for b in (1, 2, 3):
        arrived(s2b.at[b], gsr.at[3 + b])
        total = total + s2b[b]
    s3b[0] = total
    for o in (1, 2, 3):
        start(moved, s3b.at[0], s3b.at[o], gss.at[6 + o], gsr.at[6 + o], zp[o])
    out_last(C2)
    out_last(C1)
    out_last(B)
    out_fifth(A)
    total = s3b[0]
    for o in (1, 2, 3):
        arrived(s3b.at[o], gsr.at[6 + o])
        total = total + s3b[o]
    own_row = lax.broadcasted_iota(jnp.int32, (8, 128), 0) == me
    gs[...] = jnp.broadcast_to(jnp.sum(jnp.where(own_row, total, 0.0), 0, keepdims=True), (8, 128))
    arrived(ep_out.at[0], tr.at[2, 1])
    arrived(pi_out.at[0], tr.at[2, 0])

    result_done()
    out_last(A)
    for c in ends:
        c.wait()
    for t in (A, B, C1, C2):
        sends_done(t.sent)
        sends_done(t.back)
        sends_done(t.late)
    sends_done(moved)


def layer(*operands):
    V, DMA, S = pltpu.VMEM, pltpu.SemaphoreType.DMA, jax.ShapeDtypeStruct
    vm, hbm = pl.BlockSpec(memory_space=pltpu.VMEM), pl.BlockSpec(memory_space=pl.ANY)
    return pl.pallas_call(
        layer_kernel,
        out_shape=[S((3, 2, 16, D), f32), S((24, D), f32), S((8, 128), f32), S((2, 112, D), bf), S((2, 112, D), bf), S((2, 384, D), bf)],
        in_specs=[hbm] * 10 + [vm] + [hbm] * 3 + [vm] * 2, out_specs=[vm] * 3 + [hbm] * 3,
        scratch_shapes=[
            V((16, 4, 4, 48, D), bf), V((8, 6, D), bf), V((6, 4 * D), bf), V((24, D), bf), V((8, 96, D), bf), V((2, 32, D), bf),
            V((4, 4, 16, 128), bf), V((16, 128), bf), V((4, 112, D), bf), V((4, 384, D), bf), V((2, 112, D), bf),
            V((16, D), f32), V((8, D), f32), V((KEYS, D), bf), V((SPAN, D), bf), V((KEYS, D), bf), V((KEYS, D), bf),
            V((SPAN, D), bf), V((6, SPAN, 128), f32), V((SPAN, D), bf), V((SPAN, D), bf), V((FRAMES, D), bf), V((FRAMES, D), bf),
            V((SPAN, D), bf), V((6, SPAN, 128), f32), V((SPAN, D), f32), V((SPAN, D), f32), V((SPAN, D), bf),
            V((2, SPAN, D), f32), V((SPAN, KEYS), f32), V((SPAN, FRAMES), bf), V((SPAN, D), bf), V((SPAN, D), bf),
            V((2, SPAN, D), bf), V((16, D), f32), V((8, D), f32),
            V((2, 112, D), bf), V((4, 112, D), bf), V((2, 112, D), bf), V((2, 384, D), bf),
            V((2, 4, 4, 4, 48, HALF), bf), V((2, 3, 4, 4, 48, HALF), bf), V((2, 3, 4, 48, HALF), bf), V((3, 4, 48, HALF), bf), V((3, 48, HALF), bf), V((4, 4, 48, HALF), bf),
            V((2, 48, D), bf), V((3, 8, 16, D), bf), V((3, 3, 2, 16, D), bf), V((3, 16, D), bf), V((3, 16, D), bf),
            V((2, 48, HALF), bf), V((16, 128), f32),
            V((4, 4, 8, 128), f32), V((4, 4, 8, 128), f32), V((4, 4, 8, 128), f32), V((4, 8, 128), f32), V((4, 8, 128), f32),
            DMA((16,)), DMA((4, 4)), DMA((4, 4)), DMA((4, 4)), DMA((4, 4)), DMA((4, 2, 4)), DMA((4, 2, 4)), DMA((4, 2, 8)), DMA((4, 2, 8)),
            DMA((4, 2, 8)), DMA((4, 2, 8)), DMA((4,)), DMA((4,)), DMA((4,)), DMA((4,)), DMA((6,)), DMA((7,)), DMA((2,)), DMA((2,)),
            DMA((4, 4)), DMA((4, 4)), DMA((4, 2, 6)), DMA((4, 2, 6)), DMA((4, 2, 3)), DMA((4, 2, 3)), DMA((3, 3)), DMA((3, 3)),
            DMA((4,)), DMA((4,)), DMA((10,)), DMA((10,)), DMA((3, 2)), DMA((4, 2)), DMA((2,)), pltpu.SemaphoreType.REGULAR((2,))],
        compiler_params=pltpu.CompilerParams(collective_id=0, has_side_effects=True, vmem_limit_bytes=63 << 20),
        name="layer",
    )(*operands)


def unpack_kernel(*refs):
    ins, outs, (fin, fin2, bo, pi, ep, sems) = refs[:5], refs[5:18], refs[18:]
    copies = [pltpu.make_async_copy(src, dst, sems.at[i]) for i, (src, dst) in enumerate(zip(ins, (fin, fin2, bo, pi, ep)))]
    for c in copies:
        c.start()
    for c in copies:
        c.wait()
    out, gi, ge, mats, h_in, h_out = outs[0], outs[1], outs[2], outs[3:11], outs[11], outs[12]
    out[...] = bo[...][:, None]
    gi[...] = pi[...].astype(f32)[:, None]
    for micro in (0, 1):
        ge[micro, :, 0, :] = ep[micro, :375].astype(f32)
    for i in range(4):
        mats[i][...] = fin[0, i // 2, 6 * (i % 2):6 * (i % 2) + 6]
        mats[4 + i][...] = fin[1, i // 2, 6 * (i % 2):6 * (i % 2) + 6]
        h_in[:, D * i:D * i + D] = fin[2, i // 2, 6 * (i % 2):6 * (i % 2) + 6]
    h_out[...] = fin2[...]


def unpack(fin, fin2, bo, pi, ep):
    S, V, hbm = jax.ShapeDtypeStruct, pltpu.VMEM, pl.BlockSpec(memory_space=pl.ANY)
    return pl.pallas_call(
        unpack_kernel,
        out_shape=[S((2, 1, 112, D), bf), S((2, 1, 112, D), f32), S((2, 375, 1, D), f32)] + [S((6, D), f32)] * 8
        + [S((6, 4 * D), f32), S((24, D), f32)],
        in_specs=[hbm] * 5,
        scratch_shapes=[V((3, 2, 16, D), f32), V((24, D), f32), V((2, 112, D), bf), V((2, 112, D), bf), V((2, 384, D), bf),
                        pltpu.SemaphoreType.DMA((5,))],
        compiler_params=pltpu.CompilerParams(vmem_limit_bytes=60 << 20),
        name="unpack",
    )(fin, fin2, bo, pi, ep)


def per_device(
    tokens, encoder_states, segments, frame_clips, out_grad,
    self_gain, self_shift, self_query, self_query_bias, self_key, self_value, self_value_bias, self_output,
    self_output_bias, cross_gain, cross_shift, cross_query, cross_query_bias, cross_key, cross_value,
    cross_value_bias, cross_output, cross_output_bias, final_gain, final_shift, hidden_in, hidden_in_bias,
    hidden_out, hidden_out_bias,
):
    vectors = (self_gain, self_shift, self_query_bias, self_value_bias, self_output_bias, cross_gain, cross_shift,
               cross_query_bias, cross_value_bias, cross_output_bias, final_gain, final_shift, hidden_out_bias)
    small = jnp.pad(hidden_in_bias.astype(f32), (78, 26))
    for i, vector in enumerate(vectors):
        small = small + jnp.pad(vector.astype(f32), (6 * i, 122 - 6 * i))
    small = jnp.broadcast_to(small[None], (8, 128))
    frames = jnp.pad(encoder_states, ((0, 0), (0, 0), (0, 9), (0, 0))).reshape(2, 384, D)
    clip = jnp.pad(frame_clips.reshape(2, 4, 375), ((0, 0), (0, 0), (0, 9)), constant_values=-1).reshape(2, FRAMES)
    fin, fin2, gs, bo, pi, ep = layer(
        self_query, self_key, self_value, self_output, cross_query, cross_key, cross_value, cross_output, hidden_in, hidden_out,
        small, tokens[:, 0], frames, out_grad[:, 0], segments[:, 0], clip)
    out, gi, ge, *m = unpack(fin, fin2, bo, pi, ep)
    gv = [gs[0, 6 * i:6 * i + 6] for i in range(13)]
    return (out, gi, ge.transpose(0, 2, 1, 3),
            gv[0], gv[1], m[0], gv[2], m[1], m[2], gv[3], m[3], gv[4],
            gv[5], gv[6], m[4], gv[7], m[5], m[6], gv[8], m[7], gv[9],
            gv[10], gv[11], m[8], gs[0, 78:102], m[9], gv[12])


def solution(mesh):
    rows = P(None, "win", "seq", None)
    vector, matrix = P(("win", "seq")), P(("win", "seq"), None)
    kinds = "vvmvmmvmvvvmvmmvmvvvmvmv"
    weights = tuple(matrix if kind == "m" else vector for kind in kinds)
    in_specs = (rows, rows, P(None, "win", None), P(None, "win", None), rows) + weights
    return jax.shard_map(per_device, mesh=mesh, in_specs=in_specs, out_specs=(rows, rows, rows) + weights, check_vma=False)
```

```python
import jax
import jax.numpy as jnp
from jax import lax
from jax.experimental import pallas as pl
from jax.experimental.pallas import tpu as pltpu
from jax.sharding import PartitionSpec as P

bf, f32 = jnp.bfloat16, jnp.float32
HEAD_DIM = 64
EPS = 1e-05
SCALE = 0.125
BLOCKED = -1e30
MESH = pl.DeviceIdType.MESH
D = 768
HALF = D // 2


def coords():
    win, seq = lax.axis_index("win"), lax.axis_index("seq")
    x, y = win // 8, lax.rem(win // 2, 4)
    z = (seq // 2) * 2 + lax.rem(win, 2)
    return x, y, z, lax.rem(seq, 2)


def device_at(x, y, z, core):
    return (x * 8 + y * 2 + lax.rem(z, 2), (z // 2) * 2 + core)


def member(z, core):
    return lax.rem(z, 2) * 4 + (z // 2) * 2 + core


KEYS, FRAMES, SPAN = 448, 1536, 224


def dot(a, b):
    return jnp.dot(a, b, preferred_element_type=f32)


def dot_back(a, b):
    return lax.dot_general(a, b, (((1,), (1,)), ((), ())), preferred_element_type=f32)


def dot_grad(a, b):
    return lax.dot_general(a, b, (((0,), (0,)), ((), ())), preferred_element_type=f32)


def normed(values):
    mean = jnp.mean(values, -1, keepdims=True)
    centered = values - mean
    spread = jnp.mean(centered * centered, -1, keepdims=True)
    r = lax.rsqrt(spread + EPS)
    return centered * r, r


def norm_back(e, n, r, gain):
    eg = e * gain
    return r * (eg - jnp.mean(eg, -1, keepdims=True) - n * jnp.mean(eg * n, -1, keepdims=True))


def row_sum(v):
    return jnp.sum(v, 0, keepdims=True)


def one_head(v, e):
    at = lax.broadcasted_iota(jnp.int32, v.shape, 1)
    return jnp.where((at < 64) if e == 0 else (at >= 64), v, jnp.zeros_like(v))


def two_heads(a, b):
    at = lax.broadcasted_iota(jnp.int32, a.shape, 1)
    return jnp.where(at < 64, a, b)


def attend(q, k, v, bias, mixed, lse, begin, end):
    @pl.loop(begin, end)
    def _(j):
        at = pl.ds(pl.multiple_of(j * 128, 128), 128)
        qp, kp, vp = q[:, at], k[:, at], v[:, at]
        outs, logs = [], []
        for e in (0, 1):
            s = dot_back(one_head(qp, e), kp) + bias[...]
            top = jnp.max(s, 1, keepdims=True)
            p = jnp.exp(s - top)
            total = jnp.sum(p, 1, keepdims=True)
            outs.append(dot(p.astype(bf), vp) / total)
            logs.append(top + jnp.log(total))
        mixed[:, at] = two_heads(*outs).astype(bf)
        lse[j] = two_heads(*[jnp.broadcast_to(log, (SPAN, 128)) for log in logs])


def attend_back(q, k, v, bias, mixed, lse, g, gq, gk, gv, begin, end):
    @pl.loop(begin, end)
    def _(j):
        at = pl.ds(pl.multiple_of(j * 128, 128), 128)
        qp, kp, vp, gp = q[:, at], k[:, at], v[:, at], g[:, at]
        product = gp.astype(f32) * mixed[:, at].astype(f32)
        dq, dk, dv = [], 0.0, 0.0
        for e in (0, 1):
            qe, ge = one_head(qp, e), one_head(gp, e)
            s = dot_back(qe, kp) + bias[...]
            p = jnp.exp(s - lse[j, :, 64 * e:64 * e + 1])
            dp = dot_back(ge, vp)
            delta = jnp.sum(one_head(product, e), 1, keepdims=True)
            ds = (p * (dp - delta)).astype(bf)
            dk = dk + dot_grad(ds, qe)
            dv = dv + dot_grad(p.astype(bf), ge)
            dq.append(dot(ds, kp) * SCALE)
        gk[:, at] = dk.astype(bf)
        gv[:, at] = dv.astype(bf)
        gq[:, at] = two_heads(*dq).astype(bf)


def blocks(total, step, body):
    @pl.loop(0, total // step)
    def _(i):
        body(pl.ds(pl.multiple_of(i * step, step), step))


class Chunk:
    def __init__(self, index, base, row, rows, step=0):
        self.index, self.base, self.row, self.rows, self.step = index, base, row, rows, step
        self.half = step > 0
        self.sent = []


class Share:
    def __init__(self, index, out, slot, fin, kind="full", first=0):
        self.index, self.out, self.slot, self.fin, self.first = index, out, slot, fin, first
        self.half, self.across = kind == "half", kind == "across"
        self.pieces = 2 if self.half else 4
        self.sent, self.back, self.late = [], [], []

    def blocks(self, c):
        return pl.ds(self.first + c, 1) if self.half else pl.ds(2 * c, 2)


def one_hot(source, width):
    cols = lax.broadcasted_iota(jnp.int32, (source.shape[0], width), 1)
    return jnp.where(cols == source, 1.0, 0.0).astype(bf)


def spread_matrix(core, half):
    r = lax.broadcasted_iota(jnp.int32, (48 if half else 96, 1), 0)
    piece, at = r // 48, lax.rem(r, 48)
    unit, stride = (core, 16) if half else (2 * core + piece, 32)
    return one_hot((at // 6) * stride + unit * 6 + lax.rem(at, 6), 8 * stride)


def split_matrix(half):
    r = lax.broadcasted_iota(jnp.int32, (128, 1), 0)
    k, i = r // 16, lax.rem(r, 16)
    count = 6 if half else 12
    return one_hot(jnp.where(i < count, (i // 6) * 48 + 6 * k + lax.rem(i, 6), -1), 4 * count * 2)


def vector_tables():
    f = lax.broadcasted_iota(jnp.int32, (D, 128), 0)
    c = lax.broadcasted_iota(jnp.int32, (D, 128), 1)
    owner = jnp.where((f >= 6 * c) & (f < 6 * c + 6), 1.0, 0.0).astype(bf)
    inner = jnp.where(lax.rem(f, 6) == lax.rem(c, 6), 1.0, 0.0)
    v = lax.broadcasted_iota(jnp.int32, (16, 128), 0)
    c = lax.broadcasted_iota(jnp.int32, (16, 128), 1)
    which = jnp.where((c >= 6 * v) & (c < 6 * v + 6) & (v < 13), 1.0, 0.0).astype(bf)
    return owner, inner, which


def hidden_tables(n):
    q = lax.broadcasted_iota(jnp.int32, (D, 128), 0)
    c = lax.broadcasted_iota(jnp.int32, (D, 128), 1)
    start = 24 * (c - 32 * n)
    owner = jnp.where((q >= start) & (q < start + 24), 1.0, 0.0).astype(bf)
    inner = jnp.where(c == 78 + lax.rem(q, 24), 1.0, 0.0)
    return owner, inner


def layer_kernel(m0, m1, m2, m3, m4, m5, m6, m7, h_in, h_out, small, tok_in, enc_in, og_in, seg2, clip2,
                 fin, fin2, gs, bo_out, pi_out, ep_out,
                 w, s6, sh1, sh2, zbuf, c2buf, sm, smbuf, tok, enc, og, vec, hib, first, q, k, v, mixed, lse, second, cq, ck, cv,
                 cmixed, clse, after_self, stream, third, acc, bias_s, bias_c, g, gq, wide, gvec, ghib,
                 BO, PI, pib, eib, db, r1, r2, r2a, r2b, ptot, red, shares, r3, sx, r4, c2sum, c2r, SG, sd, s1b, s2b, s3b,
                 clips, ls, zs, zr, ds, dr, as1, ar1, as2, ar2, cs, cr, ss1, sr1, ss2, sr2, es, er, fs, fr,
                 bds, bdr, b1s, b1r, b2s, b2r, b3s, b3r, b4s, b4r, gss, gsr, ts, tr, os_, credit):
    x, y, z, core = coords()
    hi = z // 2
    other = 1 - core
    s = 1 - 2 * core
    partner = device_at(x, y, z, other)
    across = lax.rem(z + 2, 4)
    home = device_at(x, y, across, core)
    pos = (x, y, z)

    def turn(axis, off):
        return lax.rem(pos[axis] + off + 8, 4)

    def peer(axis, off):
        at = list(pos)
        at[axis] = turn(axis, off)
        return device_at(at[0], at[1], at[2], core)
    xp = [None] + [peer(0, o) for o in (1, 2, 3)]
    yp = [None] + [peer(1, o) for o in (1, 2, 3)]
    zp = [None] + [peer(2, o) for o in (1, 2, 3)]
    near = [partner] + xp[1:] + yp[1:]
    peers = near + [device_at(x, y, across, other)] + zp[1:]
    barrier = pltpu.get_barrier_semaphore()
    for to in peers:
        pl.semaphore_signal(barrier, inc=1, device_id=to, device_id_type=MESH)
    me = member(z, core)
    qm = me // 2
    lanes = pl.ds(pl.multiple_of(core * HALF, 128), HALF)
    lanes_other = pl.ds(pl.multiple_of(other * HALF, 128), HALF)
    halves = (pl.ds(0, HALF), pl.ds(HALF, HALF))
    A, B, C1, C2 = Chunk(0, 0, 0, 32), Chunk(1, 4, 32, 32), Chunk(2, 8, 64, 32), Chunk(3, 12, 0, 0)
    R1, R2 = Share(0, 8, 1, 0), Share(1, 12, 0, None, "across")
    RB, RA = Share(2, 12, 1, 1), Share(3, 8, 0, 2)
    moved = []

    def remote(src, dst, send, recv, to):
        return pltpu.make_async_remote_copy(src_ref=src, dst_ref=dst, send_sem=send, recv_sem=recv,
                                            device_id=to, device_id_type=MESH)

    def start(sent, *a):
        c = remote(*a)
        c.start()
        sent.append(c)

    def arrived(at, sem):
        remote(at, at, fs.at[0], sem, partner).wait_recv()

    def local(src, dst, sem):
        c = pltpu.make_async_copy(src, dst, sem)
        c.start()
        return c

    def sends_done(sent):
        for c in sent:
            c.wait_send()
        sent.clear()

    def z_start(t):
        at = pl.ds(t.row, t.rows)
        for o in (1, 3, 2):
            start(t.sent, zbuf.at[me, at], zbuf.at[me, at], zs.at[t.index, o], zr.at[t.index, o], zp[o])
        start(t.sent, zbuf.at[me, at], zbuf.at[me, at], ds.at[t.index, 0], dr.at[t.index, 0], partner)

    def z_mid(t):
        at = pl.ds(t.row, t.rows)
        for o in (1, 3, 2):
            here = zbuf.at[member(turn(2, -o), core), at]
            arrived(here, zr.at[t.index, o])
            start(t.sent, here, here, ds.at[t.index, o], dr.at[t.index, o], partner)

    def spread(t):
        at = pl.ds(t.row, t.rows)
        for o in range(4):
            arrived(zbuf.at[me, at], dr.at[t.index, o])
        packed = zbuf[:, at].reshape(8 * t.rows, D)
        slab = dot(spread_matrix(core, t.half), packed).astype(bf)
        if t.half:
            w[t.base + t.step * core, x, y] = slab
        else:
            w[pl.ds(t.base + core * 2, 2), x, y] = slab.reshape(2, 48, D)
        if t is A:
            r = lax.broadcasted_iota(jnp.int32, (16, 1), 0)
            smbuf[...] = dot(one_hot(lax.rem(r, 8) * 32 + 24, 256), packed[:, :128]).astype(bf)
            sm[x, y] = smbuf[...]

    def piece(t, c):
        if t.half:
            return w.at[t.base + t.step * core, x, y, :, halves[c]]
        return w.at[t.base + core * 2 + c, x, y]

    def xy1(t):
        for o in (1, 3, 2):
            for c in (0, 1):
                here = piece(t, c)
                start(t.sent, here, here, as1.at[t.index, c, o], ar1.at[t.index, c, o], (xp, yp)[c][o])
            if t is A:
                start(t.sent, smbuf, sm.at[x, y], ss1.at[o], sr1.at[o], xp[o])

    both = (0, 1)

    def line(t, c, off, h):
        at = pl.ds(2 * h, 2)
        if t.half:
            u = w.at[t.base + t.step * core, :, :, :, halves[c]]
        else:
            u = w.at[t.base + core * 2 + c]
        return u.at[at, turn(1, off)] if c == 0 else u.at[turn(0, off), at]

    def hand(t, c, p, off, h):
        here = line(t, c, off, h)
        start(t.sent, here, here, cs.at[t.index, c, 2 * p + h], cr.at[t.index, c, 2 * p + h], partner)

    def xy2(t):
        for c in (0, 1):
            here = piece(t, c)
            for o in (1, 2, 3):
                arrived(here, ar1.at[t.index, c, o])
        for p, off in ((1, s), (3, -s)):
            for h in both:
                for c in (0, 1):
                    here = line(t, c, 0, h)
                    start(t.sent, here, here, as2.at[t.index, c, 2 * p + h], ar2.at[t.index, c, 2 * p + h], peer(1 - c, off))
        for h in both:
            for c in (0, 1):
                hand(t, c, 0, 0, h)
        if t is A:
            for o in (1, 2, 3):
                arrived(smbuf, sr1.at[o])
            for p in (1, 2, 3):
                start(t.sent, sm.at[:, y], sm.at[:, y], ss2.at[p], sr2.at[p], yp[p])

    def relay(t):
        for h in both:
            for c in (0, 1):
                here = line(t, c, -s, h)
                arrived(here, ar2.at[t.index, c, 2 + h])
                start(t.sent, here, here, as2.at[t.index, c, 4 + h], ar2.at[t.index, c, 4 + h], peer(1 - c, s))
                hand(t, c, 1, -s, h)

    def hand_over(t):
        for p, off in ((3, s), (2, 2)):
            for h in both:
                for c in (0, 1):
                    arrived(line(t, c, off, h), ar2.at[t.index, c, 2 * p + h])
                    hand(t, c, p, off, h)
        if t is A:
            for p in (1, 2, 3):
                arrived(sm.at[:, y], sr2.at[p])

    def finish(t):
        for p in (0, 1, 3, 2):
            for h in both:
                for c in (0, 1):
                    arrived(line(t, c, 0, h), cr.at[t.index, c, 2 * p + h])

    def plane(off, h):
        there = turn(2, off)
        return w.at[pl.ds(12 + 2 * h, 2), :, lax.rem(there, 2) * 2 + there // 2, :, lanes]

    def plane_hand(p, off, h):
        start(C2.sent, plane(off, h), plane(off, h), cs.at[3, 0, 2 * p + h], cr.at[3, 0, 2 * p + h], partner)

    def c2_first():
        arrived(c2buf.at[0], dr.at[3, 0])
        both = c2buf[...].astype(f32)[:, :24].reshape(48, D).astype(bf)
        w[12 + x, y, qm, :, lanes] = jnp.where(core == 0, both[:, :HALF], both[:, HALF:])
        here = w.at[12 + x, y, qm, :, lanes]
        for o in (1, 3, 2):
            to = device_at(turn(0, o * other), turn(1, o * core), z, core)
            start(C2.sent, here, here, as1.at[3, 0, o], ar1.at[3, 0, o], to)

    def c2_second():
        here = w.at[12 + x, y, qm, :, lanes]
        for o in (1, 2, 3):
            arrived(here, ar1.at[3, 0, o])
        lines = (w.at[12:16, y, qm, :, lanes], w.at[12 + x, :, qm, :, lanes])
        copies = [[remote(ref, ref, as1.at[3, 1, o], ar1.at[3, 1, o], device_at(turn(0, o * core), turn(1, o * other), z, core))
                   for o in (1, 3, 2)] for ref in lines]
        for c in both:
            @pl.when(core == c)
            def _():
                for copy in copies[c]:
                    copy.start()
        C2.sent.extend(copies[0])

    def c2_third():
        for o in (1, 2, 3):
            arrived(w.at[12:16, y, qm, :, lanes], ar1.at[3, 1, o])
        for p, off in ((1, s), (3, -s)):
            for h in both:
                start(C2.sent, plane(0, h), plane(0, h), as2.at[3, 0, 2 * p + h], ar2.at[3, 0, 2 * p + h], peer(2, off))
        for h in both:
            plane_hand(0, 0, h)

    def c2_relay():
        for h in both:
            here = plane(-s, h)
            arrived(here, ar2.at[3, 0, 2 + h])
            start(C2.sent, here, here, as2.at[3, 0, 4 + h], ar2.at[3, 0, 4 + h], peer(2, s))
            plane_hand(1, -s, h)

    def c2_hand():
        for p, off in ((3, s), (2, 2)):
            for h in both:
                arrived(plane(off, h), ar2.at[3, 0, 2 * p + h])
                plane_hand(p, off, h)

    def c2_finish():
        for p in range(4):
            for h in both:
                arrived(plane(0, h), cr.at[3, 0, 2 * p + h])

    block = hi * 2 + core
    pairs = ((tok_in, tok), (enc_in, enc))
    own = {}

    def input_start(i):
        src, dst = pairs[i]
        start(moved, src.at[1 - hi], dst.at[block], es.at[i], er.at[i], home)
        start(moved, src.at[hi], dst.at[block], es.at[2 + i], er.at[2 + i], partner)
        own[i] = local(src.at[hi], dst.at[block], ls.at[1 + i])

    def input_forward(i):
        far = pairs[i][1].at[(1 - hi) * 2 + core]
        arrived(far, er.at[i])
        start(moved, far, far, fs.at[i], fr.at[i], partner)

    def input_ready(i):
        here = pairs[i][1].at[0]
        own[i].wait()
        arrived(here, er.at[2 + i])
        arrived(here, fr.at[i])

    def grad_start():
        start(moved, og_in.at[1 - hi], og.at[core], es.at[4], er.at[4 + core], device_at(x, y, across, hi))

        @pl.when(core == hi)
        def _():
            c = pltpu.make_async_copy(og_in.at[hi], og.at[core], ls.at[3])
            c.start()
            c.wait()

        @pl.when(core != hi)
        def _():
            c = remote(og_in.at[hi], og.at[core], es.at[5], er.at[6], partner)
            c.start()
            c.wait_send()

    def grad_ready():
        @pl.when(hi == core)
        def _():
            arrived(og.at[0], er.at[6])

        @pl.when(hi != core)
        def _():
            for i in (0, 1):
                arrived(og.at[0], er.at[4 + i])

    def out_piece(t, i):
        if t.across:
            src = w.at[12 + i, :, :, :, lanes_other]
        elif t.half:
            src = w.at[t.out + other, :, :, :, halves[i]]
        else:
            src = w.at[t.out + 2 * other + i // 2, :, :, :, halves[i % 2]]
        return remote(src, db.at[t.slot, t.first + i], bds.at[t.index, i], bdr.at[t.index, i], partner)

    def out_start(t):
        for i in range(t.pieces):
            c = out_piece(t, i)
            c.start()
            t.sent.append(c)

    def out_early(i):
        c = out_piece(R2, i)
        c.start()
        R2.sent.append(c)
        pieces = [out_piece(R1, 2 * (i % 2) + h) for h in both]

        @pl.when(other == i // 2)
        def _():
            for c in pieces:
                c.start()
        if i < 2:
            R1.sent.extend(pieces)

    def out_line(t, c, off, at):
        if t.across:
            there = turn(2, off)
            return db.at[t.slot, at, :, lax.rem(there, 2) * 2 + there // 2]
        if c == 0:
            return db.at[t.slot, t.blocks(0), at, turn(1, off)]
        return db.at[t.slot, t.blocks(1), turn(0, off), at]

    def out_axis(t, c):
        return 2 if t.across else 1 - c

    def out_colors(t):
        return (0,) if t.across else (0, 1)

    def out_slot(t, c, p, at):
        return r1.at[t.slot, p, at] if t.across else r1.at[t.slot, p, t.blocks(c), at]

    parts = (pl.ds(0, 2), pl.ds(2, 2))
    whole = pl.ds(0, 4)

    def add_into(to, *terms):
        n = to.shape[0]

        @pl.loop(0, n)
        def _(i):
            if len(terms) == 1:
                to[i] = to[i] + terms[0][i]
            else:
                total = to[i].astype(f32)
                for term in terms:
                    total = total + term[i].astype(f32)
                to[i] = total.astype(bf)

    def out_first(t):
        for i in range(t.pieces):
            here = db.at[t.slot, t.first + i]
            arrived(here, bdr.at[t.index, i])
            if t.across:
                add_into(here, w.at[12 + i, :, :, :, lanes])
            elif t.half:
                add_into(here, w.at[t.out + core, :, :, :, halves[i]])
            else:
                add_into(here, w.at[t.out + 2 * core + i // 2, :, :, :, halves[i % 2]])
            if t.across and i < 3 or not t.half and i % 2 == 0:
                continue
            c = 0 if t.across else i if t.half else i // 2
            for p, off, to in ((0, 2, s), (1, -s, -s)):
                for h, at in enumerate(parts):
                    start(t.back, out_line(t, c, off, at), out_slot(t, c, p, at), b1s.at[t.index, c, 2 * p + h],
                          b1r.at[t.index, c, 2 * p + h], peer(out_axis(t, c), to))

    def out_second(t):
        for h, at in enumerate(parts):
            for c in out_colors(t):
                arrived(out_slot(t, c, 0, at), b1r.at[t.index, c, h])
                here = out_line(t, c, s, at)
                add_into(here, out_slot(t, c, 0, at))
                start(t.back, here, out_slot(t, c, 2, at), b1s.at[t.index, c, 4 + h], b1r.at[t.index, c, 4 + h],
                      peer(out_axis(t, c), s))

    def out_third(t):
        for c in out_colors(t):
            for p in (1, 2):
                for h, at in enumerate(parts):
                    arrived(out_slot(t, c, p, at), b1r.at[t.index, c, 2 * p + h])
            if t.across:
                @pl.loop(0, 4)
                def _(i):
                    total = db[t.slot, i, :, qm].astype(f32)
                    for p in (1, 2):
                        total = total + r1[t.slot, p, i].astype(f32)
                    ptot[i] = total.astype(bf)
            else:
                add_into(out_line(t, c, 0, whole), out_slot(t, c, 1, whole), out_slot(t, c, 2, whole))
            for o in (1, 3, 2):
                if t.across:
                    src, dst, to, sent = ptot.at[:, turn(1, o)], r2a.at[o - 1], yp[o], t.late
                elif c == 0:
                    src, dst, to, sent = db.at[t.slot, t.blocks(0), turn(0, o), y], r2.at[t.slot, o - 1, t.blocks(0)], xp[o], t.back
                else:
                    src, dst, to, sent = db.at[t.slot, t.blocks(1), x, turn(1, o)], r2.at[t.slot, o - 1, t.blocks(1)], yp[o], t.back
                start(sent, src, dst, b2s.at[t.index, c, o - 1], b2r.at[t.index, c, o - 1], to)

    def out_fourth(t):
        if t.across:
            for o in (0, 1, 2):
                arrived(r2a.at[o], b2r.at[t.index, 0, o])
            add_into(ptot.at[:, y], *[r2a.at[o] for o in (0, 1, 2)])
            for o in (1, 3, 2):
                start(t.late, ptot.at[turn(0, o), y], r2b.at[o - 1], b2s.at[t.index, 1, o - 1], b2r.at[t.index, 1, o - 1], xp[o])
            return
        for c in (0, 1):
            for o in (0, 1, 2):
                arrived(r2.at[t.slot, o, t.blocks(c)], b2r.at[t.index, c, o])
        for i in range(t.pieces):
            total = db[t.slot, t.first + i, x, y].astype(f32)
            for o in (0, 1, 2):
                total = total + r2[t.slot, o, t.first + i].astype(f32)
            red[i // 2, :, (i % 2) * HALF:(i % 2 + 1) * HALF] = total.astype(bf)
        rows = red[0] if t.half else red[...].reshape(96, D)
        shares[t.fin] = dot(split_matrix(t.half), rows).astype(bf).reshape(8, 16, D)
        for o in (1, 3, 2):
            start(t.late, shares.at[t.fin, pl.ds(member(turn(2, o), 0), 2)], r3.at[t.fin, o - 1], b3s.at[t.fin, o - 1],
                  b3r.at[t.fin, o - 1], zp[o])

    def out_fifth(t):
        if t.across:
            for o in (0, 1, 2):
                arrived(r2b.at[o], b2r.at[t.index, 1, o])
            total = ptot[x, y].astype(f32)
            for o in (0, 1, 2):
                total = total + r2b[o].astype(f32)
            c2sum[core] = total.astype(bf)
            start(t.late, c2sum.at[core], c2sum.at[core], b4s.at[t.index], b4r.at[t.index], partner)
            return
        for o in (0, 1, 2):
            arrived(r3.at[t.fin, o], b3r.at[t.fin, o])
        base = member(z, 0)

        def share(c):
            total = shares[t.fin, base + c].astype(f32)
            for o in (0, 1, 2):
                total = total + r3[t.fin, o, c].astype(f32)
            return total
        fin[t.fin, core] = share(core)
        sx[t.fin] = share(other).astype(bf)
        start(t.late, sx.at[t.fin], r4.at[t.fin], b4s.at[t.index], b4r.at[t.index], partner)

    def out_last(t):
        if t.across:
            arrived(c2sum.at[other], b4r.at[t.index])
            rows = jnp.concatenate([c2sum[0], c2sum[1]], 1).astype(f32)
            fin2[...] = jnp.where(core == 0, rows[:24], rows[24:])
            return
        arrived(r4.at[t.fin], b4r.at[t.index])
        fin[t.fin, other] = r4[t.fin].astype(f32)

    def give_credit(t):
        sends_done(t.back)
        for to in near:
            pl.semaphore_signal(credit.at[t.slot], inc=1, device_id=to, device_id_type=MESH)

    def take_credit(t):
        pl.semaphore_wait(credit.at[t.slot], len(near))

    def home_start(i, src, buf):
        for n in (0, 1):
            start(moved, src.at[2 * n + other], buf.at[n], ts.at[i, n], tr.at[i, n], partner)

    def home_sum(i, src, buf, out):
        for n in (0, 1):
            arrived(buf.at[n], tr.at[i, n])

            @pl.loop(0, buf.shape[1] // 16)
            def _(a):
                at = pl.ds(pl.multiple_of(a * 16, 16), 16)
                src[2 * n + core, at] = src[2 * n + core, at] + buf[n, at]
        start(moved, src.at[2 * (1 - hi) + core], out.at[hi], ts.at[2, i], tr.at[2, i], home)
        return local(src.at[2 * hi + core], out.at[hi], ls.at[4 + i])

    def result_copies():
        stays = pltpu.make_async_copy(BO.at[core], bo_out.at[hi], ls.at[3])
        passed = remote(BO.at[other], bo_out.at[hi], os_.at[0], tr.at[3, 0], partner)
        crossed = [remote(BO.at[n], bo_out.at[hi], os_.at[n], tr.at[3, 1], device_at(x, y, across, n)) for n in (0, 1)]
        return stays, passed, crossed

    def result_start():
        @pl.when(core == hi)
        def _():
            stays, passed, _ = result_copies()
            stays.start()
            passed.start()

        @pl.when(core != hi)
        def _():
            for c in result_copies()[2]:
                c.start()

    def result_done():
        @pl.when(core == hi)
        def _():
            stays, passed, _ = result_copies()
            stays.wait()
            passed.wait_send()

        @pl.when(core != hi)
        def _():
            for c in result_copies()[2]:
                c.wait_send()
            arrived(bo_out.at[0], tr.at[3, 0])
        arrived(bo_out.at[0], tr.at[3, 1])

    def weight(u):
        return w[u].reshape(D, D)

    def weight_grad(u, a, b):
        if a.shape[-2] * (a.shape[0] if len(a.shape) > 2 else 1) <= KEYS:
            w[u] = dot_grad(a[...].reshape(-1, D), b[...]).astype(bf).reshape(4, 4, 48, D)
            return

        @pl.loop(0, 2)
        def _(i):
            at = pl.ds(pl.multiple_of(i * HALF, 128), HALF)
            w[u, pl.ds(2 * i, 2)] = dot_grad(a[:, :, at].reshape(-1, HALF), b[...]).astype(bf).reshape(2, 4, 48, D)

    mine = pl.ds(pl.multiple_of(core * SPAN, 32), SPAN)

    loads = [local(m, s6.at[i], ls.at[6 + i]) for i, m in enumerate((m0, m1, m2, m3, m4, m5, m6, m7))]
    loads += [local(h_in, sh1, ls.at[14]), local(h_out, sh2, ls.at[15])]
    acc[0, 0:96] = jnp.zeros((96, D), f32)
    acc[1, 0:32] = jnp.zeros((32, D), f32)
    for c in loads:
        c.wait()
    for i in range(4):
        acc[0, 6 * i:6 * i + 6] = s6[i].astype(f32)
        acc[0, 32 + 6 * i:38 + 6 * i] = s6[4 + i].astype(f32)
        acc[0, 64 + 6 * i:70 + 6 * i] = sh1[:, D * i:D * i + D].astype(f32)
    acc[0, 24:25, 0:128] = small[...]
    acc[1, 0:24] = sh2[...].astype(f32)
    zbuf[me] = acc[0, 0:96].astype(bf)
    c2buf[core] = acc[1, 0:32].astype(bf)
    pl.semaphore_wait(barrier, len(peers))
    z_start(A)
    start(C2.sent, c2buf.at[core], c2buf.at[core], ds.at[3, 0], dr.at[3, 0], partner)
    z_start(B)
    z_start(C1)
    input_start(0)
    c2_first()
    z_mid(A)
    spread(A)
    xy1(A)
    z_mid(B)
    spread(B)
    xy1(B)
    c2_second()
    z_mid(C1)
    spread(C1)
    xy2(A)
    krow = seg2[hi]
    clips[...] = jnp.full((8, FRAMES), -1, jnp.int32)
    clips[0:1, 0:1500] = clip2[hi]
    raw = clips[...]
    at = lax.broadcasted_iota(jnp.int32, (8, FRAMES), 1)
    moved_ids = raw
    for b in (1, 2, 3):
        moved_ids = jnp.where(at >= 384 * b, pltpu.roll(raw, 9 * b, 1), moved_ids)
    crow = jnp.where(lax.rem(at, 384) < 375, moved_ids, -1)[0:1]
    ids = jnp.broadcast_to(krow, (8, KEYS)).astype(f32).T[:, 0:1].astype(jnp.int32)
    qcol = jnp.where(core == 0, ids[:SPAN], ids[SPAN:])
    key_at = lax.broadcasted_iota(jnp.int32, (SPAN, KEYS), 1)
    query_at = lax.broadcasted_iota(jnp.int32, (SPAN, KEYS), 0) + core * SPAN
    bias_s[...] = jnp.where((qcol == krow) & (key_at <= query_at), 0.0, BLOCKED)
    bias_c[...] = jnp.where(qcol == crow, 0.0, BLOCKED).astype(bf)
    c2_third()
    input_start(1)
    relay(A)
    xy2(B)
    xy1(C1)
    grad_start()
    input_forward(0)
    input_ready(0)
    hand_over(A)

    S = sm[...].astype(f32).reshape(16, 16, 128)[:, :8].reshape(128, 128).astype(bf)
    owner, inner, which = vector_tables()
    vec[...] = dot_back(which, (dot(owner, S) * inner).astype(bf))
    for n in range(4):
        owner, inner = hidden_tables(n)
        hib[n:n + 1] = dot_back(jnp.ones((8, 128), bf), (dot(owner, S) * inner).astype(bf))[0:1]

    @pl.loop(0, 4)
    def _(i):
        n, _ = normed(tok[i].astype(f32))
        first[pl.ds(pl.multiple_of(i * 112, 16), 112)] = (n * vec[0:1] + vec[1:2]).astype(bf)
    finish(A)
    relay(B)
    xy2(C1)

    def keys(at):
        k[at] = dot(first[at], weight(1)).astype(bf)
    blocks(KEYS, SPAN, keys)

    def values(at):
        v[at] = (dot(first[at], weight(2)) + vec[3:4]).astype(bf)
    blocks(KEYS, SPAN, values)
    q[...] = (dot(first[mine], weight(0)) + vec[2:3]).astype(bf) * SCALE
    hand_over(B)
    attend(q, k, v, bias_s, mixed, lse, 0, 3)
    c2_relay()
    relay(C1)
    input_forward(1)
    attend(q, k, v, bias_s, mixed, lse, 3, 6)
    after_self[...] = tok[pl.ds(2 * core, 2)].reshape(SPAN, D).astype(f32) + dot(mixed[...], weight(3)) + vec[4:5]
    n, r = normed(after_self[...])
    second[...] = (n * vec[5:6] + vec[6:7]).astype(bf)
    finish(B)
    cq[...] = (dot(second[...], weight(4)) + vec[7:8]).astype(bf) * SCALE
    hand_over(C1)
    input_ready(1)

    @pl.loop(0, 4)
    def _(i):
        ck[pl.ds(pl.multiple_of(i * 384, 128), 384)] = dot(enc[i], weight(5)).astype(bf)

    @pl.loop(0, 4)
    def _(i):
        cv[pl.ds(pl.multiple_of(i * 384, 128), 384)] = (dot(enc[i], weight(6)) + vec[8:9]).astype(bf)
    attend(cq, ck, cv, bias_c, cmixed, clse, 0, 3)
    c2_hand()
    attend(cq, ck, cv, bias_c, cmixed, clse, 3, 6)
    stream[...] = after_self[...] + dot(cmixed[...], weight(7)) + vec[9:10]
    n, r = normed(stream[...])
    third[...] = (n * vec[10:11] + vec[11:12]).astype(bf)
    acc[0] = stream[...] + vec[12:13]
    acc[1] = jnp.zeros((SPAN, D), f32)
    grad_ready()
    g[...] = og[...].reshape(SPAN, D)
    finish(C1)
    c2_finish()
    for t in (A, B, C1, C2):
        sends_done(t.sent)
    sends_done(moved)
    for i in range(4):
        pre = dot(third[...], weight(8 + i)) + hib[i:i + 1]
        cdf = 0.5 * (1.0 + lax.erf(pre * 0.7071067811865476))
        act = (pre * cdf).astype(bf)
        slope = cdf + pre * (0.3989422804014327 * jnp.exp(-0.5 * pre * pre))
        wide[0] = act
        acc[0] += dot(act, weight(12 + i))
        g_pre = (dot_back(g[...], weight(12 + i)) * slope).astype(bf)
        wide[1] = g_pre
        weight_grad(12 + i, wide.at[0], g)
        ghib[i:i + 1] = row_sum(g_pre.astype(f32))
        acc[1] += dot_back(g_pre, weight(8 + i))
        weight_grad(8 + i, third, wide.at[1])
        out_early(i)
    BO[...] = acc[0].astype(bf).reshape(2, 112, D)
    e = acc[1]
    ogf = g[...].astype(f32)
    n, r = normed(stream[...])
    gvec[13:16] = jnp.zeros((3, D), f32)
    gvec[12:13] = row_sum(ogf)
    gvec[10:11] = row_sum(e * n)
    gvec[11:12] = row_sum(e)
    stream[...] = ogf + norm_back(e, n, r, vec[10:11])
    wide[0] = stream[...].astype(bf)
    gvec[9:10] = row_sum(wide[0].astype(f32))
    out_first(R2)
    g[...] = dot_back(wide[0], weight(7)).astype(bf)
    out_first(R1)
    sends_done(R2.sent)
    sends_done(R1.sent)
    weight_grad(15, cmixed, wide.at[0])
    attend_back(cq, ck, cv, bias_c, cmixed, clse, g, gq, ck, cv, 0, 4)
    out_second(R1)
    attend_back(cq, ck, cv, bias_c, cmixed, clse, g, gq, ck, cv, 4, 6)
    out_second(R2)
    out_third(R1)
    weight_grad(13, enc, ck)
    weight_grad(14, enc, cv)
    weight_grad(12, second, gq)
    out_fourth(R1)
    give_credit(R1)
    e = dot_back(gq[...], weight(4))
    gvec[7:8] = row_sum(gq[...].astype(f32))
    gvec[8:9] = row_sum(cv[...].astype(f32))
    take_credit(RB)
    out_start(RB)
    n, r = normed(after_self[...])
    gvec[5:6] = row_sum(e * n)
    gvec[6:7] = row_sum(e)
    stream[...] += norm_back(e, n, r, vec[5:6])
    wide[0] = stream[...].astype(bf)
    gvec[4:5] = row_sum(wide[0].astype(f32))
    g[...] = dot_back(wide[0], weight(3)).astype(bf)
    weight_grad(11, mixed, wide.at[0])
    out_first(RB)
    out_third(R2)
    give_credit(R2)
    attend_back(q, k, v, bias_s, mixed, lse, g, gq, k, v, 0, 6)
    wide[0] = first[mine]
    weight_grad(8, wide.at[0], gq)
    weight_grad(9, first, k)
    weight_grad(10, first, v)
    take_credit(RA)
    out_start(RA)
    out_second(RB)

    @pl.loop(0, 4)
    def _(i):
        at = pl.ds(pl.multiple_of(i * 384, 128), 384)
        enc[i] = (dot_back(ck[at], weight(5)) + dot_back(cv[at], weight(6))).astype(bf)
    home_start(1, enc, eib)
    out_first(RA)
    out_third(RB)
    out_fourth(R2)
    ends = [home_sum(1, enc, eib, ep_out)]
    result_start()
    gvec[2:3] = row_sum(gq[...].astype(f32))
    gvec[3:4] = row_sum(v[...].astype(f32))
    gvec[0:2] = jnp.zeros((2, D), f32)
    acc[0] = dot_back(gq[...], weight(0))
    for h in (0, 1):
        at = pl.ds(h * SPAN, SPAN)
        is_own = core == h
        e = dot_back(k[at], weight(1)) + dot_back(v[at], weight(2)) + jnp.where(is_own, acc[0], 0.0)
        n, r = normed(tok[2 * h:2 * h + 2].reshape(SPAN, D).astype(f32))
        gvec[0:1] += row_sum(e * n)
        gvec[1:2] += row_sum(e)
        PI[2 * h:2 * h + 2] = (norm_back(e, n, r, vec[0:1]) + jnp.where(is_own, stream[...], 0.0)).astype(bf).reshape(2, 112, D)
    home_start(0, PI, pib)
    out_second(RA)
    out_fourth(RB)
    owner, inner, which = vector_tables()
    spread_out = lax.dot_general(gvec[...].astype(bf), which, (((0,), (0,)), ((), ())), preferred_element_type=f32)
    total = dot_grad(owner, (spread_out * inner).astype(bf))
    for n in range(4):
        owner, inner = hidden_tables(n)
        column = jnp.broadcast_to(ghib[n:n + 1], (8, D)).T[:, 0:1]
        total = total + dot_grad(owner, (column * inner).astype(bf))
    SG[...] = total.reshape(4, 4, 8, 128)
    swap = remote(SG, sd, gss.at[0], gsr.at[0], partner)
    swap.start()
    swap.wait()
    SG[...] = SG[...] + sd[...]
    for p in (1, 2, 3):
        start(moved, SG.at[:, turn(1, p)], s1b.at[p], gss.at[p], gsr.at[p], yp[p])
    ends.append(home_sum(0, PI, pib, pi_out))
    out_third(RA)
    out_fifth(R2)
    out_fifth(R1)
    out_fifth(RB)
    total = SG[:, y]
    for p in (1, 2, 3):
        arrived(s1b.at[p], gsr.at[p])
        total = total + s1b[p]
    SG[:, y] = total
    for b in (1, 2, 3):
        start(moved, SG.at[turn(0, b), y], s2b.at[b], gss.at[3 + b], gsr.at[3 + b], xp[b])
    out_fourth(RA)
    total = SG[x, y]
    for b in (1, 2, 3):
        arrived(s2b.at[b], gsr.at[3 + b])
        total = total + s2b[b]
    s3b[0] = total
    for o in (1, 2, 3):
        start(moved, s3b.at[0], s3b.at[o], gss.at[6 + o], gsr.at[6 + o], zp[o])
    out_last(R2)
    out_last(R1)
    out_last(RB)
    out_fifth(RA)
    total = s3b[0]
    for o in (1, 2, 3):
        arrived(s3b.at[o], gsr.at[6 + o])
        total = total + s3b[o]
    own_row = lax.broadcasted_iota(jnp.int32, (8, 128), 0) == me
    gs[...] = jnp.broadcast_to(jnp.sum(jnp.where(own_row, total, 0.0), 0, keepdims=True), (8, 128))
    arrived(ep_out.at[0], tr.at[2, 1])
    arrived(pi_out.at[0], tr.at[2, 0])

    result_done()
    out_last(RA)
    for c in ends:
        c.wait()
    for t in (R1, R2, RB, RA):
        sends_done(t.sent)
        sends_done(t.back)
        sends_done(t.late)
    sends_done(moved)


def layer(*operands):
    V, DMA, S = pltpu.VMEM, pltpu.SemaphoreType.DMA, jax.ShapeDtypeStruct
    vm, hbm = pl.BlockSpec(memory_space=pltpu.VMEM), pl.BlockSpec(memory_space=pl.ANY)
    return pl.pallas_call(
        layer_kernel,
        out_shape=[S((3, 2, 16, D), f32), S((24, D), f32), S((8, 128), f32), S((2, 112, D), bf), S((2, 112, D), bf), S((2, 384, D), bf)],
        in_specs=[hbm] * 10 + [vm] + [hbm] * 3 + [vm] * 2, out_specs=[vm] * 3 + [hbm] * 3,
        scratch_shapes=[
            V((16, 4, 4, 48, D), bf), V((8, 6, D), bf), V((6, 4 * D), bf), V((24, D), bf), V((8, 96, D), bf), V((2, 32, D), bf),
            V((4, 4, 16, 128), bf), V((16, 128), bf), V((4, 112, D), bf), V((4, 384, D), bf), V((2, 112, D), bf),
            V((16, D), f32), V((8, D), f32), V((KEYS, D), bf), V((SPAN, D), bf), V((KEYS, D), bf), V((KEYS, D), bf),
            V((SPAN, D), bf), V((6, SPAN, 128), f32), V((SPAN, D), bf), V((SPAN, D), bf), V((FRAMES, D), bf), V((FRAMES, D), bf),
            V((SPAN, D), bf), V((6, SPAN, 128), f32), V((SPAN, D), f32), V((SPAN, D), f32), V((SPAN, D), bf),
            V((2, SPAN, D), f32), V((SPAN, KEYS), f32), V((SPAN, FRAMES), bf), V((SPAN, D), bf), V((SPAN, D), bf),
            V((2, SPAN, D), bf), V((16, D), f32), V((8, D), f32),
            V((2, 112, D), bf), V((4, 112, D), bf), V((2, 112, D), bf), V((2, 384, D), bf),
            V((2, 4, 4, 4, 48, HALF), bf), V((2, 3, 4, 4, 48, HALF), bf), V((2, 3, 4, 48, HALF), bf), V((3, 4, 48, HALF), bf), V((3, 48, HALF), bf), V((4, 4, 48, HALF), bf),
            V((2, 48, D), bf), V((3, 8, 16, D), bf), V((3, 3, 2, 16, D), bf), V((3, 16, D), bf), V((3, 16, D), bf),
            V((2, 48, HALF), bf), V((16, 128), f32),
            V((4, 4, 8, 128), f32), V((4, 4, 8, 128), f32), V((4, 4, 8, 128), f32), V((4, 8, 128), f32), V((4, 8, 128), f32),
            V((8, FRAMES), jnp.int32),
            DMA((16,)), DMA((5, 4)), DMA((5, 4)), DMA((5, 4)), DMA((5, 4)), DMA((5, 2, 4)), DMA((5, 2, 4)), DMA((5, 2, 8)), DMA((5, 2, 8)),
            DMA((5, 2, 8)), DMA((5, 2, 8)), DMA((4,)), DMA((4,)), DMA((4,)), DMA((4,)), DMA((6,)), DMA((7,)), DMA((2,)), DMA((2,)),
            DMA((5, 4)), DMA((5, 4)), DMA((5, 2, 6)), DMA((5, 2, 6)), DMA((5, 2, 3)), DMA((5, 2, 3)), DMA((4, 3)), DMA((4, 3)),
            DMA((5,)), DMA((5,)), DMA((10,)), DMA((10,)), DMA((3, 2)), DMA((4, 2)), DMA((2,)), pltpu.SemaphoreType.REGULAR((2,))],
        compiler_params=pltpu.CompilerParams(collective_id=0, has_side_effects=True, vmem_limit_bytes=63 << 20),
        name="layer",
    )(*operands)


def unpack_kernel(*refs):
    ins, outs, (fin, fin2, bo, pi, ep, sems) = refs[:5], refs[5:18], refs[18:]
    copies = [pltpu.make_async_copy(src, dst, sems.at[i]) for i, (src, dst) in enumerate(zip(ins, (fin, fin2, bo, pi, ep)))]
    for c in copies:
        c.start()
    for c in copies:
        c.wait()
    out, gi, ge, mats, h_in, h_out = outs[0], outs[1], outs[2], outs[3:11], outs[11], outs[12]
    out[...] = bo[...][:, None]
    gi[...] = pi[...].astype(f32)[:, None]
    for micro in (0, 1):
        ge[micro, :, 0, :] = ep[micro, :375].astype(f32)
    for i in range(4):
        mats[i][...] = fin[2, i // 2, 6 * (i % 2):6 * (i % 2) + 6]
        mats[4 + i][...] = fin[1, i // 2, 6 * (i % 2):6 * (i % 2) + 6]
        h_in[:, D * i:D * i + D] = fin[0, i // 2, 6 * (i % 2):6 * (i % 2) + 6]
    h_out[...] = fin2[...]


def unpack(fin, fin2, bo, pi, ep):
    S, V, hbm = jax.ShapeDtypeStruct, pltpu.VMEM, pl.BlockSpec(memory_space=pl.ANY)
    return pl.pallas_call(
        unpack_kernel,
        out_shape=[S((2, 1, 112, D), bf), S((2, 1, 112, D), f32), S((2, 375, 1, D), f32)] + [S((6, D), f32)] * 8
        + [S((6, 4 * D), f32), S((24, D), f32)],
        in_specs=[hbm] * 5,
        scratch_shapes=[V((3, 2, 16, D), f32), V((24, D), f32), V((2, 112, D), bf), V((2, 112, D), bf), V((2, 384, D), bf),
                        pltpu.SemaphoreType.DMA((5,))],
        compiler_params=pltpu.CompilerParams(vmem_limit_bytes=60 << 20),
        name="unpack",
    )(fin, fin2, bo, pi, ep)


def per_device(
    tokens, encoder_states, segments, frame_clips, out_grad,
    self_gain, self_shift, self_query, self_query_bias, self_key, self_value, self_value_bias, self_output,
    self_output_bias, cross_gain, cross_shift, cross_query, cross_query_bias, cross_key, cross_value,
    cross_value_bias, cross_output, cross_output_bias, final_gain, final_shift, hidden_in, hidden_in_bias,
    hidden_out, hidden_out_bias,
):
    vectors = (self_gain, self_shift, self_query_bias, self_value_bias, self_output_bias, cross_gain, cross_shift,
               cross_query_bias, cross_value_bias, cross_output_bias, final_gain, final_shift, hidden_out_bias)
    small = jnp.pad(hidden_in_bias.astype(f32), (78, 26))
    for i, vector in enumerate(vectors):
        small = small + jnp.pad(vector.astype(f32), (6 * i, 122 - 6 * i))
    frames = jnp.pad(encoder_states, ((0, 0), (0, 0), (0, 9), (0, 0))).reshape(2, 384, D)
    fin, fin2, gs, bo, pi, ep = layer(
        self_query, self_key, self_value, self_output, cross_query, cross_key, cross_value, cross_output, hidden_in, hidden_out,
        small[None], tokens[:, 0], frames, out_grad[:, 0], segments, frame_clips)
    out, gi, ge, *m = unpack(fin, fin2, bo, pi, ep)
    gv = [gs[0, 6 * i:6 * i + 6] for i in range(13)]
    return (out, gi, ge.transpose(0, 2, 1, 3),
            gv[0], gv[1], m[0], gv[2], m[1], m[2], gv[3], m[3], gv[4],
            gv[5], gv[6], m[4], gv[7], m[5], m[6], gv[8], m[7], gv[9],
            gv[10], gv[11], m[8], gs[0, 78:102], m[9], gv[12])


def solution(mesh):
    rows = P(None, "win", "seq", None)
    vector, matrix = P(("win", "seq")), P(("win", "seq"), None)
    kinds = "vvmvmmvmvvvmvmmvmvvvmvmv"
    weights = tuple(matrix if kind == "m" else vector for kind in kinds)
    in_specs = (rows, rows, P(None, "win", None), P(None, "win", None), rows) + weights
    return jax.shard_map(per_device, mesh=mesh, in_specs=in_specs, out_specs=(rows, rows, rows) + weights, check_vma=False)
```

```python
import jax
import jax.numpy as jnp
from jax import lax
from jax.experimental import pallas as pl
from jax.experimental.pallas import tpu as pltpu
from jax.sharding import PartitionSpec as P

bf, f32 = jnp.bfloat16, jnp.float32
HEAD_DIM = 64
EPS = 1e-05
SCALE = 0.125
BLOCKED = -1e30
MESH = pl.DeviceIdType.MESH
D = 768
HALF = D // 2


def coords():
    win, seq = lax.axis_index("win"), lax.axis_index("seq")
    x, y = win // 8, lax.rem(win // 2, 4)
    z = (seq // 2) * 2 + lax.rem(win, 2)
    return x, y, z, lax.rem(seq, 2)


def device_at(x, y, z, core):
    return (x * 8 + y * 2 + lax.rem(z, 2), (z // 2) * 2 + core)


def member(z, core):
    return lax.rem(z, 2) * 4 + (z // 2) * 2 + core


KEYS, FRAMES, SPAN = 448, 1536, 224


def dot(a, b):
    return jnp.dot(a, b, preferred_element_type=f32)


def dot_back(a, b):
    return lax.dot_general(a, b, (((1,), (1,)), ((), ())), preferred_element_type=f32)


def dot_grad(a, b):
    return lax.dot_general(a, b, (((0,), (0,)), ((), ())), preferred_element_type=f32)


def normed(values):
    mean = jnp.mean(values, -1, keepdims=True)
    centered = values - mean
    spread = jnp.mean(centered * centered, -1, keepdims=True)
    r = lax.rsqrt(spread + EPS)
    return centered * r, r


def norm_back(e, n, r, gain):
    eg = e * gain
    return r * (eg - jnp.mean(eg, -1, keepdims=True) - n * jnp.mean(eg * n, -1, keepdims=True))


def row_sum(v):
    return jnp.sum(v, 0, keepdims=True)


def one_head(v, e):
    at = lax.broadcasted_iota(jnp.int32, v.shape, 1)
    return jnp.where((at < 64) if e == 0 else (at >= 64), v, jnp.zeros_like(v))


def two_heads(a, b):
    at = lax.broadcasted_iota(jnp.int32, a.shape, 1)
    return jnp.where(at < 64, a, b)


def attend(q, k, v, bias, mixed, lse, begin, end):
    @pl.loop(begin, end)
    def _(j):
        at = pl.ds(pl.multiple_of(j * 128, 128), 128)
        qp, kp, vp = q[:, at], k[:, at], v[:, at]
        outs, logs = [], []
        for e in (0, 1):
            s = dot_back(one_head(qp, e), kp) + bias[...]
            top = jnp.max(s, 1, keepdims=True)
            p = jnp.exp(s - top)
            total = jnp.sum(p, 1, keepdims=True)
            outs.append(dot(p.astype(bf), vp) / total)
            logs.append(top + jnp.log(total))
        mixed[:, at] = two_heads(*outs).astype(bf)
        lse[j] = two_heads(*[jnp.broadcast_to(log, (SPAN, 128)) for log in logs])


def attend_back(q, k, v, bias, mixed, lse, g, gq, gk, gv, begin, end):
    @pl.loop(begin, end)
    def _(j):
        at = pl.ds(pl.multiple_of(j * 128, 128), 128)
        qp, kp, vp, gp = q[:, at], k[:, at], v[:, at], g[:, at]
        product = gp.astype(f32) * mixed[:, at].astype(f32)
        dq, dk, dv = [], 0.0, 0.0
        for e in (0, 1):
            qe, ge = one_head(qp, e), one_head(gp, e)
            s = dot_back(qe, kp) + bias[...]
            p = jnp.exp(s - lse[j, :, 64 * e:64 * e + 1])
            dp = dot_back(ge, vp)
            delta = jnp.sum(one_head(product, e), 1, keepdims=True)
            ds = (p * (dp - delta)).astype(bf)
            dk = dk + dot_grad(ds, qe)
            dv = dv + dot_grad(p.astype(bf), ge)
            dq.append(dot(ds, kp) * SCALE)
        gk[:, at] = dk.astype(bf)
        gv[:, at] = dv.astype(bf)
        gq[:, at] = two_heads(*dq).astype(bf)


def blocks(total, step, body):
    @pl.loop(0, total // step)
    def _(i):
        body(pl.ds(pl.multiple_of(i * step, step), step))


class Chunk:
    def __init__(self, index, base, row, rows, step=0):
        self.index, self.base, self.row, self.rows, self.step = index, base, row, rows, step
        self.half = step > 0
        self.sent = []


class Share:
    def __init__(self, index, out, slot, fin, kind="full", first=0):
        self.index, self.out, self.slot, self.fin, self.first = index, out, slot, fin, first
        self.half, self.across = kind == "half", kind == "across"
        self.pieces = 2 if self.half else 4
        self.sent, self.back, self.late = [], [], []

    def blocks(self, c):
        return pl.ds(self.first + c, 1) if self.half else pl.ds(2 * c, 2)


def one_hot(source, width):
    cols = lax.broadcasted_iota(jnp.int32, (source.shape[0], width), 1)
    return jnp.where(cols == source, 1.0, 0.0).astype(bf)


def spread_matrix(core, half):
    r = lax.broadcasted_iota(jnp.int32, (48 if half else 96, 1), 0)
    piece, at = r // 48, lax.rem(r, 48)
    unit, stride = (core, 16) if half else (2 * core + piece, 32)
    return one_hot((at // 6) * stride + unit * 6 + lax.rem(at, 6), 8 * stride)


def split_matrix(half):
    r = lax.broadcasted_iota(jnp.int32, (128, 1), 0)
    k, i = r // 16, lax.rem(r, 16)
    count = 6 if half else 12
    return one_hot(jnp.where(i < count, (i // 6) * 48 + 6 * k + lax.rem(i, 6), -1), 4 * count * 2)


def vector_tables():
    f = lax.broadcasted_iota(jnp.int32, (D, 128), 0)
    c = lax.broadcasted_iota(jnp.int32, (D, 128), 1)
    owner = jnp.where((f >= 6 * c) & (f < 6 * c + 6), 1.0, 0.0).astype(bf)
    inner = jnp.where(lax.rem(f, 6) == lax.rem(c, 6), 1.0, 0.0)
    v = lax.broadcasted_iota(jnp.int32, (16, 128), 0)
    c = lax.broadcasted_iota(jnp.int32, (16, 128), 1)
    which = jnp.where((c >= 6 * v) & (c < 6 * v + 6) & (v < 13), 1.0, 0.0).astype(bf)
    return owner, inner, which


def hidden_tables(n):
    q = lax.broadcasted_iota(jnp.int32, (D, 128), 0)
    c = lax.broadcasted_iota(jnp.int32, (D, 128), 1)
    start = 24 * (c - 32 * n)
    owner = jnp.where((q >= start) & (q < start + 24), 1.0, 0.0).astype(bf)
    inner = jnp.where(c == 78 + lax.rem(q, 24), 1.0, 0.0)
    return owner, inner


def layer_kernel(m0, m1, m2, m3, m4, m5, m6, m7, h_in, h_out, small, tok_in, enc_in, og_in, seg2, clip2,
                 fin, fin2, gs, bo_out, pi_out, ep_out,
                 w, s6, sh1, sh2, zbuf, c2buf, sm, smbuf, tok, enc, og, vec, hib, first, q, k, v, mixed, lse, second, cq, ck, cv,
                 cmixed, clse, after_self, stream, third, acc, bias_s, bias_c, g, gq, wide, gvec, ghib,
                 BO, PI, pib, eib, db, r1, r2, r2a, r2b, ptot, red, shares, r3, sx, r4, c2sum, c2r, SG, sd, s1b, s2b, s3b,
                 clips, ls, zs, zr, ds, dr, as1, ar1, as2, ar2, cs, cr, ss1, sr1, ss2, sr2, es, er, fs, fr,
                 bds, bdr, b1s, b1r, b2s, b2r, b3s, b3r, b4s, b4r, gss, gsr, ts, tr, os_, credit):
    x, y, z, core = coords()
    hi = z // 2
    other = 1 - core
    s = 1 - 2 * core
    partner = device_at(x, y, z, other)
    across = lax.rem(z + 2, 4)
    home = device_at(x, y, across, core)
    pos = (x, y, z)

    def turn(axis, off):
        return lax.rem(pos[axis] + off + 8, 4)

    def peer(axis, off):
        at = list(pos)
        at[axis] = turn(axis, off)
        return device_at(at[0], at[1], at[2], core)
    xp = [None] + [peer(0, o) for o in (1, 2, 3)]
    yp = [None] + [peer(1, o) for o in (1, 2, 3)]
    zp = [None] + [peer(2, o) for o in (1, 2, 3)]
    near = [partner] + xp[1:] + yp[1:]
    peers = near + [device_at(x, y, across, other)] + zp[1:]
    barrier = pltpu.get_barrier_semaphore()
    for to in peers:
        pl.semaphore_signal(barrier, inc=1, device_id=to, device_id_type=MESH)
    me = member(z, core)
    qm = me // 2
    lanes = pl.ds(pl.multiple_of(core * HALF, 128), HALF)
    lanes_other = pl.ds(pl.multiple_of(other * HALF, 128), HALF)
    halves = (pl.ds(0, HALF), pl.ds(HALF, HALF))
    A, B, C1, C2 = Chunk(0, 0, 0, 32), Chunk(1, 4, 32, 32), Chunk(2, 8, 64, 32), Chunk(3, 12, 0, 0)
    R1, R2 = Share(0, 8, 1, 0), Share(1, 12, 0, None, "across")
    RB, RA = Share(2, 12, 1, 1), Share(3, 8, 0, 2)
    moved = []

    def remote(src, dst, send, recv, to):
        return pltpu.make_async_remote_copy(src_ref=src, dst_ref=dst, send_sem=send, recv_sem=recv,
                                            device_id=to, device_id_type=MESH)

    def start(sent, *a):
        c = remote(*a)
        c.start()
        sent.append(c)

    def arrived(at, sem):
        remote(at, at, fs.at[0], sem, partner).wait_recv()

    def local(src, dst, sem):
        c = pltpu.make_async_copy(src, dst, sem)
        c.start()
        return c

    def sends_done(sent):
        for c in sent:
            c.wait_send()
        sent.clear()

    def z_start(t):
        at = pl.ds(t.row, t.rows)
        for o in (1, 3, 2):
            start(t.sent, zbuf.at[me, at], zbuf.at[me, at], zs.at[t.index, o], zr.at[t.index, o], zp[o])
        start(t.sent, zbuf.at[me, at], zbuf.at[me, at], ds.at[t.index, 0], dr.at[t.index, 0], partner)

    def z_mid(t):
        at = pl.ds(t.row, t.rows)
        for o in (1, 3, 2):
            here = zbuf.at[member(turn(2, -o), core), at]
            arrived(here, zr.at[t.index, o])
            start(t.sent, here, here, ds.at[t.index, o], dr.at[t.index, o], partner)

    def spread(t):
        at = pl.ds(t.row, t.rows)
        for o in range(4):
            arrived(zbuf.at[me, at], dr.at[t.index, o])
        packed = zbuf[:, at].reshape(8 * t.rows, D)
        slab = dot(spread_matrix(core, t.half), packed).astype(bf)
        if t.half:
            w[t.base + t.step * core, x, y] = slab
        else:
            w[pl.ds(t.base + core * 2, 2), x, y] = slab.reshape(2, 48, D)
        if t is A:
            r = lax.broadcasted_iota(jnp.int32, (16, 1), 0)
            smbuf[...] = dot(one_hot(lax.rem(r, 8) * 32 + 24, 256), packed[:, :128]).astype(bf)
            sm[x, y] = smbuf[...]

    def piece(t, c):
        if t.half:
            return w.at[t.base + t.step * core, x, y, :, halves[c]]
        return w.at[t.base + core * 2 + c, x, y]

    def xy1(t):
        for o in (1, 3, 2):
            for c in (0, 1):
                here = piece(t, c)
                start(t.sent, here, here, as1.at[t.index, c, o], ar1.at[t.index, c, o], (xp, yp)[c][o])
            if t is A:
                start(t.sent, smbuf, sm.at[x, y], ss1.at[o], sr1.at[o], xp[o])

    both = (0, 1)

    def line(t, c, off, h):
        at = pl.ds(2 * h, 2)
        if t.half:
            u = w.at[t.base + t.step * core, :, :, :, halves[c]]
        else:
            u = w.at[t.base + core * 2 + c]
        return u.at[at, turn(1, off)] if c == 0 else u.at[turn(0, off), at]

    def hand(t, c, p, off, h):
        here = line(t, c, off, h)
        start(t.sent, here, here, cs.at[t.index, c, 2 * p + h], cr.at[t.index, c, 2 * p + h], partner)

    def xy2(t):
        for c in (0, 1):
            here = piece(t, c)
            for o in (1, 2, 3):
                arrived(here, ar1.at[t.index, c, o])
        for p, off in ((1, s), (3, -s)):
            for h in both:
                for c in (0, 1):
                    here = line(t, c, 0, h)
                    start(t.sent, here, here, as2.at[t.index, c, 2 * p + h], ar2.at[t.index, c, 2 * p + h], peer(1 - c, off))
        for h in both:
            for c in (0, 1):
                hand(t, c, 0, 0, h)
        if t is A:
            for o in (1, 2, 3):
                arrived(smbuf, sr1.at[o])
            for p in (1, 2, 3):
                start(t.sent, sm.at[:, y], sm.at[:, y], ss2.at[p], sr2.at[p], yp[p])

    def relay(t):
        for h in both:
            for c in (0, 1):
                here = line(t, c, -s, h)
                arrived(here, ar2.at[t.index, c, 2 + h])
                start(t.sent, here, here, as2.at[t.index, c, 4 + h], ar2.at[t.index, c, 4 + h], peer(1 - c, s))
                hand(t, c, 1, -s, h)

    def hand_over(t):
        for p, off in ((3, s), (2, 2)):
            for h in both:
                for c in (0, 1):
                    arrived(line(t, c, off, h), ar2.at[t.index, c, 2 * p + h])
                    hand(t, c, p, off, h)
        if t is A:
            for p in (1, 2, 3):
                arrived(sm.at[:, y], sr2.at[p])

    def finish(t):
        for p in (0, 1, 3, 2):
            for h in both:
                for c in (0, 1):
                    arrived(line(t, c, 0, h), cr.at[t.index, c, 2 * p + h])

    def plane(off, h):
        there = turn(2, off)
        return w.at[pl.ds(12 + 2 * h, 2), :, lax.rem(there, 2) * 2 + there // 2, :, lanes]

    def plane_hand(p, off, h):
        start(C2.sent, plane(off, h), plane(off, h), cs.at[3, 0, 2 * p + h], cr.at[3, 0, 2 * p + h], partner)

    def c2_first():
        arrived(c2buf.at[0], dr.at[3, 0])
        both = c2buf[...].astype(f32)[:, :24].reshape(48, D).astype(bf)
        w[12 + x, y, qm, :, lanes] = jnp.where(core == 0, both[:, :HALF], both[:, HALF:])
        here = w.at[12 + x, y, qm, :, lanes]
        for o in (1, 3, 2):
            to = device_at(turn(0, o * other), turn(1, o * core), z, core)
            start(C2.sent, here, here, as1.at[3, 0, o], ar1.at[3, 0, o], to)

    def c2_second():
        here = w.at[12 + x, y, qm, :, lanes]
        for o in (1, 2, 3):
            arrived(here, ar1.at[3, 0, o])
        lines = (w.at[12:16, y, qm, :, lanes], w.at[12 + x, :, qm, :, lanes])
        copies = [[remote(ref, ref, as1.at[3, 1, o], ar1.at[3, 1, o], device_at(turn(0, o * core), turn(1, o * other), z, core))
                   for o in (1, 3, 2)] for ref in lines]
        for c in both:
            @pl.when(core == c)
            def _():
                for copy in copies[c]:
                    copy.start()
        C2.sent.extend(copies[0])

    def c2_third():
        for o in (1, 2, 3):
            arrived(w.at[12:16, y, qm, :, lanes], ar1.at[3, 1, o])
        for p, off in ((1, s), (3, -s)):
            for h in both:
                start(C2.sent, plane(0, h), plane(0, h), as2.at[3, 0, 2 * p + h], ar2.at[3, 0, 2 * p + h], peer(2, off))
        for h in both:
            plane_hand(0, 0, h)

    def c2_relay():
        for h in both:
            here = plane(-s, h)
            arrived(here, ar2.at[3, 0, 2 + h])
            start(C2.sent, here, here, as2.at[3, 0, 4 + h], ar2.at[3, 0, 4 + h], peer(2, s))
            plane_hand(1, -s, h)

    def c2_hand():
        for p, off in ((3, s), (2, 2)):
            for h in both:
                arrived(plane(off, h), ar2.at[3, 0, 2 * p + h])
                plane_hand(p, off, h)

    def c2_finish():
        for p in range(4):
            for h in both:
                arrived(plane(0, h), cr.at[3, 0, 2 * p + h])

    block = hi * 2 + core
    pairs = ((tok_in, tok), (enc_in, enc))
    own = {}

    def input_start(i):
        src, dst = pairs[i]
        start(moved, src.at[1 - hi], dst.at[block], es.at[i], er.at[i], home)
        start(moved, src.at[hi], dst.at[block], es.at[2 + i], er.at[2 + i], partner)
        own[i] = local(src.at[hi], dst.at[block], ls.at[1 + i])

    def input_forward(i):
        far = pairs[i][1].at[(1 - hi) * 2 + core]
        arrived(far, er.at[i])
        start(moved, far, far, fs.at[i], fr.at[i], partner)

    def input_ready(i):
        here = pairs[i][1].at[0]
        own[i].wait()
        arrived(here, er.at[2 + i])
        arrived(here, fr.at[i])

    def grad_start():
        start(moved, og_in.at[1 - hi], og.at[core], es.at[4], er.at[4 + core], device_at(x, y, across, hi))

        @pl.when(core == hi)
        def _():
            c = pltpu.make_async_copy(og_in.at[hi], og.at[core], ls.at[3])
            c.start()
            c.wait()

        @pl.when(core != hi)
        def _():
            c = remote(og_in.at[hi], og.at[core], es.at[5], er.at[6], partner)
            c.start()
            c.wait_send()

    def grad_ready():
        @pl.when(hi == core)
        def _():
            arrived(og.at[0], er.at[6])

        @pl.when(hi != core)
        def _():
            for i in (0, 1):
                arrived(og.at[0], er.at[4 + i])

    def out_piece(t, i):
        if t.across:
            src = w.at[12 + i, :, :, :, lanes_other]
        elif t.half:
            src = w.at[t.out + other, :, :, :, halves[i]]
        else:
            src = w.at[t.out + 2 * other + i // 2, :, :, :, halves[i % 2]]
        return remote(src, db.at[t.slot, t.first + i], bds.at[t.index, i], bdr.at[t.index, i], partner)

    def out_start(t):
        for i in range(t.pieces):
            c = out_piece(t, i)
            c.start()
            t.sent.append(c)

    def out_early(i):
        c = out_piece(R2, i)
        c.start()
        R2.sent.append(c)
        pieces = [out_piece(R1, 2 * (i % 2) + h) for h in both]

        @pl.when(other == i // 2)
        def _():
            for c in pieces:
                c.start()
        if i < 2:
            R1.sent.extend(pieces)

    def out_line(t, c, off, at):
        if t.across:
            there = turn(2, off)
            return db.at[t.slot, at, :, lax.rem(there, 2) * 2 + there // 2]
        if c == 0:
            return db.at[t.slot, t.blocks(0), at, turn(1, off)]
        return db.at[t.slot, t.blocks(1), turn(0, off), at]

    def out_axis(t, c):
        return 2 if t.across else 1 - c

    def out_colors(t):
        return (0,) if t.across else (0, 1)

    def out_slot(t, c, p, at):
        return r1.at[t.slot, p, at] if t.across else r1.at[t.slot, p, t.blocks(c), at]

    parts = (pl.ds(0, 2), pl.ds(2, 2))
    whole = pl.ds(0, 4)

    def add_into(to, *terms):
        n = to.shape[0]

        @pl.loop(0, n)
        def _(i):
            if len(terms) == 1:
                to[i] = to[i] + terms[0][i]
            else:
                total = to[i].astype(f32)
                for term in terms:
                    total = total + term[i].astype(f32)
                to[i] = total.astype(bf)

    def out_first(t):
        for i in range(t.pieces):
            here = db.at[t.slot, t.first + i]
            arrived(here, bdr.at[t.index, i])
            if t.across:
                add_into(here, w.at[12 + i, :, :, :, lanes])
            elif t.half:
                add_into(here, w.at[t.out + core, :, :, :, halves[i]])
            else:
                add_into(here, w.at[t.out + 2 * core + i // 2, :, :, :, halves[i % 2]])
            if t.across and i < 3 or not t.half and i % 2 == 0:
                continue
            c = 0 if t.across else i if t.half else i // 2
            for p, off, to in ((0, 2, s), (1, -s, -s)):
                for h, at in enumerate(parts):
                    start(t.back, out_line(t, c, off, at), out_slot(t, c, p, at), b1s.at[t.index, c, 2 * p + h],
                          b1r.at[t.index, c, 2 * p + h], peer(out_axis(t, c), to))

    def out_second(t):
        for h, at in enumerate(parts):
            for c in out_colors(t):
                arrived(out_slot(t, c, 0, at), b1r.at[t.index, c, h])
                here = out_line(t, c, s, at)
                add_into(here, out_slot(t, c, 0, at))
                start(t.back, here, out_slot(t, c, 2, at), b1s.at[t.index, c, 4 + h], b1r.at[t.index, c, 4 + h],
                      peer(out_axis(t, c), s))

    def out_third(t):
        for c in out_colors(t):
            for p in (1, 2):
                for h, at in enumerate(parts):
                    arrived(out_slot(t, c, p, at), b1r.at[t.index, c, 2 * p + h])
            if t.across:
                @pl.loop(0, 4)
                def _(i):
                    total = db[t.slot, i, :, qm].astype(f32)
                    for p in (1, 2):
                        total = total + r1[t.slot, p, i].astype(f32)
                    ptot[i] = total.astype(bf)
            else:
                add_into(out_line(t, c, 0, whole), out_slot(t, c, 1, whole), out_slot(t, c, 2, whole))
            for o in (1, 3, 2):
                if t.across:
                    src, dst, to, sent = ptot.at[:, turn(1, o)], r2a.at[o - 1], yp[o], t.late
                elif c == 0:
                    src, dst, to, sent = db.at[t.slot, t.blocks(0), turn(0, o), y], r2.at[t.slot, o - 1, t.blocks(0)], xp[o], t.back
                else:
                    src, dst, to, sent = db.at[t.slot, t.blocks(1), x, turn(1, o)], r2.at[t.slot, o - 1, t.blocks(1)], yp[o], t.back
                start(sent, src, dst, b2s.at[t.index, c, o - 1], b2r.at[t.index, c, o - 1], to)

    def out_fourth(t):
        if t.across:
            for o in (0, 1, 2):
                arrived(r2a.at[o], b2r.at[t.index, 0, o])
            add_into(ptot.at[:, y], *[r2a.at[o] for o in (0, 1, 2)])
            for o in (1, 3, 2):
                start(t.late, ptot.at[turn(0, o), y], r2b.at[o - 1], b2s.at[t.index, 1, o - 1], b2r.at[t.index, 1, o - 1], xp[o])
            return
        for c in (0, 1):
            for o in (0, 1, 2):
                arrived(r2.at[t.slot, o, t.blocks(c)], b2r.at[t.index, c, o])
        for i in range(t.pieces):
            total = db[t.slot, t.first + i, x, y].astype(f32)
            for o in (0, 1, 2):
                total = total + r2[t.slot, o, t.first + i].astype(f32)
            red[i // 2, :, (i % 2) * HALF:(i % 2 + 1) * HALF] = total.astype(bf)
        rows = red[0] if t.half else red[...].reshape(96, D)
        shares[t.fin] = dot(split_matrix(t.half), rows).astype(bf).reshape(8, 16, D)
        for o in (1, 3, 2):
            start(t.late, shares.at[t.fin, pl.ds(member(turn(2, o), 0), 2)], r3.at[t.fin, o - 1], b3s.at[t.fin, o - 1],
                  b3r.at[t.fin, o - 1], zp[o])

    def out_fifth(t):
        if t.across:
            for o in (0, 1, 2):
                arrived(r2b.at[o], b2r.at[t.index, 1, o])
            total = ptot[x, y].astype(f32)
            for o in (0, 1, 2):
                total = total + r2b[o].astype(f32)
            c2sum[core] = total.astype(bf)
            start(t.late, c2sum.at[core], c2sum.at[core], b4s.at[t.index], b4r.at[t.index], partner)
            return
        for o in (0, 1, 2):
            arrived(r3.at[t.fin, o], b3r.at[t.fin, o])
        base = member(z, 0)

        def share(c):
            total = shares[t.fin, base + c].astype(f32)
            for o in (0, 1, 2):
                total = total + r3[t.fin, o, c].astype(f32)
            return total
        fin[t.fin, core] = share(core)
        sx[t.fin] = share(other).astype(bf)
        start(t.late, sx.at[t.fin], r4.at[t.fin], b4s.at[t.index], b4r.at[t.index], partner)

    def out_last(t):
        if t.across:
            arrived(c2sum.at[other], b4r.at[t.index])
            rows = jnp.concatenate([c2sum[0], c2sum[1]], 1).astype(f32)
            fin2[...] = jnp.where(core == 0, rows[:24], rows[24:])
            return
        arrived(r4.at[t.fin], b4r.at[t.index])
        fin[t.fin, other] = r4[t.fin].astype(f32)

    def give_credit(t):
        sends_done(t.back)
        for to in near:
            pl.semaphore_signal(credit.at[t.slot], inc=1, device_id=to, device_id_type=MESH)

    def take_credit(t):
        pl.semaphore_wait(credit.at[t.slot], len(near))

    def home_start(i, src, buf):
        for n in (0, 1):
            start(moved, src.at[2 * n + other], buf.at[n], ts.at[i, n], tr.at[i, n], partner)

    def home_sum(i, src, buf, out):
        for n in (0, 1):
            arrived(buf.at[n], tr.at[i, n])

            @pl.loop(0, buf.shape[1] // 16)
            def _(a):
                at = pl.ds(pl.multiple_of(a * 16, 16), 16)
                src[2 * n + core, at] = src[2 * n + core, at] + buf[n, at]
        start(moved, src.at[2 * (1 - hi) + core], out.at[hi], ts.at[2, i], tr.at[2, i], home)
        return local(src.at[2 * hi + core], out.at[hi], ls.at[4 + i])

    def result_copies():
        stays = pltpu.make_async_copy(BO.at[core], bo_out.at[hi], ls.at[3])
        passed = remote(BO.at[other], bo_out.at[hi], os_.at[0], tr.at[3, 0], partner)
        crossed = [remote(BO.at[n], bo_out.at[hi], os_.at[n], tr.at[3, 1], device_at(x, y, across, n)) for n in (0, 1)]
        return stays, passed, crossed

    def result_start():
        @pl.when(core == hi)
        def _():
            stays, passed, _ = result_copies()
            stays.start()
            passed.start()

        @pl.when(core != hi)
        def _():
            for c in result_copies()[2]:
                c.start()

    def result_done():
        @pl.when(core == hi)
        def _():
            stays, passed, _ = result_copies()
            stays.wait()
            passed.wait_send()

        @pl.when(core != hi)
        def _():
            for c in result_copies()[2]:
                c.wait_send()
            arrived(bo_out.at[0], tr.at[3, 0])
        arrived(bo_out.at[0], tr.at[3, 1])

    def weight(u):
        return w[u].reshape(D, D)

    def weight_grad(u, a, b):
        if a.shape[-2] * (a.shape[0] if len(a.shape) > 2 else 1) <= KEYS:
            w[u] = dot_grad(a[...].reshape(-1, D), b[...]).astype(bf).reshape(4, 4, 48, D)
            return

        @pl.loop(0, 2)
        def _(i):
            at = pl.ds(pl.multiple_of(i * HALF, 128), HALF)
            w[u, pl.ds(2 * i, 2)] = dot_grad(a[:, :, at].reshape(-1, HALF), b[...]).astype(bf).reshape(2, 4, 48, D)

    mine = pl.ds(pl.multiple_of(core * SPAN, 32), SPAN)

    loads = [local(m, s6.at[i], ls.at[6 + i]) for i, m in enumerate((m0, m1, m2, m3, m4, m5, m6, m7))]
    loads += [local(h_in, sh1, ls.at[14]), local(h_out, sh2, ls.at[15])]
    acc[0, 0:96] = jnp.zeros((96, D), f32)
    acc[1, 0:32] = jnp.zeros((32, D), f32)
    for c in loads:
        c.wait()
    for i in range(4):
        acc[0, 6 * i:6 * i + 6] = s6[i].astype(f32)
        acc[0, 32 + 6 * i:38 + 6 * i] = s6[4 + i].astype(f32)
        acc[0, 64 + 6 * i:70 + 6 * i] = sh1[:, D * i:D * i + D].astype(f32)
    acc[0, 24:25, 0:128] = small[...]
    acc[1, 0:24] = sh2[...].astype(f32)
    zbuf[me] = acc[0, 0:96].astype(bf)
    c2buf[core] = acc[1, 0:32].astype(bf)
    pl.semaphore_wait(barrier, len(peers))
    z_start(A)
    start(C2.sent, c2buf.at[core], c2buf.at[core], ds.at[3, 0], dr.at[3, 0], partner)
    z_start(B)
    z_start(C1)
    input_start(0)
    c2_first()
    z_mid(A)
    spread(A)
    xy1(A)
    z_mid(B)
    spread(B)
    xy1(B)
    c2_second()
    z_mid(C1)
    spread(C1)
    xy2(A)
    krow = seg2[hi]
    clips[...] = jnp.full((8, FRAMES), -1, jnp.int32)
    clips[0:1, 0:1500] = clip2[hi]
    raw = clips[...]
    at = lax.broadcasted_iota(jnp.int32, (8, FRAMES), 1)
    moved_ids = raw
    for b in (1, 2, 3):
        moved_ids = jnp.where(at >= 384 * b, pltpu.roll(raw, 9 * b, 1), moved_ids)
    crow = jnp.where(lax.rem(at, 384) < 375, moved_ids, -1)[0:1]
    ids = jnp.broadcast_to(krow, (8, KEYS)).astype(f32).T[:, 0:1].astype(jnp.int32)
    qcol = jnp.where(core == 0, ids[:SPAN], ids[SPAN:])
    key_at = lax.broadcasted_iota(jnp.int32, (SPAN, KEYS), 1)
    query_at = lax.broadcasted_iota(jnp.int32, (SPAN, KEYS), 0) + core * SPAN
    bias_s[...] = jnp.where((qcol == krow) & (key_at <= query_at), 0.0, BLOCKED)
    bias_c[...] = jnp.where(qcol == crow, 0.0, BLOCKED).astype(bf)
    c2_third()
    input_start(1)
    relay(A)
    xy2(B)
    xy1(C1)
    input_forward(0)
    input_ready(0)
    hand_over(A)

    S = sm[...].astype(f32).reshape(16, 16, 128)[:, :8].reshape(128, 128).astype(bf)
    owner, inner, which = vector_tables()
    vec[...] = dot_back(which, (dot(owner, S) * inner).astype(bf))
    for n in range(4):
        owner, inner = hidden_tables(n)
        hib[n:n + 1] = dot_back(jnp.ones((8, 128), bf), (dot(owner, S) * inner).astype(bf))[0:1]

    @pl.loop(0, 4)
    def _(i):
        n, _ = normed(tok[i].astype(f32))
        first[pl.ds(pl.multiple_of(i * 112, 16), 112)] = (n * vec[0:1] + vec[1:2]).astype(bf)
    finish(A)
    relay(B)
    xy2(C1)

    def keys(at):
        k[at] = dot(first[at], weight(1)).astype(bf)
    blocks(KEYS, SPAN, keys)

    def values(at):
        v[at] = (dot(first[at], weight(2)) + vec[3:4]).astype(bf)
    blocks(KEYS, SPAN, values)
    q[...] = (dot(first[mine], weight(0)) + vec[2:3]).astype(bf) * SCALE
    hand_over(B)
    attend(q, k, v, bias_s, mixed, lse, 0, 3)
    c2_relay()
    grad_start()
    relay(C1)
    input_forward(1)
    attend(q, k, v, bias_s, mixed, lse, 3, 6)
    after_self[...] = tok[pl.ds(2 * core, 2)].reshape(SPAN, D).astype(f32) + dot(mixed[...], weight(3)) + vec[4:5]
    n, r = normed(after_self[...])
    second[...] = (n * vec[5:6] + vec[6:7]).astype(bf)
    finish(B)
    cq[...] = (dot(second[...], weight(4)) + vec[7:8]).astype(bf) * SCALE
    hand_over(C1)
    input_ready(1)

    @pl.loop(0, 4)
    def _(i):
        ck[pl.ds(pl.multiple_of(i * 384, 128), 384)] = dot(enc[i], weight(5)).astype(bf)

    @pl.loop(0, 4)
    def _(i):
        cv[pl.ds(pl.multiple_of(i * 384, 128), 384)] = (dot(enc[i], weight(6)) + vec[8:9]).astype(bf)
    attend(cq, ck, cv, bias_c, cmixed, clse, 0, 3)
    c2_hand()
    attend(cq, ck, cv, bias_c, cmixed, clse, 3, 6)
    stream[...] = after_self[...] + dot(cmixed[...], weight(7)) + vec[9:10]
    n, r = normed(stream[...])
    third[...] = (n * vec[10:11] + vec[11:12]).astype(bf)
    acc[0] = stream[...] + vec[12:13]
    acc[1] = jnp.zeros((SPAN, D), f32)
    grad_ready()
    g[...] = og[...].reshape(SPAN, D)
    finish(C1)
    c2_finish()
    for t in (A, B, C1, C2):
        sends_done(t.sent)
    sends_done(moved)
    for i in range(4):
        pre = dot(third[...], weight(8 + i)) + hib[i:i + 1]
        cdf = 0.5 * (1.0 + lax.erf(pre * 0.7071067811865476))
        act = (pre * cdf).astype(bf)
        slope = cdf + pre * (0.3989422804014327 * jnp.exp(-0.5 * pre * pre))
        wide[0] = act
        acc[0] += dot(act, weight(12 + i))
        g_pre = (dot_back(g[...], weight(12 + i)) * slope).astype(bf)
        wide[1] = g_pre
        weight_grad(12 + i, wide.at[0], g)
        ghib[i:i + 1] = row_sum(g_pre.astype(f32))
        acc[1] += dot_back(g_pre, weight(8 + i))
        weight_grad(8 + i, third, wide.at[1])
        out_early(i)
    BO[...] = acc[0].astype(bf).reshape(2, 112, D)
    e = acc[1]
    ogf = g[...].astype(f32)
    n, r = normed(stream[...])
    gvec[13:16] = jnp.zeros((3, D), f32)
    gvec[12:13] = row_sum(ogf)
    gvec[10:11] = row_sum(e * n)
    gvec[11:12] = row_sum(e)
    stream[...] = ogf + norm_back(e, n, r, vec[10:11])
    wide[0] = stream[...].astype(bf)
    gvec[9:10] = row_sum(wide[0].astype(f32))
    out_first(R2)
    g[...] = dot_back(wide[0], weight(7)).astype(bf)
    out_first(R1)
    sends_done(R2.sent)
    sends_done(R1.sent)
    weight_grad(15, cmixed, wide.at[0])
    attend_back(cq, ck, cv, bias_c, cmixed, clse, g, gq, ck, cv, 0, 4)
    out_second(R1)
    attend_back(cq, ck, cv, bias_c, cmixed, clse, g, gq, ck, cv, 4, 6)
    out_second(R2)
    out_third(R1)
    weight_grad(13, enc, ck)
    weight_grad(14, enc, cv)
    weight_grad(12, second, gq)
    out_fourth(R1)
    give_credit(R1)
    e = dot_back(gq[...], weight(4))
    gvec[7:8] = row_sum(gq[...].astype(f32))
    gvec[8:9] = row_sum(cv[...].astype(f32))
    take_credit(RB)
    out_start(RB)
    n, r = normed(after_self[...])
    gvec[5:6] = row_sum(e * n)
    gvec[6:7] = row_sum(e)
    stream[...] += norm_back(e, n, r, vec[5:6])
    wide[0] = stream[...].astype(bf)
    gvec[4:5] = row_sum(wide[0].astype(f32))
    g[...] = dot_back(wide[0], weight(3)).astype(bf)
    weight_grad(11, mixed, wide.at[0])
    out_first(RB)
    out_third(R2)
    give_credit(R2)
    attend_back(q, k, v, bias_s, mixed, lse, g, gq, k, v, 0, 6)
    wide[0] = first[mine]
    weight_grad(8, wide.at[0], gq)
    weight_grad(9, first, k)
    weight_grad(10, first, v)
    take_credit(RA)
    out_start(RA)
    out_second(RB)

    @pl.loop(0, 4)
    def _(i):
        at = pl.ds(pl.multiple_of(i * 384, 128), 384)
        enc[i] = (dot_back(ck[at], weight(5)) + dot_back(cv[at], weight(6))).astype(bf)
    home_start(1, enc, eib)
    out_first(RA)
    out_third(RB)
    out_fourth(R2)
    ends = [home_sum(1, enc, eib, ep_out)]
    result_start()
    gvec[2:3] = row_sum(gq[...].astype(f32))
    gvec[3:4] = row_sum(v[...].astype(f32))
    gvec[0:2] = jnp.zeros((2, D), f32)
    acc[0] = dot_back(gq[...], weight(0))
    for h in (0, 1):
        at = pl.ds(h * SPAN, SPAN)
        is_own = core == h
        e = dot_back(k[at], weight(1)) + dot_back(v[at], weight(2)) + jnp.where(is_own, acc[0], 0.0)
        n, r = normed(tok[2 * h:2 * h + 2].reshape(SPAN, D).astype(f32))
        gvec[0:1] += row_sum(e * n)
        gvec[1:2] += row_sum(e)
        PI[2 * h:2 * h + 2] = (norm_back(e, n, r, vec[0:1]) + jnp.where(is_own, stream[...], 0.0)).astype(bf).reshape(2, 112, D)
    home_start(0, PI, pib)
    out_second(RA)
    out_fourth(RB)
    owner, inner, which = vector_tables()
    spread_out = lax.dot_general(gvec[...].astype(bf), which, (((0,), (0,)), ((), ())), preferred_element_type=f32)
    total = dot_grad(owner, (spread_out * inner).astype(bf))
    for n in range(4):
        owner, inner = hidden_tables(n)
        column = jnp.broadcast_to(ghib[n:n + 1], (8, D)).T[:, 0:1]
        total = total + dot_grad(owner, (column * inner).astype(bf))
    SG[...] = total.reshape(4, 4, 8, 128)
    swap = remote(SG, sd, gss.at[0], gsr.at[0], partner)
    swap.start()
    swap.wait()
    SG[...] = SG[...] + sd[...]
    for p in (1, 2, 3):
        start(moved, SG.at[:, turn(1, p)], s1b.at[p], gss.at[p], gsr.at[p], yp[p])
    ends.append(home_sum(0, PI, pib, pi_out))
    out_third(RA)
    out_fifth(R2)
    out_fifth(R1)
    out_fifth(RB)
    total = SG[:, y]
    for p in (1, 2, 3):
        arrived(s1b.at[p], gsr.at[p])
        total = total + s1b[p]
    SG[:, y] = total
    for b in (1, 2, 3):
        start(moved, SG.at[turn(0, b), y], s2b.at[b], gss.at[3 + b], gsr.at[3 + b], xp[b])
    out_fourth(RA)
    total = SG[x, y]
    for b in (1, 2, 3):
        arrived(s2b.at[b], gsr.at[3 + b])
        total = total + s2b[b]
    s3b[0] = total
    for o in (1, 2, 3):
        start(moved, s3b.at[0], s3b.at[o], gss.at[6 + o], gsr.at[6 + o], zp[o])
    out_last(R2)
    out_last(R1)
    out_last(RB)
    out_fifth(RA)
    total = s3b[0]
    for o in (1, 2, 3):
        arrived(s3b.at[o], gsr.at[6 + o])
        total = total + s3b[o]
    own_row = lax.broadcasted_iota(jnp.int32, (8, 128), 0) == me
    gs[...] = jnp.broadcast_to(jnp.sum(jnp.where(own_row, total, 0.0), 0, keepdims=True), (8, 128))
    arrived(ep_out.at[0], tr.at[2, 1])
    arrived(pi_out.at[0], tr.at[2, 0])

    result_done()
    out_last(RA)
    for c in ends:
        c.wait()
    for t in (R1, R2, RB, RA):
        sends_done(t.sent)
        sends_done(t.back)
        sends_done(t.late)
    sends_done(moved)


def layer(*operands):
    V, DMA, S = pltpu.VMEM, pltpu.SemaphoreType.DMA, jax.ShapeDtypeStruct
    vm, hbm = pl.BlockSpec(memory_space=pltpu.VMEM), pl.BlockSpec(memory_space=pl.ANY)
    return pl.pallas_call(
        layer_kernel,
        out_shape=[S((3, 2, 16, D), f32), S((24, D), f32), S((8, 128), f32), S((2, 112, D), bf), S((2, 112, D), bf), S((2, 384, D), bf)],
        in_specs=[hbm] * 10 + [vm] + [hbm] * 3 + [vm] * 2, out_specs=[vm] * 3 + [hbm] * 3,
        scratch_shapes=[
            V((16, 4, 4, 48, D), bf), V((8, 6, D), bf), V((6, 4 * D), bf), V((24, D), bf), V((8, 96, D), bf), V((2, 32, D), bf),
            V((4, 4, 16, 128), bf), V((16, 128), bf), V((4, 112, D), bf), V((4, 384, D), bf), V((2, 112, D), bf),
            V((16, D), f32), V((8, D), f32), V((KEYS, D), bf), V((SPAN, D), bf), V((KEYS, D), bf), V((KEYS, D), bf),
            V((SPAN, D), bf), V((6, SPAN, 128), f32), V((SPAN, D), bf), V((SPAN, D), bf), V((FRAMES, D), bf), V((FRAMES, D), bf),
            V((SPAN, D), bf), V((6, SPAN, 128), f32), V((SPAN, D), f32), V((SPAN, D), f32), V((SPAN, D), bf),
            V((2, SPAN, D), f32), V((SPAN, KEYS), f32), V((SPAN, FRAMES), bf), V((SPAN, D), bf), V((SPAN, D), bf),
            V((2, SPAN, D), bf), V((16, D), f32), V((8, D), f32),
            V((2, 112, D), bf), V((4, 112, D), bf), V((2, 112, D), bf), V((2, 384, D), bf),
            V((2, 4, 4, 4, 48, HALF), bf), V((2, 3, 4, 4, 48, HALF), bf), V((2, 3, 4, 48, HALF), bf), V((3, 4, 48, HALF), bf), V((3, 48, HALF), bf), V((4, 4, 48, HALF), bf),
            V((2, 48, D), bf), V((3, 8, 16, D), bf), V((3, 3, 2, 16, D), bf), V((3, 16, D), bf), V((3, 16, D), bf),
            V((2, 48, HALF), bf), V((16, 128), f32),
            V((4, 4, 8, 128), f32), V((4, 4, 8, 128), f32), V((4, 4, 8, 128), f32), V((4, 8, 128), f32), V((4, 8, 128), f32),
            V((8, FRAMES), jnp.int32),
            DMA((16,)), DMA((5, 4)), DMA((5, 4)), DMA((5, 4)), DMA((5, 4)), DMA((5, 2, 4)), DMA((5, 2, 4)), DMA((5, 2, 8)), DMA((5, 2, 8)),
            DMA((5, 2, 8)), DMA((5, 2, 8)), DMA((4,)), DMA((4,)), DMA((4,)), DMA((4,)), DMA((6,)), DMA((7,)), DMA((2,)), DMA((2,)),
            DMA((5, 4)), DMA((5, 4)), DMA((5, 2, 6)), DMA((5, 2, 6)), DMA((5, 2, 3)), DMA((5, 2, 3)), DMA((4, 3)), DMA((4, 3)),
            DMA((5,)), DMA((5,)), DMA((10,)), DMA((10,)), DMA((3, 2)), DMA((4, 2)), DMA((2,)), pltpu.SemaphoreType.REGULAR((2,))],
        compiler_params=pltpu.CompilerParams(collective_id=0, has_side_effects=True, vmem_limit_bytes=63 << 20),
        name="layer",
    )(*operands)


def unpack_kernel(*refs):
    ins, outs, (fin, fin2, bo, pi, ep, sems) = refs[:5], refs[5:18], refs[18:]
    copies = [pltpu.make_async_copy(src, dst, sems.at[i]) for i, (src, dst) in enumerate(zip(ins, (fin, fin2, bo, pi, ep)))]
    for c in copies:
        c.start()
    for c in copies:
        c.wait()
    out, gi, ge, mats, h_in, h_out = outs[0], outs[1], outs[2], outs[3:11], outs[11], outs[12]
    out[...] = bo[...][:, None]
    gi[...] = pi[...].astype(f32)[:, None]
    for micro in (0, 1):
        ge[micro, :, 0, :] = ep[micro, :375].astype(f32)
    for i in range(4):
        mats[i][...] = fin[2, i // 2, 6 * (i % 2):6 * (i % 2) + 6]
        mats[4 + i][...] = fin[1, i // 2, 6 * (i % 2):6 * (i % 2) + 6]
        h_in[:, D * i:D * i + D] = fin[0, i // 2, 6 * (i % 2):6 * (i % 2) + 6]
    h_out[...] = fin2[...]


def unpack(fin, fin2, bo, pi, ep):
    S, V, hbm = jax.ShapeDtypeStruct, pltpu.VMEM, pl.BlockSpec(memory_space=pl.ANY)
    return pl.pallas_call(
        unpack_kernel,
        out_shape=[S((2, 1, 112, D), bf), S((2, 1, 112, D), f32), S((2, 375, 1, D), f32)] + [S((6, D), f32)] * 8
        + [S((6, 4 * D), f32), S((24, D), f32)],
        in_specs=[hbm] * 5,
        scratch_shapes=[V((3, 2, 16, D), f32), V((24, D), f32), V((2, 112, D), bf), V((2, 112, D), bf), V((2, 384, D), bf),
                        pltpu.SemaphoreType.DMA((5,))],
        compiler_params=pltpu.CompilerParams(vmem_limit_bytes=60 << 20),
        name="unpack",
    )(fin, fin2, bo, pi, ep)


def per_device(
    tokens, encoder_states, segments, frame_clips, out_grad,
    self_gain, self_shift, self_query, self_query_bias, self_key, self_value, self_value_bias, self_output,
    self_output_bias, cross_gain, cross_shift, cross_query, cross_query_bias, cross_key, cross_value,
    cross_value_bias, cross_output, cross_output_bias, final_gain, final_shift, hidden_in, hidden_in_bias,
    hidden_out, hidden_out_bias,
):
    vectors = (self_gain, self_shift, self_query_bias, self_value_bias, self_output_bias, cross_gain, cross_shift,
               cross_query_bias, cross_value_bias, cross_output_bias, final_gain, final_shift, hidden_out_bias)
    small = jnp.pad(hidden_in_bias.astype(f32), (78, 26))
    for i, vector in enumerate(vectors):
        small = small + jnp.pad(vector.astype(f32), (6 * i, 122 - 6 * i))
    frames = jnp.pad(encoder_states, ((0, 0), (0, 0), (0, 9), (0, 0))).reshape(2, 384, D)
    fin, fin2, gs, bo, pi, ep = layer(
        self_query, self_key, self_value, self_output, cross_query, cross_key, cross_value, cross_output, hidden_in, hidden_out,
        small[None], tokens[:, 0], frames, out_grad[:, 0], segments, frame_clips)
    out, gi, ge, *m = unpack(fin, fin2, bo, pi, ep)
    gv = [gs[0, 6 * i:6 * i + 6] for i in range(13)]
    return (out, gi, ge.transpose(0, 2, 1, 3),
            gv[0], gv[1], m[0], gv[2], m[1], m[2], gv[3], m[3], gv[4],
            gv[5], gv[6], m[4], gv[7], m[5], m[6], gv[8], m[7], gv[9],
            gv[10], gv[11], m[8], gs[0, 78:102], m[9], gv[12])


def solution(mesh):
    rows = P(None, "win", "seq", None)
    vector, matrix = P(("win", "seq")), P(("win", "seq"), None)
    kinds = "vvmvmmvmvvvmvmmvmvvvmvmv"
    weights = tuple(matrix if kind == "m" else vector for kind in kinds)
    in_specs = (rows, rows, P(None, "win", None), P(None, "win", None), rows) + weights
    return jax.shard_map(per_device, mesh=mesh, in_specs=in_specs, out_specs=(rows, rows, rows) + weights, check_vma=False)
```
